32 devices in a mesh: tm: 16 (over z, y, core), batch: 2 (over x).
Axes of the slice: x: 2, y: 2, z: 4, core: 2. Of those that a mesh axis runs over, the one named last changes fastest.
Arguments:
- block_entry_input: bfloat16 [2, 8192, 384], P('batch', 'tm'), may hold values from -90 to 90
- prelude_output: bfloat16 [2, 8192, 256], P('batch', 'tm'), may hold values from -90 to 90
- leading_block_output: bfloat16 [2, 8192, 256], P('batch', 'tm'), may hold values from -90 to 90
- lengths: int32 [2, 16], P('batch'), may hold values from 1 to 1024, 8192 in all within a row
- leading_conv_weight: bfloat16 [512, 17, 384], replicated, may hold values from -0.078125 to 0.078125
- remaining_conv_weight: bfloat16 [4, 512, 17, 512], replicated, may hold values from -0.0625 to 0.0625
- gain: float32 [5, 512], replicated, may hold values from 0.25 to 1.75
- shift: float32 [5, 512], replicated, may hold values from -3 to 3
- residual_pointwise_weight: bfloat16 [512, 896], replicated, may hold values from -0.375 to 0.375
- residual_norm_scale: float32 [3, 512], replicated, may hold values from 0.4 to 0.8
- residual_norm_bias: float32 [3, 512], replicated, may hold values from -3 to 3
- cotangent: bfloat16 [2, 8192, 512], P('batch', 'tm'), may hold values from -90 to 90
Outputs:
- block_output: bfloat16 [2, 8192, 512], P('batch', 'tm')
- grad_block_input: bfloat16 [2, 8192, 384], P('batch', 'tm')
- prelude_gradient: bfloat16 [2, 8192, 256], P('batch', 'tm')
- grad_first: bfloat16 [2, 8192, 256], P('batch', 'tm')
- grad_w_first: float32 [512, 17, 384], P('tm')
- grad_w_rest: float32 [4, 512, 17, 512], P(None, 'tm')
- grad_gain: float32 [5, 512], P(None, 'tm')
- grad_shift: float32 [4, 512], P(None, 'tm')
- grad_last_shift: float32 [512], P('tm')
- grad_res_weight: float32 [512, 896], P('tm')
- grad_res_gain: float32 [3, 512], P(None, 'tm')
- grad_res_shift: float32 [3, 512], P(None, 'tm')
The draws below stay inside these ranges and needn't reach their ends.
Inputs may be any that keep to these rules, and one draw needn't show every extreme that they name: Each row's 16 utterance lengths sum to 8192, and the longest is exactly 1024.
All inputs are finite; a program needn't handle non-finite values.
Results may differ from the reference program's by a relative error of at most 0.023.
Values may be sent and summed in bfloat16 or wider, within the bound.
No kernel may reach another device: no remote copies, remote signals or barrier semaphores. Data moves between devices by JAX's collectives and lax.ppermute only.
A program may use at most 256 MiB of HBM per device.

```python
import math
import jax
import jax.numpy as jnp
import numpy as np
from jax import lax

CH = 512
CIN = 384
CPRO = 256
CONE = 256
KERNEL = 17
SUBS = 5
HALF = 8
REST = 4
CRES = 896
FRAMES = 8192
ROWS = 2
UTTS = 16
MAX_UTT = 1024


def textured(key, channels, offset, ramp, base):
    key_frame, key_chan = jax.random.split(key)
    position = jnp.arange(FRAMES, dtype=jnp.float32) / (FRAMES - 1)
    trend = 1.0 + (ramp - 1.0) * position
    frame_scale = jnp.exp(math.log(10.0) * (jax.random.uniform(key_frame, (ROWS, FRAMES, 1)) - 0.5))
    chan_scale = jnp.exp(math.log(4.0) * (jax.random.uniform(key_chan, (channels,)) - 0.5))
    return trend[None, :, None] * frame_scale * chan_scale * (base + offset)


def draw_block_entry_input(key, part):
    key = jax.random.fold_in(key, 11)
    key_base, key_rest = jax.random.split(key)
    base = jnp.clip(jax.random.normal(key_base, (ROWS, FRAMES, CIN)), -4.0, 4.0)
    ramp = 3.0
    return textured(key_rest, CIN, 0.5, ramp, base).astype(jnp.bfloat16)


def draw_prelude_output(key, part):
    key = jax.random.fold_in(key, 23)
    key_base, key_rest = jax.random.split(key)
    base = jnp.clip(jax.random.normal(key_base, (ROWS, FRAMES, CPRO)), -4.0, 4.0)
    ramp = 3.0
    return textured(key_rest, CPRO, 0.5, ramp, base).astype(jnp.bfloat16)


def draw_leading_block_output(key, part):
    key = jax.random.fold_in(key, 37)
    key_base, key_rest = jax.random.split(key)
    base = jnp.clip(jax.random.normal(key_base, (ROWS, FRAMES, CONE)), -4.0, 4.0)
    ramp = 3.0
    return textured(key_rest, CONE, 0.5, ramp, base).astype(jnp.bfloat16)


def draw_cotangent(key, part):
    key = jax.random.fold_in(key, 41)
    key_base, key_rest = jax.random.split(key)
    base = jnp.clip(jax.random.normal(key_base, (ROWS, FRAMES, CH)), -4.0, 4.0)
    ramp = 3.0
    return textured(key_rest, CH, 0.2, ramp, base).astype(jnp.bfloat16)


def profile(number_of, total, limit, lean):
    portions = [(1 << 20) // math.isqrt(rank ** lean) + 1 for rank in range(2, number_of + 1)]
    rest, holding = total - limit - (number_of - 1), [1] * (number_of - 1)
    while rest > 0:
        movable = [i for i in range(number_of - 1) if holding[i] < limit]
        pool, budget = sum([portions[i] for i in movable]), rest
        for i in movable:
            addition = min(limit - holding[i], max(1, budget * portions[i] // pool), rest)
            holding[i] = holding[i] + addition
            rest = rest - addition
    return np.array([limit] + holding)


def uneven_parts(key, count, total, reach, lean):
    if count == 2:
        one = jax.random.randint(key, (), max(1, total - reach), min(reach, total - 1) + 1)
        return jnp.stack([one, total - one])
    sizes = jnp.asarray(profile(count, total, reach, lean), jnp.int32)
    couples = (count - 1) // 2
    giver, sink = sizes[1:1 + 2 * couples:2], sizes[2:2 + 2 * couples:2]
    room = jnp.minimum(giver - 1, reach - sink)
    moved = jax.random.randint(jax.random.fold_in(key, 1), (couples,), 0, 1 << 20) % (room + 1)
    sizes = sizes.at[1:1 + 2 * couples:2].set(giver - moved).at[2:2 + 2 * couples:2].set(sink + moved)
    return sizes[jax.random.permutation(jax.random.fold_in(key, 2), count)]


def normal_values(rng, shape, scale, most, kind=jnp.bfloat16):
    values = jax.random.normal(rng, shape, jnp.float32) * scale
    return jnp.minimum(jnp.maximum(values, -most), most).astype(kind)


def setup_inputs(seed: int = 0) -> dict:
    key_list = jax.random.split(jax.random.key(seed), 13)
    block_entry_input = draw_block_entry_input(jax.random.fold_in(key_list[12], 71), 0)
    prelude_output = draw_prelude_output(jax.random.fold_in(key_list[12], 71), 0)
    leading_block_output = draw_leading_block_output(jax.random.fold_in(key_list[12], 71), 0)
    lengths = jax.vmap(lambda own: uneven_parts(own, UTTS, FRAMES, MAX_UTT, 2))(jax.random.split(key_list[3], ROWS)).reshape((ROWS, UTTS)).astype(jnp.int32)
    leading_conv_weight = normal_values(key_list[4], (CH, KERNEL, CIN), (KERNEL * CIN) ** -0.5, 0.078125)
    remaining_conv_weight = normal_values(key_list[5], (REST, CH, KERNEL, CH), (KERNEL * CH) ** -0.5, 0.0625)
    gain = jnp.clip(1.0 + 0.15 * jax.random.normal(key_list[6], (SUBS, CH), jnp.float32), 0.25, 1.75)
    shift = normal_values(key_list[7], (SUBS, CH), 0.5, 3.0, jnp.float32)
    residual_pointwise_weight = normal_values(key_list[8], (CH, CRES), CPRO ** -0.5, 0.375)
    residual_norm_scale = jnp.clip(jax.random.uniform(key_list[9], (3, CH), jnp.float32, 0.4, 0.8), 0.4, 0.8)
    residual_norm_bias = normal_values(key_list[10], (3, CH), 0.5, 3.0, jnp.float32)
    cotangent = draw_cotangent(jax.random.fold_in(key_list[12], 71), 0)
    return dict(block_entry_input=block_entry_input, prelude_output=prelude_output, leading_block_output=leading_block_output, lengths=lengths, leading_conv_weight=leading_conv_weight, remaining_conv_weight=remaining_conv_weight, gain=gain, shift=shift, residual_pointwise_weight=residual_pointwise_weight, residual_norm_scale=residual_norm_scale, residual_norm_bias=residual_norm_bias, cotangent=cotangent)


norm_eps = 0.001

@jax.custom_vjp
def low(v):
    return lax.optimization_barrier(v.astype(jnp.bfloat16)).astype(jnp.float32)

@jax.custom_vjp
def low_back(v):
    return v

def low_keep(v):
    return (low(v), None)

def low_pass(kept, grad):
    return (grad,)

def back_keep(v):
    return (v, None)

def back_low(kept, grad):
    return (low(grad),)
low.defvjp(low_keep, low_pass)
low_back.defvjp(back_keep, back_low)

def normalize(values, scale, bias):
    average = lax.optimization_barrier(jnp.mean(values, axis=(0, 1)))
    spread = lax.optimization_barrier(jnp.mean(values * values, axis=(0, 1))) - average * average
    return (values - average) * lax.rsqrt(spread + norm_eps) * scale + bias

def reference(block_entry_input, prelude_output, leading_block_output, lengths, leading_conv_weight, remaining_conv_weight, gain, shift, residual_pointwise_weight, residual_norm_scale, residual_norm_bias, cotangent):
    starts = jnp.cumsum(lengths, axis=1) - lengths
    frame_pos = jnp.arange(FRAMES, dtype=jnp.int32)
    segment = lax.optimization_barrier(jnp.sum((frame_pos[None, :, None] >= starts[:, None, :]).astype(jnp.int32), axis=2)) - 1
    padded_seg = jnp.pad(segment, ((0, 0), (HALF, HALF)), constant_values=-1)
    tap_masks = jnp.stack([(padded_seg[:, tap_index:tap_index + FRAMES] == segment).astype(jnp.float32) for tap_index in range(KERNEL)])

    def convolve(hidden, weight):
        padded = jnp.pad(hidden, ((0, 0), (HALF, HALF), (0, 0)))

        def add_tap(running, tap_index):
            piece = lax.dynamic_slice_in_dim(padded, tap_index, FRAMES, 1) * tap_masks[tap_index][:, :, None]
            tap_weight = lax.dynamic_index_in_dim(weight, tap_index, 1, keepdims=False)
            return (running + jnp.einsum('rtc,oc->rto', piece, tap_weight, precision=lax.Precision.HIGHEST), None)
        initial = jnp.zeros((hidden.shape[0], FRAMES, weight.shape[0]), jnp.float32)
        running, unused = lax.scan(add_tap, initial, jnp.arange(KERNEL, dtype=jnp.int32))
        return running
    convolve = jax.checkpoint(convolve)

    def forward_pass(entry_activations, prelude_input, leading_input, leading_weight_matrix, remaining_weight_matrix, combined_gains, combined_biases, residual_weight_matrix, residual_gains, residual_biases):
        hidden = entry_activations
        for layer in range(SUBS):
            weight = leading_weight_matrix if layer == 0 else remaining_weight_matrix[layer - 1]
            conv_out = low_back(convolve(hidden, weight))
            pre_act = normalize(conv_out, combined_gains[layer], combined_biases[layer])
            if layer < SUBS - 1:
                hidden = low(jax.nn.silu(pre_act))
        bounds = [0, CPRO, CPRO + CONE, CPRO + CONE + CIN]
        fragment_list = (prelude_input, leading_input, entry_activations)
        residual = jnp.zeros_like(pre_act)
        for branch in range(3):
            res_part = residual_weight_matrix[:, bounds[branch]:bounds[branch + 1]]
            projected = low_back(jnp.einsum('rtc,oc->rto', fragment_list[branch], res_part, precision=lax.Precision.HIGHEST))
            residual = residual + normalize(projected, residual_gains[branch], residual_biases[branch])
        return jax.nn.silu(pre_act + residual)
    float_tensors = [value_result.astype(jnp.float32) for value_result in (block_entry_input, prelude_output, leading_block_output, leading_conv_weight, remaining_conv_weight, gain, shift, residual_pointwise_weight, residual_norm_scale, residual_norm_bias)]
    output, pullback = jax.vjp(forward_pass, *float_tensors)
    gradients = pullback(cotangent.astype(jnp.float32))
    return (output.astype(jnp.bfloat16), gradients[0].astype(jnp.bfloat16), gradients[1].astype(jnp.bfloat16), gradients[2].astype(jnp.bfloat16), gradients[3], gradients[4], gradients[5], gradients[6][:REST], gradients[6][REST], gradients[7], gradients[8], gradients[9])
```

```python
import functools

import jax
import jax.numpy as jnp
from jax import lax
from jax.experimental import pallas as pl
from jax.experimental.pallas import tpu as pltpu
from jax.sharding import PartitionSpec as P

norm_eps = 0.001
lane = 128
half_taps = 8
group = 8
unit = 16
bf16 = jnp.bfloat16
f32 = jnp.float32
vmem_budget = 44 << 20

row_dot = (((1,), (1,)), ((), ()))
plain_dot = (((1,), (0,)), ((), ()))
column_dot = (((0,), (0,)), ((), ()))


def in_vmem():
    return pl.BlockSpec(memory_space=pltpu.VMEM)


def in_place():
    return pl.BlockSpec(memory_space=pl.ANY)


def in_smem():
    return pl.BlockSpec(memory_space=pltpu.SMEM)


def dot(a, b, dims):
    return lax.dot_general(a, b, dims, preferred_element_type=f32)


def cols(c):
    return slice(c * lane, (c + 1) * lane)


def sigmoid(v):
    return 1.0 / (1.0 + jnp.exp(-v))


def moments(total, row, count, samples):
    out = []
    for c in range(count):
        mean = total[row + c : row + c + 1] * (1.0 / samples)
        spread = total[row + count + c : row + count + c + 1] * (1.0 / samples) - mean * mean
        out.append((mean, lax.rsqrt(spread + norm_eps)))
    return out


def start_weights(w_hbm, w_vmem, sems, pick):
    for k in range(w_vmem.shape[0]):
        pltpu.make_async_copy(pick(w_hbm, k), w_vmem.at[k], sems.at[k]).start()


def wait_weights(w_hbm, w_vmem, sems, pick, k):
    pltpu.make_async_copy(pick(w_hbm, k), w_vmem.at[k], sems.at[k]).wait()


def convolve(rows, base, planes, seg_ref, w_hbm, w_vmem, sems, pick, flip, dims, acc_ref):
    taps = w_vmem.shape[0]
    blocks = planes.shape[0]
    for k in range(taps):
        tap = taps - 1 - k if flip else k
        wait_weights(w_hbm, w_vmem, sems, pick, tap)
        mask = (
            seg_ref[base + k : base + k + rows]
            == seg_ref[base + half_taps : base + half_taps + rows]
        )
        x = jnp.concatenate(
            [jnp.where(mask, planes[c, k : k + rows], 0.0).astype(bf16) for c in range(blocks)],
            axis=1,
        )
        d = dot(x, w_vmem[tap], dims)
        if k == 0:
            acc_ref[...] = d
        else:
            acc_ref[...] += d


def broadcast_sums(snd_ref, pieces):
    tile = jnp.concatenate(pieces, axis=0)
    if tile.shape[0] < snd_ref.shape[1]:
        tile = jnp.concatenate(
            [tile, jnp.zeros((snd_ref.shape[1] - tile.shape[0], lane), f32)], axis=0
        )
    for d in range(snd_ref.shape[0]):
        snd_ref[d] = tile


def sum_rows(v):
    return jnp.sum(v, axis=0, keepdims=True)


def forward_first(frames, ext, base, pick, x_ref, seg_ref, w_ref, a_ref, snd_ref, planes, w_vmem, sems):
    start_weights(w_ref, w_vmem, sems, pick)
    for c in range(planes.shape[0]):
        planes[c] = x_ref[:, cols(c)].astype(f32)
    rows = a_ref.shape[0]
    convolve(rows, base, planes, seg_ref, w_ref, w_vmem, sems, pick, False, row_dot, a_ref)
    own = slice(ext, ext + frames)
    first, second = [], []
    for c in range(a_ref.shape[1] // lane):
        v = a_ref[own, cols(c)]
        first.append(sum_rows(v))
        second.append(sum_rows(v * v))
    broadcast_sums(snd_ref, first + second)


def forward_next(
    frames, ext, base, samples, pick,
    prev_ref, st_ref, gs_ref, seg_ref, w_ref,
    a_ref, h_ref, snd_ref,
    planes, w_vmem, sems,
):
    start_weights(w_ref, w_vmem, sems, pick)
    blocks = planes.shape[0]
    total = jnp.sum(st_ref[...], axis=0)
    inner = slice(ext + half_taps, ext + half_taps + frames)
    for c, (mean, rstd) in enumerate(moments(total, 0, blocks, samples)):
        z = (prev_ref[:, cols(c)] - mean) * (rstd * gs_ref[c : c + 1])
        z = z + gs_ref[blocks + c : blocks + c + 1]
        low = (z * sigmoid(z)).astype(bf16)
        planes[c] = low.astype(f32)
        h_ref[:, cols(c)] = low[inner]
    convolve(a_ref.shape[0], base, planes, seg_ref, w_ref, w_vmem, sems, pick, False, row_dot, a_ref)
    own = slice(ext, ext + frames)
    first, second = [], []
    for c in range(blocks):
        v = a_ref[own, cols(c)]
        first.append(sum_rows(v))
        second.append(sum_rows(v * v))
    broadcast_sums(snd_ref, first + second)


def branch_operands(pl_ref, x_ref, rw_ref, rows, offset, x_offset, branch):
    sizes = (pl_ref.shape[1] // 2, pl_ref.shape[1] // 2, x_ref.shape[1])
    at = sum(sizes[:branch])
    w = rw_ref[:, at : at + sizes[branch]]
    if branch == 2:
        return x_ref[x_offset : x_offset + rows], w
    return pl_ref[offset : offset + rows, at : at + sizes[branch]], w


def branch_sums(frames, pl_ext, x_ext, pl_ref, x_ref, rw_ref, snd_ref):
    blocks = rw_ref.shape[0] // lane
    pieces = []
    for branch in range(3):
        p, w = branch_operands(pl_ref, x_ref, rw_ref, frames, pl_ext, x_ext, branch)
        q = dot(p, w, row_dot)
        pieces += [sum_rows(q[:, cols(c)]) for c in range(blocks)]
        pieces += [sum_rows(q[:, cols(c)] * q[:, cols(c)]) for c in range(blocks)]
    broadcast_sums(snd_ref, pieces)


def join(
    frames, ext, x_ext, samples,
    a_ref, st_ref, gs_ref, pl_ref, x_ref, rw_ref, qst_ref, rgs_ref, cot_ref,
    out_ref, du_ref, snd_ref, snd_res_ref,
    q_ref,
):
    rows, blocks = a_ref.shape[0], a_ref.shape[1] // lane
    for branch in range(3):
        p, w = branch_operands(pl_ref, x_ref, rw_ref, rows, 0, x_ext - ext, branch)
        q_ref[branch] = dot(p, w, row_dot)
    total = jnp.sum(st_ref[...], axis=0)
    res_total = jnp.sum(qst_ref[...], axis=0)
    main = moments(total, 0, blocks, samples)
    res = [moments(res_total, 2 * blocks * branch, blocks, samples) for branch in range(3)]
    own = slice(ext, ext + frames)
    shift_sums, gain_sums, res_sums = [], [], [[], [], []]
    for c in range(blocks):
        normed = (a_ref[:, cols(c)] - main[c][0]) * main[c][1]
        u = normed * gs_ref[c : c + 1] + gs_ref[blocks + c : blocks + c + 1]
        for branch in range(3):
            mean, rstd = res[branch][c]
            at = branch * blocks + c
            qn = (q_ref[branch, :, cols(c)] - mean) * rstd
            q_ref[branch, :, cols(c)] = qn
            u = u + qn * rgs_ref[at : at + 1] + rgs_ref[3 * blocks + at : 3 * blocks + at + 1]
        s = sigmoid(u)
        out_ref[:, cols(c)] = (u * s)[own].astype(bf16)
        du = cot_ref[:, cols(c)].astype(f32) * (s * (1.0 + u * (1.0 - s)))
        du_ref[:, cols(c)] = du
        du = du[own]
        shift_sums.append(sum_rows(du))
        gain_sums.append(sum_rows(du * normed[own]))
        for branch in range(3):
            res_sums[branch].append(sum_rows(du * q_ref[branch, own, cols(c)]))
    broadcast_sums(snd_ref, shift_sums + gain_sums)
    broadcast_sums(snd_res_ref, res_sums[0] + res_sums[1] + res_sums[2])


def branch_grads(
    frames, ext, x_ext, samples,
    du_ref, bst_ref, rst_ref, pl_ref, x_ref, rw_ref, qst_ref, rgs_ref,
    g0_ref, g1_ref, g2_ref, gw_ref,
):
    blocks = rw_ref.shape[0] // lane
    total = jnp.sum(bst_ref[...], axis=0) * (1.0 / samples)
    gains = jnp.sum(rst_ref[...], axis=0) * (1.0 / samples)
    res_total = jnp.sum(qst_ref[...], axis=0)
    own = slice(ext, ext + frames)
    at_col = 0
    for branch, g_ref in enumerate((g0_ref, g1_ref, g2_ref)):
        p, w = branch_operands(pl_ref, x_ref, rw_ref, frames, ext, x_ext, branch)
        q = dot(p, w, row_dot)
        low = []
        for c, (mean, rstd) in enumerate(moments(res_total, 2 * blocks * branch, blocks, samples)):
            at = branch * blocks + c
            qn = (q[:, cols(c)] - mean) * rstd
            v = du_ref[own, cols(c)] - total[c : c + 1] - qn * gains[at : at + 1]
            low.append((v * (rgs_ref[at : at + 1] * rstd)).astype(bf16))
        low = jnp.concatenate(low, axis=1)
        g_ref[...] = dot(low, w, plain_dot).astype(g_ref.dtype)
        width = p.shape[1]
        gw_ref[:, at_col : at_col + width] = dot(low, p, column_dot).astype(bf16)
        at_col += width


def backward_step(
    frames, ext_da, off_a, off_prev, base, samples, pick, last,
    table_ref, dz_ref, bst_ref, a_ref, st_ref, gs_ref, seg_ref, w_ref, prev_ref, prev_st_ref, prev_gs_ref,
    out_ref, x_ref, snd_ref,
    planes, turned, w_vmem, sems, acc_ref,
):
    start_weights(w_ref, w_vmem, sems, pick)
    rows, blocks = dz_ref.shape[0], dz_ref.shape[1] // lane
    sums = jnp.sum(bst_ref[...], axis=0) * (1.0 / samples)
    total = jnp.sum(st_ref[...], axis=0)
    for c, (mean, rstd) in enumerate(moments(total, 0, blocks, samples)):
        normed = (a_ref[off_a : off_a + rows, cols(c)] - mean) * rstd
        v = dz_ref[:, cols(c)] - sums[c : c + 1] - normed * sums[blocks + c : blocks + c + 1]
        planes[c, 0:rows] = (v * (gs_ref[c : c + 1] * rstd)).astype(bf16).astype(f32)
    at = ext_da - half_taps
    wide = turned.shape[1]
    for c in range(blocks):
        turned[cols(c), :] = planes[c, at : at + wide].T.astype(bf16)
    for r in range(group):
        for s in range(4):
            row = pl.multiple_of(table_ref[4 * r + s], unit)
            x_ref[r & 1, (r >> 1) & 1, r >> 2, s * unit : (s + 1) * unit, :] = turned[
                pl.ds(row, unit), :
            ]
    out_rows = rows - 2 * half_taps
    convolve(
        out_rows, base, planes, seg_ref, w_ref, w_vmem, sems, pick, True, plain_dot, acc_ref
    )
    if last:
        out_ref[...] = (acc_ref[...] + prev_ref[...]).astype(out_ref.dtype)
        return
    prev_total = jnp.sum(prev_st_ref[...], axis=0)
    own = slice(ext_da - half_taps, ext_da - half_taps + frames)
    shift_sums, gain_sums = [], []
    for c, (mean, rstd) in enumerate(moments(prev_total, 0, blocks, samples)):
        normed = (prev_ref[off_prev : off_prev + out_rows, cols(c)] - mean) * rstd
        z = normed * prev_gs_ref[c : c + 1] + prev_gs_ref[blocks + c : blocks + c + 1]
        s = sigmoid(z)
        dz = acc_ref[:, cols(c)] * (s * (1.0 + z * (1.0 - s)))
        out_ref[:, cols(c)] = dz
        dz = dz[own]
        shift_sums.append(sum_rows(dz))
        gain_sums.append(sum_rows(dz * normed[own]))
    broadcast_sums(snd_ref, shift_sums + gain_sums)


def weight_grads(frames, taps, sources, x_refs, h_refs, segs_ref, keep_ref, send_ref, left, acc_ref, h_vmem, sems):
    chunks = len(sources)

    def copies(r):
        slot = r % 2
        at, made = 0, []
        for n, (i, index, rows) in enumerate(sources[r][1]):
            src = h_refs[i].at[index] if index is not None else h_refs[i]
            made.append(
                pltpu.make_async_copy(src, h_vmem.at[slot, at : at + rows], sems.at[slot, n])
            )
            at += rows
        return made

    for copy in copies(0):
        copy.start()
    for r in range(chunks):
        if r + 1 < chunks:
            for copy in copies(r + 1):
                copy.start()
        i, index = sources[r][0]
        part = x_refs[i][index]
        seg = segs_ref[r]
        centre = seg[:, half_taps : half_taps + frames]
        for k in range(taps):
            mask = jnp.where(seg[:, k : k + frames] == centre, 1.0, 0.0).astype(bf16)
            mask = jnp.concatenate([mask] * (4 * unit // mask.shape[0]), axis=0)
            left[(taps - 1 - k) * 4 * unit : (taps - k) * 4 * unit, :] = (
                part[:, k : k + frames] * mask
            )
        for copy in copies(r):
            copy.wait()
        d = dot(left[...], h_vmem[r % 2], plain_dot)
        if r == 0:
            acc_ref[...] = d
        else:
            acc_ref[...] += d
    for k in range(taps):
        at = k * 4 * unit
        keep_ref[k] = acc_ref[at : at + 2 * unit]
        send_ref[k] = acc_ref[at + 2 * unit : at + 4 * unit].astype(bf16)


def call(body, name, out_shape, in_specs, scratch, flops, byte_count, args, out_specs=None):
    out_specs = out_specs or jax.tree.map(lambda _: in_vmem(), out_shape)
    return pl.pallas_call(
        body,
        out_shape=out_shape,
        in_specs=in_specs,
        out_specs=out_specs,
        scratch_shapes=scratch,
        compiler_params=pltpu.CompilerParams(vmem_limit_bytes=vmem_budget),
        cost_estimate=pl.CostEstimate(flops=flops, bytes_accessed=byte_count, transcendentals=0),
        name=name,
    )(*args)


def per_device(
    block_entry_input,
    prelude_output,
    leading_block_output,
    lengths,
    leading_conv_weight,
    remaining_conv_weight,
    gain,
    shift,
    residual_pointwise_weight,
    residual_norm_scale,
    residual_norm_bias,
    cotangent,
):
    tm, rows_axis = lax.axis_size("tm"), lax.axis_size("batch")
    everyone = ("tm", "batch")
    devices = tm * rows_axis
    place = lax.axis_index("tm")
    row_place = lax.axis_index("batch")
    frames, entry_width = block_entry_input.shape[1:]
    channels, taps = leading_conv_weight.shape[:2]
    blocks = channels // lane
    layers = remaining_conv_weight.shape[0] + 1
    samples = float(frames * tm * rows_axis)
    reach = half_taps * 2 * layers
    ext = [reach - half_taps * i for i in range(layers + 1)]
    ext_u = ext[layers]
    split_rows = rows_axis == 2 and channels // tm == 2 * unit

    def sds(shape, dtype):
        return jax.ShapeDtypeStruct(shape, dtype)

    def swap(v, axis, bit):
        n = lax.axis_size(axis)
        return lax.ppermute(v, axis, [(i, i ^ bit) for i in range(n)])

    def spread(v):
        return lax.all_to_all(v, everyone, 0, 0, tiled=True)

    x_own, cot_own = block_entry_input[0], cotangent[0]
    pl_own = jnp.concatenate([prelude_output[0], leading_block_output[0]], axis=1)

    def edge(part):
        side = jnp.concatenate([part(pl_own, ext_u), part(cot_own, ext_u)], axis=0)
        return jnp.concatenate([part(x_own, reach), side], axis=1)

    tail_rows = edge(lambda v, n: v[frames - n :])
    head_rows = edge(lambda v, n: v[:n])
    low = lax.ppermute(tail_rows, "tm", [(i, i + 1) for i in range(tm - 1)])
    high = lax.ppermute(head_rows, "tm", [(i + 1, i) for i in range(tm - 1)])
    x_ext = jnp.concatenate([low[:, :entry_width], x_own, high[:, :entry_width]], axis=0)
    pl_ext = jnp.concatenate(
        [low[:ext_u, entry_width:], pl_own, high[:ext_u, entry_width:]], axis=0
    )
    cot_ext = jnp.concatenate(
        [low[ext_u:, entry_width:], cot_own, high[ext_u:, entry_width:]], axis=0
    )

    counts = lengths[0]
    number = counts.shape[0]
    order = jnp.arange(number)
    starts = jnp.sum(jnp.where(order[None, :] < order[:, None], counts[None, :], 0), axis=1)

    def segments(position):
        inside = sum((position >= starts[j]).astype(f32) for j in range(number))
        inside = jnp.where(position < 0, 0.0, inside)
        return jnp.where(position < frames * tm, inside, -1.0)

    seg = segments(
        place * frames - reach + lax.broadcasted_iota(jnp.int32, (frames + 2 * reach, lane), 0)
    )
    wide = -(-(frames + 2 * half_taps) // lane) * lane
    relative = lax.broadcasted_iota(jnp.int32, (group, unit, wide), 0)
    segs = segments(
        (place ^ relative) * frames
        - half_taps
        + lax.broadcasted_iota(jnp.int32, (group, unit, wide), 2)
    )

    peer = (jnp.arange(group, dtype=jnp.int32) ^ (place % group))[:, None]
    slot = jnp.arange(4, dtype=jnp.int32)[None, :]
    high_place = place // group
    if split_rows:
        table = ((high_place ^ (slot % 2)) * group + peer) * (2 * unit)
        table = table + (row_place ^ (slot // 2)) * unit
    else:
        table = ((high_place ^ slot) * group + peer) * unit
    table = table.reshape(-1).astype(jnp.int32)

    w_first = jnp.transpose(leading_conv_weight, (1, 0, 2))
    w_rest = jnp.transpose(remaining_conv_weight, (0, 2, 1, 3))

    def weights(layer):
        if layer == 1:
            return w_first, (lambda ref, k: ref.at[k]), entry_width
        return w_rest, (lambda ref, k, at=layer - 2: ref.at[at, k]), channels

    def gain_shift(layer):
        return jnp.concatenate([gain[layer - 1], shift[layer - 1]]).reshape(2 * blocks, lane)

    gs = [None] + [gain_shift(i) for i in range(1, layers + 1)]
    res_gs = jnp.concatenate([residual_norm_scale, residual_norm_bias]).reshape(6 * blocks, lane)
    tile_sums = sds((devices, 2 * blocks, lane), f32)
    res_rows = -(-3 * blocks // 8) * 8

    def conv_scratch(planes_rows, width, w_shape):
        return [
            pltpu.VMEM((width // lane, planes_rows, lane), f32),
            pltpu.VMEM(w_shape, bf16),
            pltpu.SemaphoreType.DMA((taps,)),
        ]

    def conv_cost(rows, width):
        return 2 * rows * width * channels * taps, 2 * taps * width * channels + 8 * rows * channels

    def gather(h):
        over_y = swap(h, "tm", 2)
        over_z = swap(h, "tm", 4)
        half = frames // 2
        corner_a = swap(over_y[:half], "tm", 4)
        corner_b = swap(over_z[half:], "tm", 2)
        mine = [h, over_y, over_z, corner_a, corner_b]
        return mine + [swap(v, "tm", 1) for v in mine]

    def h_sources():
        full = frames
        half = frames // 2
        by_pair = {0: [(0, None, full)], 1: [(1, None, full)], 2: [(2, None, full)],
                   3: [(3, None, half), (4, None, half)]}
        out = []
        for r in range(group):
            entries = by_pair[r >> 1]
            out.append(tuple((i + 5 * (r & 1), index, n) for i, index, n in entries))
        return out

    def exchange(x):
        r1 = swap(x[1], "tm", 1)
        r2 = swap(jnp.stack([x[0, 1], r1[1]]), "tm", 2)
        r3 = swap(jnp.stack([x[0, 0, 1], r1[0, 1], r2[0, 1], r2[1, 1]]), "tm", 4)
        return [x, r1, r2, r3]

    x_sources = [
        (0, (0, 0, 0)), (1, (0, 0)), (2, (0, 0)), (2, (1, 0)),
        (3, (0,)), (3, (1,)), (3, (2,)), (3, (3,)),
    ]

    def weight_gradient(layer, parts, gathered):
        width = gathered[0].shape[1]
        sources = list(zip(x_sources, h_sources(), strict=True))
        nx, nh = len(parts), len(gathered)

        def body(*refs):
            x_refs, h_refs = refs[:nx], refs[nx : nx + nh]
            weight_grads(frames, taps, sources, x_refs, h_refs, *refs[nx + nh :])

        keep, send = call(
            body, "weight_grads",
            (sds((taps, 2 * unit, width), f32), sds((taps, 2 * unit, width), bf16)),
            [in_vmem()] * nx + [in_place()] * nh + [in_vmem()],
            [
                pltpu.VMEM((taps * 4 * unit, frames), bf16),
                pltpu.VMEM((taps * 4 * unit, width), f32),
                pltpu.VMEM((2, frames, width), bf16),
                pltpu.SemaphoreType.DMA((2, 2)),
            ],
            2 * taps * 4 * unit * frames * group * width,
            2 * group * frames * width,
            (*parts, *gathered, segs),
        )
        return keep, send

    def reduce_gradient(keep, send):
        first = ("batch", 1) if split_rows else ("tm", 2 * group)
        both = keep + swap(send, *first).astype(f32)
        part = both[:, :unit] + swap(both[:, unit:].astype(bf16), "tm", group).astype(f32)
        if not split_rows:
            return lax.psum(part.astype(bf16), "batch").astype(f32)
        part = part.astype(bf16)
        other = swap(part, "batch", 1)
        top = jnp.where(row_place == 0, part, other)
        bottom = jnp.where(row_place == 0, other, part)
        return jnp.concatenate([top, bottom], axis=1).astype(f32)

    row_count = [frames + 2 * e for e in ext]
    w, pick, width = weights(1)
    rows = row_count[1]
    flops, moved = conv_cost(rows, width)
    a, snd = call(
        functools.partial(forward_first, frames, ext[1], reach - ext[0], pick), "forward_first",
        (sds((rows, channels), f32), tile_sums),
        [in_vmem(), in_vmem(), in_place()],
        conv_scratch(row_count[0], width, (taps, channels, width)),
        flops, moved, (x_ext, seg, w),
    )
    stats = [None, spread(snd)]
    acts = [None, a]
    gathered = [gather(x_own)]
    q_snd = call(
        functools.partial(branch_sums, frames, ext_u, reach), "branch_sums",
        sds((devices, 6 * blocks, lane), f32),
        [in_vmem()] * 3, [], 2 * frames * residual_pointwise_weight.size, 4 << 20,
        (pl_ext, x_ext, residual_pointwise_weight),
    )
    q_stats = spread(q_snd)
    for layer in range(2, layers + 1):
        w, pick, width = weights(layer)
        rows = row_count[layer]
        flops, moved = conv_cost(rows, width)
        a, h, snd = call(
            functools.partial(
                forward_next, frames, ext[layer], reach - ext[layer - 1], samples, pick
            ),
            "forward_next",
            (sds((rows, channels), f32), sds((frames, channels), bf16), tile_sums),
            [in_vmem()] * 4 + [in_place()],
            conv_scratch(row_count[layer - 1], width, (taps, channels, width)),
            flops, moved, (acts[-1], stats[-1], gs[layer - 1], seg, w),
        )
        stats.append(spread(snd))
        acts.append(a)
        gathered.append(gather(h))

    rows = row_count[layers]
    block_output, dz, snd, res_snd = call(
        functools.partial(join, frames, ext_u, reach, samples), "join",
        (
            sds((frames, channels), bf16), sds((rows, channels), f32), tile_sums,
            sds((devices, res_rows, lane), f32),
        ),
        [in_vmem()] * 9,
        [pltpu.VMEM((3, rows, channels), f32)],
        2 * rows * residual_pointwise_weight.size, 8 << 20,
        (
            acts[layers], stats[layers], gs[layers], pl_ext, x_ext, residual_pointwise_weight,
            q_stats, res_gs, cot_ext,
        ),
    )
    du = dz
    back = [None] * (layers + 1)
    back[layers] = spread(snd)
    res_back = spread(res_snd)

    prelude_gradient, grad_first, res_entry, res_weight = call(
        functools.partial(branch_grads, frames, ext_u, reach, samples), "branch_grads",
        (
            sds((frames, prelude_output.shape[2]), bf16),
            sds((frames, leading_block_output.shape[2]), bf16),
            sds((frames, entry_width), f32),
            sds(residual_pointwise_weight.shape, bf16),
        ),
        [in_vmem()] * 8, [], 6 * frames * residual_pointwise_weight.size, 8 << 20,
        (du, back[layers], res_back, pl_ext, x_ext, residual_pointwise_weight, q_stats, res_gs),
    )
    res_share = lax.psum_scatter(res_weight, "tm", scatter_dimension=0, tiled=True)
    if rows_axis == 2:
        grad_res_weight = res_share.astype(f32) + swap(res_share, "batch", 1).astype(f32)
    else:
        grad_res_weight = lax.psum(res_share, "batch").astype(f32)

    grads = [None] * (layers + 1)
    for layer in range(layers, 0, -1):
        w, pick, width = weights(layer)
        ext_da = half_taps * layer
        rows = frames + 2 * ext_da
        out_rows = rows - 2 * half_taps
        last = layer == 1
        flops, moved = conv_cost(out_rows, width)
        prev = (res_entry, stats[1], gs[1]) if last else (
            acts[layer - 1], stats[layer - 1], gs[layer - 1]
        )
        out = sds((out_rows, width), bf16 if last else f32)
        planes_rows = max(rows, ext_da - half_taps + wide)
        dz, x, snd = call(
            functools.partial(
                backward_step, frames, ext_da, ext[layer] - ext_da,
                ext[layer - 1] - (ext_da - half_taps), reach - ext_da, samples, pick, last,
            ),
            "backward_step",
            (out, sds((2, 2, 2, 4 * unit, wide), bf16), tile_sums),
            [in_smem()] + [in_vmem()] * 6 + [in_place()] + [in_vmem()] * 3,
            [
                pltpu.VMEM((blocks, planes_rows, lane), f32),
                pltpu.VMEM((channels, wide), bf16),
                pltpu.VMEM((taps, channels, width), bf16),
                pltpu.SemaphoreType.DMA((taps,)),
                pltpu.VMEM((out_rows, width), f32),
            ],
            flops, moved,
            (table, dz, back[layer], acts[layer], stats[layer], gs[layer], seg, w, *prev),
        )
        if not last:
            back[layer - 1] = spread(snd)
        keep, send = weight_gradient(layer, exchange(x), gathered[layer - 1])
        grads[layer] = reduce_gradient(keep, send)

    grad_block_input = dz[None]
    width_dev = channels // tm

    def share(v):
        return lax.dynamic_slice_in_dim(v, place * width_dev, width_dev, axis=v.ndim - 1)

    sums = [None] + [jnp.sum(back[i], axis=0).reshape(2, channels) for i in range(1, layers + 1)]
    grad_gain = share(jnp.stack([sums[i][1] for i in range(1, layers + 1)]))
    grad_shift = share(jnp.stack([sums[i][0] for i in range(1, layers)]))
    grad_last_shift = share(sums[layers][0])
    res_sums = jnp.sum(res_back, axis=0)[: 3 * blocks].reshape(3, channels)
    grad_res_gain = share(res_sums)
    grad_res_shift = jnp.broadcast_to(grad_last_shift[None], (3, width_dev))
    grad_w_first = jnp.transpose(grads[1], (1, 0, 2))
    grad_w_rest = jnp.transpose(jnp.stack(grads[2:]), (0, 2, 1, 3))
    return (
        block_output[None],
        grad_block_input,
        prelude_gradient[None],
        grad_first[None],
        grad_w_first,
        grad_w_rest,
        grad_gain,
        grad_shift,
        grad_last_shift,
        grad_res_weight,
        grad_res_gain,
        grad_res_shift,
    )


def solution(mesh):
    split = P("batch", "tm", None)
    in_specs = (
        split, split, split, P("batch", None), P(), P(), P(), P(), P(), P(), P(), split,
    )
    out_specs = (
        split, split, split, split,
        P("tm", None, None), P(None, "tm", None, None), P(None, "tm"), P(None, "tm"), P("tm"),
        P("tm", None), P(None, "tm"), P(None, "tm"),
    )
    return jax.shard_map(
        per_device, mesh=mesh, in_specs=in_specs, out_specs=out_specs, check_vma=False
    )
```

```python
import functools

import jax
import jax.numpy as jnp
from jax import lax
from jax.experimental import pallas as pl
from jax.experimental.pallas import tpu as pltpu
from jax.sharding import PartitionSpec as P

norm_eps = 0.001
lane = 128
half_taps = 8
group = 8
bf16 = jnp.bfloat16
f32 = jnp.float32

row_dot = (((1,), (1,)), ((), ()))
plain_dot = (((1,), (0,)), ((), ()))
column_dot = (((0,), (0,)), ((), ()))


def in_vmem():
    return pl.BlockSpec(memory_space=pltpu.VMEM)


def in_place():
    return pl.BlockSpec(memory_space=pl.ANY)


def in_smem():
    return pl.BlockSpec(memory_space=pltpu.SMEM)


def dot(a, b, dims):
    return lax.dot_general(a, b, dims, preferred_element_type=f32)


def cols(c):
    return slice(c * lane, (c + 1) * lane)


def sigmoid(v):
    return 1.0 / (1.0 + jnp.exp(-v))


def sum_rows(v):
    return jnp.sum(v, axis=0, keepdims=True)


def moments(total, row, count, samples):
    out = []
    for c in range(count):
        mean = total[row + c : row + c + 1] * (1.0 / samples)
        spread = total[row + count + c : row + count + c + 1] * (1.0 / samples) - mean * mean
        out.append((mean, lax.rsqrt(spread + norm_eps)))
    return out


class Copies:
    def __init__(self, sems):
        self.sems, self.count = sems, 0

    def start(self, src, dst):
        copy = pltpu.make_async_copy(src, dst, self.sems.at[self.count])
        self.count += 1
        copy.start()
        return copy

    def load(self, pairs):
        return [self.start(src, dst) for src, dst in pairs]


def wait_all(copies):
    for copy in copies:
        copy.wait()


def start_weights(copies, w_ref, w_vmem, layer, order):
    made = {}
    for k in order:
        made[k] = copies.start(w_ref.at[k] if layer is None else w_ref.at[layer, k], w_vmem.at[k])
    return made


def convolve(rows, base, planes, seg_ref, w_vmem, w_copies, flip, dims, acc_ref):
    taps = w_vmem.shape[0]
    blocks = planes.shape[0]
    for k in range(taps):
        tap = taps - 1 - k if flip else k
        w_copies[tap].wait()
        mask = (
            seg_ref[base + k : base + k + rows]
            == seg_ref[base + half_taps : base + half_taps + rows]
        )
        x = jnp.concatenate(
            [jnp.where(mask, planes[c, k : k + rows], 0.0).astype(bf16) for c in range(blocks)],
            axis=1,
        )
        d = dot(x, w_vmem[tap], dims)
        if k == 0:
            acc_ref[...] = d
        else:
            acc_ref[...] += d


def send_sums(copies, pieces, wide_ref, snd_ref):
    tile = jnp.concatenate(pieces, axis=0)
    short = wide_ref.shape[1] - tile.shape[0]
    if short:
        tile = jnp.concatenate([tile, jnp.zeros((short, lane), f32)], axis=0)
    for d in range(wide_ref.shape[0]):
        wide_ref[d] = tile
    return copies.start(wide_ref, snd_ref)


def conv_sums(a_ref, own):
    first, second = [], []
    for c in range(a_ref.shape[1] // lane):
        v = a_ref[own, cols(c)]
        first.append(sum_rows(v))
        second.append(sum_rows(v * v))
    return first + second


def segment_of(position, counts_ref, end, row=0):
    number = counts_ref.shape[1]
    at = lax.broadcasted_iota(jnp.int32, (1, lane), 1)
    starts, start = jnp.full((1, lane), end + lane * lane, jnp.int32), jnp.int32(0)
    for j in range(number):
        starts = jnp.where(at == j, start, starts)
        start = start + counts_ref[row, j]
    begun = jnp.where(position >= starts, 1.0, 0.0).astype(bf16)
    inside = dot(begun, jnp.ones((lane, lane), bf16), plain_dot)
    return jnp.where(position < end, inside, -1.0)


def prepare(
    frames, end, reach,
    place_ref, counts_ref, x_ref,
    seg_ref, x_tail, x_head,
    sems,
):
    copies = Copies(sems)
    edge = x_tail.shape[0]
    first = copies.load([(x_ref.at[frames - edge :], x_tail), (x_ref.at[:edge], x_head)])
    rows = lax.broadcasted_iota(jnp.int32, seg_ref.shape, 0)
    seg_ref[...] = segment_of(place_ref[0] * frames - reach + rows, counts_ref, end)
    wait_all(first)


def pack_sides(frames, p_ref, l_ref, cot_ref, s_tail, s_head, sems):
    copies = Copies(sems)
    side = s_tail.shape[0]
    at, made = 0, []
    for ref in (p_ref, l_ref, cot_ref):
        width = ref.shape[1]
        made.append(copies.start(ref.at[frames - side :], s_tail.at[:, at : at + width]))
        made.append(copies.start(ref.at[:side], s_head.at[:, at : at + width]))
        at += width
    wait_all(made)


def chunk_segments(frames, end, chunks, place_ref, counts_ref, out_ref):
    ahead = lax.broadcasted_iota(jnp.int32, out_ref.shape[1:], 0) - half_taps
    for r in range(chunks):
        row = place_ref[1, r]
        out_ref[r] = segment_of(place_ref[0, r] * frames + ahead, counts_ref, end, row).astype(bf16)


def forward_first(
    frames, ext, base,
    x_ref, low_ref, high_ref, seg_hbm, w_ref,
    a_ref, snd_ref,
    x_v, planes, seg_ref, w_vmem, acc_ref, wide_ref, sems,
):
    copies = Copies(sems)
    taps = w_vmem.shape[0]
    edge = low_ref.shape[0]
    first = copies.load([
        (x_ref, x_v.at[edge : edge + frames]), (low_ref, x_v.at[:edge]), (high_ref, x_v.at[edge + frames :]),
        (seg_hbm, seg_ref),
    ])
    w_copies = start_weights(copies, w_ref, w_vmem, None, range(taps))
    wait_all(first)
    for c in range(planes.shape[0]):
        planes[c] = x_v[:, cols(c)].astype(f32)
    convolve(acc_ref.shape[0], base, planes, seg_ref, w_vmem, w_copies, False, row_dot, acc_ref)
    out = copies.start(acc_ref, a_ref)
    sent = send_sums(copies, conv_sums(acc_ref, slice(ext, ext + frames)), wide_ref, snd_ref)
    wait_all([out, sent])


def forward_next(
    frames, ext, base, samples, layer, with_extra,
    prev_hbm, st_hbm, gain_hbm, shift_hbm, seg_hbm, w_ref, *rest,
):
    extra_hbm, rest = (rest[0], rest[1:]) if with_extra else (None, rest)
    a_ref, h_ref, snd_ref, gain_ref, shift_ref, prev_ref, st_ref, low_ref, planes = rest[:9]
    seg_ref, w_vmem, acc_ref, wide_ref, sems = rest[9:14]
    copies = Copies(sems)
    blocks = planes.shape[0]
    small = copies.load([(st_hbm, st_ref), (gain_hbm, gain_ref), (shift_hbm, shift_ref)])
    prev_copies = [copies.start(prev_hbm.at[:, cols(c)], prev_ref.at[:, cols(c)]) for c in range(blocks)]
    seg_copy = copies.start(seg_hbm, seg_ref)
    w_copies = start_weights(copies, w_ref, w_vmem, layer - 2, range(w_vmem.shape[0]))
    extra = None
    if with_extra:
        extra = copies.start(extra_hbm.at[layer - 2], rest[14])
    wait_all(small)
    total = jnp.sum(st_ref[...], axis=0)
    inner = slice(ext + half_taps, ext + half_taps + frames)
    prev = slice(layer - 2, layer - 1)
    for c, (mean, rstd) in enumerate(moments(total, 0, blocks, samples)):
        prev_copies[c].wait()
        z = (prev_ref[:, cols(c)] - mean) * (rstd * gain_ref[prev, cols(c)])
        z = z + shift_ref[prev, cols(c)]
        low = (z * sigmoid(z)).astype(bf16)
        planes[c] = low.astype(f32)
        low_ref[:, cols(c)] = low[inner]
    h_copy = copies.start(low_ref, h_ref)
    seg_copy.wait()
    convolve(acc_ref.shape[0], base, planes, seg_ref, w_vmem, w_copies, False, row_dot, acc_ref)
    out = copies.start(acc_ref, a_ref)
    pieces = conv_sums(acc_ref, slice(ext, ext + frames))
    if with_extra:
        extra.wait()
        pieces.append(rest[14][...])
    sent = send_sums(copies, pieces, wide_ref, snd_ref)
    wait_all([h_copy, out, sent])


def branch_weights(rw_ref, sources):
    at, out = 0, []
    for p in sources:
        out.append(rw_ref[:, at : at + p.shape[1]])
        at += p.shape[1]
    return out


def branch_sums(p_ref, l_ref, x_ref, rw_ref, out_ref):
    blocks = rw_ref.shape[0] // lane
    sources = (p_ref, l_ref, x_ref)
    for branch, (p, w) in enumerate(zip(sources, branch_weights(rw_ref, sources), strict=True)):
        q = dot(p[...], w, row_dot)
        for c in range(blocks):
            out_ref[branch, c : c + 1] = sum_rows(q[:, cols(c)])
            out_ref[branch, blocks + c : blocks + c + 1] = sum_rows(q[:, cols(c)] * q[:, cols(c)])


def join(
    frames, ext, samples, layer,
    a_hbm, st_hbm, gain_ref, shift_ref, p_ref, l_ref, x_ref, rw_ref, q0_hbm, q1_hbm, q2_hbm, rg_ref, rb_ref, cot_ref,
    x_low, x_high, s_low, s_high,
    out_ref, du_ref, snd_ref, snd_res_ref, q_tot_ref,
    a_ref, st_ref, qst_refs, q_ref, du_v, out_v, wide_ref, wide_res_ref, sems,
):
    copies = Copies(sems)
    blocks = a_ref.shape[1] // lane
    first = copies.load(
        [(q, qst_refs.at[i]) for i, q in enumerate((q0_hbm, q1_hbm, q2_hbm))]
        + [(st_hbm, st_ref), (a_hbm, a_ref)]
    )
    sources = (p_ref, l_ref, x_ref)
    edge, side = x_low.shape[0], s_low.shape[0]
    own = slice(ext, ext + frames)
    at = 0
    for branch, w in enumerate(branch_weights(rw_ref, sources)):
        width = sources[branch].shape[1]
        if branch < 2:
            low, high = s_low[:, at : at + width], s_high[:, at : at + width]
            at += width
        else:
            low, high = x_low[edge - side :], x_high[:side]
        q_ref[branch, :ext] = dot(low, w, row_dot)[side - ext :]
        q_ref[branch, own] = dot(sources[branch][...], w, row_dot)
        q_ref[branch, ext + frames :] = dot(high, w, row_dot)[:ext]
    wait_all(first)
    total = jnp.sum(st_ref[...], axis=0)
    main = moments(total, 0, blocks, samples)
    res = []
    for branch in range(3):
        q_tot_ref[branch] = jnp.sum(qst_refs[branch], axis=0)[2 * blocks :]
        res.append(moments(q_tot_ref[branch], 0, blocks, samples))
    shift_sums, gain_sums, res_sums, done = [], [], [[], [], []], []
    mine = slice(layer - 1, layer)
    for c in range(blocks):
        normed = (a_ref[:, cols(c)] - main[c][0]) * main[c][1]
        u = normed * gain_ref[mine, cols(c)] + shift_ref[mine, cols(c)]
        for branch in range(3):
            mean, rstd = res[branch][c]
            qn = (q_ref[branch, :, cols(c)] - mean) * rstd
            q_ref[branch, :, cols(c)] = qn
            u = u + qn * rg_ref[branch : branch + 1, cols(c)] + rb_ref[branch : branch + 1, cols(c)]
        s = sigmoid(u)
        out_v[:, cols(c)] = (u * s)[own].astype(bf16)
        slope = s * (1.0 + u * (1.0 - s))
        cot = slice(at + c * lane, at + (c + 1) * lane)
        du_v[:ext, cols(c)] = s_low[:, cot].astype(f32)[side - ext :] * slope[:ext]
        du_v[ext + frames :, cols(c)] = s_high[:, cot].astype(f32)[:ext] * slope[ext + frames :]
        du = cot_ref[:, cols(c)].astype(f32) * slope[own]
        du_v[own, cols(c)] = du
        done.append(copies.start(du_v.at[:, cols(c)], du_ref.at[:, cols(c)]))
        shift_sums.append(sum_rows(du))
        gain_sums.append(sum_rows(du * normed[own]))
        for branch in range(3):
            res_sums[branch].append(sum_rows(du * q_ref[branch, own, cols(c)]))
    done.append(copies.start(out_v, out_ref))
    done.append(send_sums(copies, shift_sums + gain_sums, wide_ref, snd_ref))
    done.append(send_sums(copies, res_sums[0] + res_sums[1] + res_sums[2], wide_res_ref, snd_res_ref))
    wait_all(done)


def branch_grads(
    frames, ext, samples,
    du_ref, bst_ref, rst_ref, p_ref, l_ref, x_ref, rw_ref, qst_ref, rg_ref,
    g0_ref, g1_ref, g2_ref, gw_ref, tot_ref,
):
    blocks = rw_ref.shape[0] // lane
    total = jnp.sum(bst_ref[...], axis=0) * (1.0 / samples)
    gains = jnp.sum(rst_ref[...], axis=0)
    tot_ref[...] = gains
    gains = gains * (1.0 / samples)
    own = slice(ext, ext + frames)
    sources = (p_ref, l_ref, x_ref)
    at_col = 0
    for branch, (g_ref, w) in enumerate(
        zip((g0_ref, g1_ref, g2_ref), branch_weights(rw_ref, sources), strict=True)
    ):
        p = sources[branch][...]
        q = dot(p, w, row_dot)
        low = []
        for c, (mean, rstd) in enumerate(moments(qst_ref[branch], 0, blocks, samples)):
            at = branch * blocks + c
            qn = (q[:, cols(c)] - mean) * rstd
            v = du_ref[own, cols(c)] - total[c : c + 1] - qn * gains[at : at + 1]
            low.append((v * (rg_ref[branch : branch + 1, cols(c)] * rstd)).astype(bf16))
        low = jnp.concatenate(low, axis=1)
        g_ref[...] = dot(low, w, plain_dot).astype(g_ref.dtype)
        width = p.shape[1]
        gw_ref[:, at_col : at_col + width] = dot(low, p, column_dot).astype(bf16)
        at_col += width


def channel_order(channels, peers, unit):
    per = channels // peers
    n = lax.broadcasted_iota(jnp.int32, (1, channels), 1)
    source = (n % per // unit * peers + n // per) * unit + n % unit
    row = lax.broadcasted_iota(jnp.int32, (channels, channels), 0)
    return jnp.where(row == source, 1.0, 0.0).astype(bf16)


def lane_group(per):
    return lax.broadcasted_iota(jnp.int32, (1, lane), 1) // per


def turn(v, lanes):
    return pltpu.roll(v, lanes % lane, 1) if lanes % lane else v


def pick_lanes(which, parts):
    out = parts[0]
    for j in range(1, len(parts)):
        out = jnp.where(which == j, parts[j], out)
    return out


class InputGrad:
    def __init__(self, copies, bst_hbm, st_hbm, dz_hbm, a_hbm, bst_v, st_v, dz_v, a_v, off_a):
        rows, channels = dz_v.shape
        self.blocks = channels // lane
        self.bst_v, self.st_v, self.dz_v, self.a_v = bst_v, st_v, dz_v, a_v
        self.first = copies.load([(bst_hbm, bst_v), (st_hbm, st_v)])
        self.columns = [
            copies.load([
                (dz_hbm.at[:, cols(c)], dz_v.at[:, cols(c)]),
                (a_hbm.at[off_a : off_a + rows, cols(c)], a_v.at[:, cols(c)]),
            ])
            for c in range(self.blocks)
        ]

    def make(self, samples, gain_row, tot_ref, at, low_ref, put):
        blocks = self.blocks
        wait_all(self.first)
        sums = jnp.sum(self.bst_v[...], axis=0)
        tot_ref[...] = sums
        sums = sums * (1.0 / samples)
        total = jnp.sum(self.st_v[...], axis=0)
        near = low_ref.shape[0]
        for c, (mean, rstd) in enumerate(moments(total, 0, blocks, samples)):
            wait_all(self.columns[c])
            normed = (self.a_v[:, cols(c)] - mean) * rstd
            v = self.dz_v[:, cols(c)] - sums[c : c + 1] - normed * sums[blocks + c : blocks + c + 1]
            low = (v * (gain_row[:, cols(c)] * rstd)).astype(bf16)
            put(c, low)
            low_ref[:, cols(c)] = low.astype(f32)[at : at + near].astype(bf16)


def pack_peers(frames, unit, low_ref, xs_ref):
    channels = low_ref.shape[1]
    peers, held = xs_ref.shape[:2]
    per = channels // peers
    fold = lane // per
    step = frames // fold
    which = lane_group(per)
    ordered = dot(low_ref[...], channel_order(channels, peers, unit), plain_dot)
    for c in range(channels // lane):
        v = ordered[:, cols(c)]
        turned = [turn(v, i * per) for i in range(fold)]
        for i in range(fold):
            parts = [turned[(j - i) % fold][j * step : j * step + held] for j in range(fold)]
            xs_ref[fold * c + i] = pick_lanes(which, parts).astype(bf16)


def backward_step(
    frames, ext_da, off_a, off_prev, base, samples, layer, unit,
    dz_hbm, bst_hbm, a_hbm, st_hbm, gain_hbm, shift_hbm, seg_hbm, w_ref, prev_hbm, prev_st_hbm,
    out_ref, x_ref, tot_ref, snd_ref,
    gain_ref, shift_ref, dz_v, bst_v, a_v, st_v, seg_ref, prev_v, prev_st_v, planes, low_ref, xs_ref, w_vmem, acc_ref, out_v, wide_ref,
    sems,
):
    copies = Copies(sems)
    affine = copies.load([(gain_hbm, gain_ref), (shift_hbm, shift_ref)])
    grad = InputGrad(copies, bst_hbm, st_hbm, dz_hbm, a_hbm, bst_v, st_v, dz_v, a_v, off_a)
    rows, channels = dz_v.shape
    blocks = channels // lane
    seg_copy = copies.start(seg_hbm, seg_ref)
    w_copies = start_weights(copies, w_ref, w_vmem, layer - 2, range(w_vmem.shape[0] - 1, -1, -1))
    out_rows = rows - 2 * half_taps
    late = copies.load([
        (prev_hbm.at[off_prev : off_prev + out_rows], prev_v), (prev_st_hbm, prev_st_v),
    ])

    def put(c, low):
        planes[c] = low.astype(f32)

    at = ext_da - half_taps
    wait_all(affine)
    grad.make(samples, gain_ref[layer - 1 : layer], tot_ref, at, low_ref, put)
    pack_peers(frames, unit, low_ref, xs_ref)
    x_copy = copies.start(xs_ref, x_ref)
    seg_copy.wait()
    convolve(out_rows, base, planes, seg_ref, w_vmem, w_copies, True, plain_dot, acc_ref)
    wait_all(late)
    prev_total = jnp.sum(prev_st_v[...], axis=0)
    own = slice(at, at + frames)
    shift_sums, gain_sums, done = [], [], [x_copy]
    before = slice(layer - 2, layer - 1)
    for c, (mean, rstd) in enumerate(moments(prev_total, 0, blocks, samples)):
        normed = (prev_v[:, cols(c)] - mean) * rstd
        z = normed * gain_ref[before, cols(c)] + shift_ref[before, cols(c)]
        s = sigmoid(z)
        dz = acc_ref[:, cols(c)] * (s * (1.0 + z * (1.0 - s)))
        out_v[:, cols(c)] = dz
        done.append(copies.start(out_v.at[:, cols(c)], out_ref.at[:, cols(c)]))
        dz = dz[own]
        shift_sums.append(sum_rows(dz))
        gain_sums.append(sum_rows(dz * normed[own]))
    done.append(send_sums(copies, shift_sums + gain_sums, wide_ref, snd_ref))
    wait_all(done)


def backward_norm(
    frames, ext_da, off_a, samples, layer, unit,
    dz_hbm, bst_hbm, a_hbm, st_hbm, gain_hbm,
    da_ref, x_ref, tot_ref,
    gain_ref, dz_v, bst_v, a_v, st_v, da_v, low_ref, xs_ref, sems,
):
    copies = Copies(sems)
    affine = copies.start(gain_hbm, gain_ref)
    grad = InputGrad(copies, bst_hbm, st_hbm, dz_hbm, a_hbm, bst_v, st_v, dz_v, a_v, off_a)
    affine.wait()

    def put(c, low):
        da_v[:, cols(c)] = low

    grad.make(samples, gain_ref[layer - 1 : layer], tot_ref, ext_da - half_taps, low_ref, put)
    pack_peers(frames, unit, low_ref, xs_ref)
    wait_all(copies.load([(xs_ref, x_ref), (da_v, da_ref)]))


def backward_conv(
    base, da_hbm, seg_hbm, w_ref, add_hbm, out_ref,
    da_v, seg_ref, add_v, planes, w_vmem, acc_ref, out_v, sems,
):
    copies = Copies(sems)
    first = copies.load([(da_hbm, da_v), (seg_hbm, seg_ref)])
    w_copies = start_weights(copies, w_ref, w_vmem, None, range(w_vmem.shape[0] - 1, -1, -1))
    late = copies.start(add_hbm, add_v)
    wait_all(first)
    for c in range(planes.shape[0]):
        planes[c] = da_v[:, cols(c)].astype(f32)
    convolve(acc_ref.shape[0], base, planes, seg_ref, w_vmem, w_copies, True, plain_dot, acc_ref)
    late.wait()
    out_v[...] = (acc_ref[...] + add_v[...]).astype(out_v.dtype)
    copies.start(out_v, out_ref).wait()


def weight_grads(
    frames, taps, unit,
    x_ref, segs_ref, h_ref, out_ref,
    acc_ref, x_v, seg_v, h_v, folded, stacked, seg_f, seg_stacked, out_v, sems,
):
    copies = Copies(sems)
    peers, held = x_ref.shape[:2]
    slots = out_ref.shape[0]
    per = slots * unit
    fold = lane // per
    step = frames // fold
    near = frames + 2 * half_taps
    chunk = [
        copies.load([(x_ref.at[r], x_v.at[r]), (segs_ref.at[r], seg_v.at[r]), (h_ref.at[r], h_v.at[r])])
        for r in range(peers)
    ]
    which = lane_group(per)
    pieces = -(-taps // fold)
    edges = [0] + [q * step + half_taps for q in range(1, fold)] + [near]
    for r in range(peers):
        b = r % 2
        wait_all(chunk[r][:2])
        v = x_v[r].astype(f32)
        for i in range(fold):
            folded[b, i, :held] = turn(v, i * per)
        for q in range(fold):
            lo, hi = edges[q], edges[q + 1]
            at = lo - q * step
            stacked[b, lo:hi] = pick_lanes(
                which,
                [folded[b, (j - q) % fold, at + j : at + j + hi - lo] for j in range(fold)],
            )
        seg_f[b, :near] = seg_v[r].astype(f32)
        seg_stacked[b] = pick_lanes(which, [seg_f[b, j : j + near] for j in range(fold)])
        chunk[r][2].wait()
        for p in range(0, pieces, 3):
            q = min(pieces, p + 3)
            parts = [
                jnp.where(
                    seg_stacked[b, fold * n : fold * n + frames] == seg_f[b, half_taps : half_taps + frames],
                    stacked[b, fold * n : fold * n + frames],
                    0.0,
                ).astype(bf16)
                for n in range(p, q)
            ]
            d = dot(jnp.concatenate(parts, axis=1), h_v[r], column_dot)
            if r == 0:
                acc_ref[p * lane : q * lane] = d
            else:
                acc_ref[p * lane : q * lane] += d
    for k in range(taps):
        at = (taps - 1 - k) * per
        for n in range(slots):
            out_v[n, k] = acc_ref[at + n * unit : at + (n + 1) * unit].astype(bf16)
    copies.start(out_v, out_ref).wait()


def call(body, name, out_shape, in_specs, scratch, flops, byte_count, args, out_specs=None, budget=60):
    out_specs = out_specs or jax.tree.map(lambda _: in_vmem(), out_shape)
    return pl.pallas_call(
        body,
        out_shape=out_shape,
        in_specs=in_specs,
        out_specs=out_specs,
        scratch_shapes=scratch,
        compiler_params=pltpu.CompilerParams(vmem_limit_bytes=budget << 20),
        cost_estimate=pl.CostEstimate(flops=flops, bytes_accessed=byte_count, transcendentals=0),
        name=name,
    )(*args)


def after(value, *others):
    return lax.optimization_barrier((value, *others))[0]


def per_device(
    block_entry_input,
    prelude_output,
    leading_block_output,
    lengths,
    leading_conv_weight,
    remaining_conv_weight,
    gain,
    shift,
    residual_pointwise_weight,
    residual_norm_scale,
    residual_norm_bias,
    cotangent,
):
    tm, rows_axis = lax.axis_size("tm"), lax.axis_size("batch")
    everyone = ("tm", "batch")
    devices = tm * rows_axis
    place = lax.axis_index("tm")
    frames, entry_width = block_entry_input.shape[1:]
    channels, taps = leading_conv_weight.shape[:2]
    blocks = channels // lane
    layers = remaining_conv_weight.shape[0] + 1
    samples = float(frames * tm * rows_axis)
    end = frames * tm
    reach = half_taps * 2 * layers
    ext = [reach - half_taps * i for i in range(layers + 1)]
    ext_u = ext[layers]
    side = -(-ext_u // 16) * 16
    unit = channels // tm
    group_count = devices // group
    groups = [[j * group + i for i in range(group)] for j in range(group_count)]
    across = [[j * group + i for j in range(group_count)] for i in range(group)]
    row_place = lax.axis_index("batch")
    me = place * rows_axis + row_place
    share_rows = channels // devices
    near = frames + 2 * half_taps

    def sds(shape, dtype):
        return jax.ShapeDtypeStruct(shape, dtype)

    def swap(v, axis, bit):
        n = lax.axis_size(axis)
        return lax.ppermute(v, axis, [(i, i ^ bit) for i in range(n)])

    def spread(v):
        return lax.all_to_all(v, everyone, 0, 0, tiled=True)

    x_own, p_own, l_own = block_entry_input[0], prelude_output[0], leading_block_output[0]
    cot_own = cotangent[0]
    side_width = p_own.shape[1] + l_own.shape[1] + channels
    place_1 = place.astype(jnp.int32).reshape(1)
    members = (me // group * group + jnp.arange(group)).astype(jnp.int32)
    group_places = jnp.stack([members // rows_axis, members % rows_axis])
    row_places = jnp.stack([jnp.arange(tm, dtype=jnp.int32), jnp.zeros((tm,), jnp.int32)])
    if rows_axis == 2:
        other_lengths = swap(lengths, "batch", 1)
        mine = jnp.where(row_place == 0, lengths, other_lengths)
        all_lengths = jnp.concatenate([mine, lengths + other_lengths - mine], axis=0)
    else:
        all_lengths = lax.all_gather(lengths[0], "batch")

    any_ = in_place
    vmem, smem = in_vmem, in_smem

    def sems(count):
        return pltpu.SemaphoreType.DMA((count,))

    seg, x_tail, x_head = call(
        functools.partial(prepare, frames, end, reach), "prepare",
        (
            sds((frames + 2 * reach, lane), f32),
            sds((reach, entry_width), bf16), sds((reach, entry_width), bf16),
        ),
        [smem()] * 2 + [any_()], [sems(2)], 1000, 1 << 20, (place_1, lengths, x_own),
    )
    upward = [(i, i + 1) for i in range(tm - 1)]
    downward = [(i + 1, i) for i in range(tm - 1)]
    x_low, x_high = lax.ppermute(x_tail, "tm", upward), lax.ppermute(x_head, "tm", downward)

    w_first = jnp.transpose(leading_conv_weight, (1, 0, 2))
    w_rest = jnp.transpose(remaining_conv_weight, (0, 2, 1, 3))

    def weights(layer):
        return (w_first, entry_width) if layer == 1 else (w_rest, channels)

    tile_sums = sds((devices, 2 * blocks, lane), f32)
    res_rows = -(-3 * blocks // 8) * 8
    sums_v = pltpu.VMEM(tile_sums.shape, f32)
    affine_v = [pltpu.VMEM(gain.shape, f32), pltpu.VMEM(shift.shape, f32)]
    seg_rows = pltpu.VMEM((frames + 2 * reach, lane), f32)

    def conv_cost(rows, width):
        return 2 * rows * width * channels * taps, 2 * taps * width * channels + 8 * rows * channels

    def planes(rows, width):
        return pltpu.VMEM((width // lane, rows, lane), f32)

    def wide_rows(rows, width, dtype=f32):
        return pltpu.VMEM((rows, width), dtype)

    row_count = [frames + 2 * e for e in ext]
    a, snd = call(
        functools.partial(forward_first, frames, ext[1], reach - ext[0]), "forward_first",
        (sds((row_count[1], channels), f32), tile_sums),
        [any_()] * 5,
        [
            wide_rows(row_count[0], entry_width, bf16), planes(row_count[0], entry_width), seg_rows,
            pltpu.VMEM((taps, channels, entry_width), bf16), wide_rows(row_count[1], channels), sums_v,
            sems(taps + 6),
        ],
        *conv_cost(row_count[1], entry_width), (x_own, x_low, x_high, seg, w_first),
        (any_(), any_()),
    )
    stats, acts = [None, spread(snd)], [None, a]
    gathered = []

    def gather(h, peers):
        if peers == tm:
            gathered.append(lax.all_gather(h, "tm", axis=0))
        else:
            gathered.append(lax.all_gather(h, everyone, axis=0, axis_index_groups=groups))

    gather(x_own, tm)
    q_sums = call(
        branch_sums, "branch_sums", sds((3, 2 * blocks, lane), f32),
        [vmem()] * 4, [], 2 * frames * residual_pointwise_weight.size, 4 << 20,
        (p_own, l_own, x_own, residual_pointwise_weight),
    )
    def segments(chunk_places, counts):
        chunks = chunk_places.shape[1]
        return call(
            functools.partial(chunk_segments, frames, end, chunks), "chunk_segments",
            sds((chunks, near, lane), bf16), [smem()] * 2, [], 1000, 4 << 20, (chunk_places, counts),
        )

    segs = segments(group_places, all_lengths)
    row_segs = segments(row_places, lengths)
    s_tail, s_head = call(
        functools.partial(pack_sides, frames), "pack_sides",
        (sds((side, side_width), bf16), sds((side, side_width), bf16)),
        [any_()] * 3, [sems(6)], 1000, 1 << 20, (p_own, l_own, cot_own),
    )
    s_low, s_high = lax.ppermute(s_tail, "tm", upward), lax.ppermute(s_head, "tm", downward)
    for layer in range(2, layers + 1):
        held = []
        if layer == 2:
            held = [s_tail, q_sums]
        if layer == 3:
            held = [s_low, s_high]
        if layer == 5:
            held = [segs, gathered[0]]
        if held:
            stats[layer - 1] = after(stats[layer - 1], *held)
        rows, before = row_count[layer], row_count[layer - 1]
        st = stats[layer - 1]
        with_extra = layer <= 4
        tile = sds((devices, 4 * blocks, lane), f32) if with_extra else tile_sums
        a, h, snd = call(
            functools.partial(
                forward_next, frames, ext[layer], reach - ext[layer - 1], samples, layer, with_extra
            ),
            "forward_next",
            (sds((rows, channels), f32), sds((frames, channels), bf16), tile),
            [any_()] * (6 + with_extra),
            [
                *affine_v, wide_rows(before, channels), pltpu.VMEM(st.shape, f32), wide_rows(frames, channels, bf16),
                planes(before, channels), seg_rows, pltpu.VMEM((taps, channels, channels), bf16),
                wide_rows(rows, channels), pltpu.VMEM(tile.shape, f32), sems(taps + blocks + 8),
                *([pltpu.VMEM((2 * blocks, lane), f32)] if with_extra else []),
            ],
            *conv_cost(rows, channels),
            (acts[-1], st, gain, shift, seg, w_rest, *([q_sums] if with_extra else [])),
            (any_(), any_(), any_()),
        )
        stats.append(spread(snd))
        acts.append(a)
        gather(after(h, stats[layer]), group)

    rows = row_count[layers]
    block_output, du, snd, res_snd, q_tot = call(
        functools.partial(join, frames, ext_u, samples, layers), "join",
        (
            sds((frames, channels), bf16), sds((rows, channels), f32), tile_sums,
            sds((devices, res_rows, lane), f32), sds((3, 2 * blocks, lane), f32),
        ),
        [any_()] * 2 + [vmem()] * 6 + [any_()] * 3 + [vmem()] * 7,
        [
            wide_rows(rows, channels), sums_v, pltpu.VMEM((3, devices, 4 * blocks, lane), f32),
            pltpu.VMEM((3, rows, channels), f32), wide_rows(rows, channels),
            wide_rows(frames, channels, bf16), sums_v, pltpu.VMEM((devices, res_rows, lane), f32),
            sems(blocks + 8),
        ],
        2 * rows * residual_pointwise_weight.size, 8 << 20,
        (
            acts[layers], after(stats[layers], gathered[1], gathered[2]), gain, shift, p_own, l_own, x_own,
            residual_pointwise_weight,
            *stats[2:5], residual_norm_scale, residual_norm_bias, cot_own, x_low, x_high, s_low, s_high,
        ),
        (any_(), any_(), any_(), any_(), vmem()),
    )
    back = [None] * (layers + 1)
    back[layers] = spread(snd)
    res_back = spread(res_snd)

    prelude_gradient, grad_first, res_entry, res_weight, res_tot = call(
        functools.partial(branch_grads, frames, ext_u, samples), "branch_grads",
        (
            sds(p_own.shape, bf16), sds(l_own.shape, bf16), sds(x_own.shape, f32),
            sds(residual_pointwise_weight.shape, bf16), sds((res_rows, lane), f32),
        ),
        [vmem()] * 9, [], 6 * frames * residual_pointwise_weight.size, 8 << 20,
        (
            du, back[layers], res_back, p_own, l_own, x_own, residual_pointwise_weight, q_tot,
            residual_norm_scale,
        ),
    )
    grads, totals = [None] * (layers + 1), [None] * (layers + 1)
    xs, turned, made, sent, sums = {}, {}, {}, {}, {}

    def exchange(x):
        if x.shape[0] == tm:
            return lax.all_to_all(x, "tm", 0, 0, tiled=True)
        return lax.all_to_all(x, everyone, 0, 0, tiled=True, axis_index_groups=groups)

    def x_shape(layer):
        peers = tm if layer == 1 else group
        return peers, frames * channels // peers // lane + 2 * half_taps, lane

    def make_grad(layer, x):
        width = gathered[layer - 1].shape[2]
        peers, held = x.shape[:2]
        per = channels // peers
        fold = lane // per
        rows = 16 if peers == group else unit
        out = (per // rows, taps, rows, width)
        return call(
            functools.partial(weight_grads, frames, taps, rows), "weight_grads", sds(out, bf16),
            [any_()] * 3,
            [
                wide_rows(-(-taps // fold) * lane, width), pltpu.VMEM(x.shape, bf16),
                pltpu.VMEM((peers, near, lane), bf16), pltpu.VMEM((peers, frames, width), bf16),
                pltpu.VMEM((2, fold, held + 8, lane), f32), pltpu.VMEM((2, near, lane), f32),
                pltpu.VMEM((2, near + 8, lane), f32), pltpu.VMEM((2, near, lane), f32),
                pltpu.VMEM(out, bf16), sems(3 * peers + 1),
            ],
            2 * taps * per * frames * peers * width, 2 * peers * frames * width,
            (x, segs if peers == group else row_segs, gathered[layer - 1]), any_(),
        )

    def reduce_groups(part):
        parts, rows = part.shape[0], part.shape[2]
        split = rows // share_rows
        if split > 1:
            part = part.reshape(parts, taps, split, share_rows, -1).transpose(0, 2, 1, 3, 4)
            part = part.reshape(parts * split, taps, share_rows, -1)
        return lax.psum_scatter(part, everyone, scatter_dimension=0, axis_index_groups=across)

    def join_rows(part):
        if rows_axis == 2:
            other = swap(part, "batch", 1)
            first = jnp.where(row_place == 0, part, other)
            last = jnp.where(row_place == 0, other, part)
            return jnp.concatenate([first, last], axis=1).astype(f32)
        return lax.all_gather(part, "batch", axis=1, tiled=True).astype(f32)

    def add_rows(part):
        if rows_axis == 2:
            return part.astype(f32) + swap(part, "batch", 1).astype(f32)
        return lax.psum(part, "batch").astype(f32)

    dz = du
    for layer in range(layers, 1, -1):
        ext_da = half_taps * layer
        rows = frames + 2 * ext_da
        out_rows = rows - 2 * half_taps
        held = []
        if layer + 2 <= layers:
            made[layer + 2] = make_grad(layer + 2, after(turned[layer + 2], sent[layer]))
            held.append(made[layer + 2])
            sums[layer + 2] = reduce_groups(after(made[layer + 2], back[layer]))
        if layer == layers - 1:
            held += [prelude_gradient]
        if layer == layers - 2:
            held += [gathered[4], row_segs]
        bst = after(back[layer], *held) if held else back[layer]
        if layer + 1 <= layers:
            turned[layer + 1] = exchange(after(xs[layer + 1], bst))
        dz, xs[layer], totals[layer], snd = call(
            functools.partial(
                backward_step, frames, ext_da, ext[layer] - ext_da,
                ext[layer - 1] - (ext_da - half_taps), reach - ext_da, samples, layer, share_rows,
            ),
            "backward_step",
            (sds((out_rows, channels), f32), sds(x_shape(layer), bf16), sds((2 * blocks, lane), f32), tile_sums),
            [any_()] * 10,
            [
                *affine_v, wide_rows(rows, channels), sums_v, wide_rows(rows, channels),
                pltpu.VMEM(stats[layer].shape, f32), seg_rows,
                wide_rows(out_rows, channels), pltpu.VMEM(stats[layer - 1].shape, f32), planes(rows, channels),
                wide_rows(near, channels, bf16), pltpu.VMEM(x_shape(layer), bf16),
                pltpu.VMEM((taps, channels, channels), bf16), wide_rows(out_rows, channels),
                wide_rows(out_rows, channels), sums_v,
                sems(taps + 3 * blocks + 9),
            ],
            *conv_cost(out_rows, channels),
            (
                dz, bst, acts[layer], stats[layer], gain, shift, seg, w_rest, acts[layer - 1],
                stats[layer - 1],
            ),
            (any_(), any_(), vmem(), any_()),
        )
        if layer + 1 <= layers:
            snd = after(snd, turned[layer + 1])
        back[layer - 1] = spread(snd)
        sent[layer - 1] = snd

    ext_da = half_taps
    rows = frames + 2 * ext_da
    made[3] = make_grad(3, after(turned[3], sent[1]))
    sums[3] = reduce_groups(after(made[3], back[1]))
    bst = after(back[1], made[3])
    turned[2] = exchange(after(xs[2], bst))
    da, x, totals[1] = call(
        functools.partial(backward_norm, frames, ext_da, ext[1] - ext_da, samples, 1, unit),
        "backward_norm",
        (sds((rows, channels), bf16), sds(x_shape(1), bf16), sds((2 * blocks, lane), f32)),
        [any_()] * 5,
        [
            affine_v[0], wide_rows(rows, channels), sums_v, wide_rows(rows, channels), sums_v,
            wide_rows(rows, channels, bf16), wide_rows(near, channels, bf16),
            pltpu.VMEM(x_shape(1), bf16), sems(2 * blocks + 5),
        ],
        1000, 4 << 20, (dz, bst, acts[1], stats[1], gain), (any_(), any_(), vmem()),
    )
    turned[1] = exchange(after(x, turned[2]))
    made[2] = make_grad(2, after(turned[2], x))
    sums[2] = reduce_groups(made[2])
    dz = call(
        functools.partial(backward_conv, reach - ext_da), "backward_conv",
        sds((frames, entry_width), bf16),
        [any_()] * 4,
        [
            wide_rows(rows, channels, bf16), seg_rows, wide_rows(frames, entry_width), planes(rows, channels),
            pltpu.VMEM((taps, channels, entry_width), bf16), wide_rows(frames, entry_width),
            wide_rows(frames, entry_width, bf16), sems(taps + 4),
        ],
        *conv_cost(frames, entry_width), (after(da, made[2]), seg, w_first, res_entry), any_(),
    )
    for layer in range(layers, 2, -1):
        grads[layer] = join_rows(after(sums[layer], turned[1]))
    made[1] = make_grad(1, after(turned[1], dz, made[2]))
    grads[1] = add_rows(made[1][0])
    grads[2] = join_rows(sums[2])

    part = after(res_weight, x).reshape(tm, unit, -1)
    waits = [made[2], dz, made[1]]
    bit = 1
    while bit < tm:
        pairs = part.reshape(part.shape[0] // 2, 2, unit, -1)
        mine = place // bit % 2
        there = swap(lax.dynamic_index_in_dim(pairs, 1 - mine, 1, keepdims=False), "tm", bit)
        if waits:
            there = after(there, waits.pop(0))
        part = lax.dynamic_index_in_dim(pairs, mine, 1, keepdims=False).astype(f32) + there.astype(f32)
        part = part.astype(bf16)
        bit *= 2
    grad_res_weight = add_rows(part[0])

    grad_block_input = dz[None]

    def share(v):
        return lax.dynamic_slice_in_dim(v, place * unit, unit, axis=v.ndim - 1)

    norm_sums = share(jnp.stack(totals[1:]).reshape(layers, 2, channels))
    grad_shift, grad_gain = norm_sums[: layers - 1, 0], norm_sums[:, 1]
    grad_last_shift = norm_sums[layers - 1, 0]
    grad_res_gain = share(res_tot[: 3 * blocks].reshape(3, channels))
    grad_res_shift = jnp.broadcast_to(grad_last_shift[None], (3, unit))
    grad_w_first = jnp.transpose(grads[1], (1, 0, 2))
    grad_w_rest = jnp.transpose(jnp.stack(grads[2:]), (0, 2, 1, 3))
    return (
        block_output[None],
        grad_block_input,
        prelude_gradient[None],
        grad_first[None],
        grad_w_first,
        grad_w_rest,
        grad_gain,
        grad_shift,
        grad_last_shift,
        grad_res_weight,
        grad_res_gain,
        grad_res_shift,
    )


def solution(mesh):
    split = P("batch", "tm", None)
    in_specs = (
        split, split, split, P("batch", None), P(), P(), P(), P(), P(), P(), P(), split,
    )
    out_specs = (
        split, split, split, split,
        P("tm", None, None), P(None, "tm", None, None), P(None, "tm"), P(None, "tm"), P("tm"),
        P("tm", None), P(None, "tm"), P(None, "tm"),
    )
    return jax.shard_map(
        per_device, mesh=mesh, in_specs=in_specs, out_specs=out_specs, check_vma=False
    )
```

```python
import functools

import jax
import jax.numpy as jnp
from jax import lax
from jax.experimental import pallas as pl
from jax.experimental.pallas import tpu as pltpu
from jax.sharding import PartitionSpec as P

norm_eps = 0.001
lane = 128
half_taps = 8
group = 8
bf16 = jnp.bfloat16
f32 = jnp.float32

row_dot = (((1,), (1,)), ((), ()))
plain_dot = (((1,), (0,)), ((), ()))
column_dot = (((0,), (0,)), ((), ()))


def in_vmem():
    return pl.BlockSpec(memory_space=pltpu.VMEM)


def in_place():
    return pl.BlockSpec(memory_space=pl.ANY)


def in_smem():
    return pl.BlockSpec(memory_space=pltpu.SMEM)


def dot(a, b, dims):
    return lax.dot_general(a, b, dims, preferred_element_type=f32)


def cols(c):
    return slice(c * lane, (c + 1) * lane)


def sigmoid(v):
    return 1.0 / (1.0 + jnp.exp(-v))


def sum_rows(v):
    return jnp.sum(v, axis=0, keepdims=True)


def moments(total, row, count, samples):
    out = []
    for c in range(count):
        mean = total[row + c : row + c + 1] * (1.0 / samples)
        spread = total[row + count + c : row + count + c + 1] * (1.0 / samples) - mean * mean
        out.append((mean, lax.rsqrt(spread + norm_eps)))
    return out


class Copies:
    def __init__(self, sems):
        self.sems, self.count = sems, 0

    def start(self, src, dst):
        copy = pltpu.make_async_copy(src, dst, self.sems.at[self.count])
        self.count += 1
        copy.start()
        return copy

    def load(self, pairs):
        return [self.start(src, dst) for src, dst in pairs]


def wait_all(copies):
    for copy in copies:
        copy.wait()


def start_weights(copies, w_ref, w_vmem, layer, order):
    made = {}
    for k in order:
        made[k] = copies.start(w_ref.at[k] if layer is None else w_ref.at[layer, k], w_vmem.at[k])
    return made


def convolve(rows, base, planes, seg_ref, w_vmem, w_copies, flip, dims, acc_ref):
    taps = w_vmem.shape[0]
    blocks = planes.shape[0]
    for k in range(taps):
        tap = taps - 1 - k if flip else k
        w_copies[tap].wait()
        mask = (
            seg_ref[base + k : base + k + rows]
            == seg_ref[base + half_taps : base + half_taps + rows]
        )
        x = jnp.concatenate(
            [jnp.where(mask, planes[c, k : k + rows], 0.0).astype(bf16) for c in range(blocks)],
            axis=1,
        )
        d = dot(x, w_vmem[tap], dims)
        if k == 0:
            acc_ref[...] = d
        else:
            acc_ref[...] += d


def send_sums(copies, pieces, wide_ref, snd_ref):
    tile = jnp.concatenate(pieces, axis=0)
    short = wide_ref.shape[1] - tile.shape[0]
    if short:
        tile = jnp.concatenate([tile, jnp.zeros((short, lane), f32)], axis=0)
    for d in range(wide_ref.shape[0]):
        wide_ref[d] = tile
    return copies.start(wide_ref, snd_ref)


def conv_sums(a_ref, own):
    first, second = [], []
    for c in range(a_ref.shape[1] // lane):
        v = a_ref[own, cols(c)]
        first.append(sum_rows(v))
        second.append(sum_rows(v * v))
    return first + second


def segment_of(position, counts_ref, end, row=0):
    number = counts_ref.shape[1]
    at = lax.broadcasted_iota(jnp.int32, (1, lane), 1)
    starts, start = jnp.full((1, lane), end + lane * lane, jnp.int32), jnp.int32(0)
    for j in range(number):
        starts = jnp.where(at == j, start, starts)
        start = start + counts_ref[row, j]
    begun = jnp.where(position >= starts, 1.0, 0.0).astype(bf16)
    inside = dot(begun, jnp.ones((lane, lane), bf16), plain_dot)
    return jnp.where(position < end, inside, -1.0)


def prepare(
    frames, end, reach,
    place_ref, counts_ref, x_ref,
    seg_ref, x_tail, x_head,
    sems,
):
    copies = Copies(sems)
    edge = x_tail.shape[0]
    first = copies.load([(x_ref.at[frames - edge :], x_tail), (x_ref.at[:edge], x_head)])
    rows = lax.broadcasted_iota(jnp.int32, seg_ref.shape, 0)
    seg_ref[...] = segment_of(place_ref[0] * frames - reach + rows, counts_ref, end)
    wait_all(first)


def pack_sides(frames, p_ref, l_ref, cot_ref, s_tail, s_head, sems):
    copies = Copies(sems)
    side = s_tail.shape[0]
    at, made = 0, []
    for ref in (p_ref, l_ref, cot_ref):
        width = ref.shape[1]
        made.append(copies.start(ref.at[frames - side :], s_tail.at[:, at : at + width]))
        made.append(copies.start(ref.at[:side], s_head.at[:, at : at + width]))
        at += width
    wait_all(made)


def chunk_segments(frames, end, chunks, place_ref, counts_ref, out_ref):
    ahead = lax.broadcasted_iota(jnp.int32, out_ref.shape[1:], 0) - half_taps
    for r in range(chunks):
        row = place_ref[1, r]
        out_ref[r] = segment_of(place_ref[0, r] * frames + ahead, counts_ref, end, row).astype(bf16)


def forward_first(
    frames, ext, base,
    x_ref, low_ref, high_ref, seg_hbm, w_ref,
    a_ref, snd_ref,
    x_v, planes, seg_ref, w_vmem, acc_ref, wide_ref, sems,
):
    copies = Copies(sems)
    taps = w_vmem.shape[0]
    edge = low_ref.shape[0]
    first = copies.load([
        (x_ref, x_v.at[edge : edge + frames]), (low_ref, x_v.at[:edge]), (high_ref, x_v.at[edge + frames :]),
        (seg_hbm, seg_ref),
    ])
    w_copies = start_weights(copies, w_ref, w_vmem, None, range(taps))
    wait_all(first)
    for c in range(planes.shape[0]):
        planes[c] = x_v[:, cols(c)].astype(f32)
    convolve(acc_ref.shape[0], base, planes, seg_ref, w_vmem, w_copies, False, row_dot, acc_ref)
    out = copies.start(acc_ref, a_ref)
    sent = send_sums(copies, conv_sums(acc_ref, slice(ext, ext + frames)), wide_ref, snd_ref)
    wait_all([out, sent])


def forward_next(
    frames, ext, base, samples, layer, with_extra,
    prev_hbm, st_hbm, gain_hbm, shift_hbm, seg_hbm, w_ref, *rest,
):
    extra_hbm, rest = (rest[0], rest[1:]) if with_extra else (None, rest)
    a_ref, h_ref, snd_ref, gain_ref, shift_ref, prev_ref, st_ref, low_ref, planes = rest[:9]
    seg_ref, w_vmem, acc_ref, wide_ref, sems = rest[9:14]
    copies = Copies(sems)
    blocks = planes.shape[0]
    small = copies.load([(st_hbm, st_ref), (gain_hbm, gain_ref), (shift_hbm, shift_ref)])
    prev_copies = [copies.start(prev_hbm.at[:, cols(c)], prev_ref.at[:, cols(c)]) for c in range(blocks)]
    seg_copy = copies.start(seg_hbm, seg_ref)
    w_copies = start_weights(copies, w_ref, w_vmem, layer - 2, range(w_vmem.shape[0]))
    extra = None
    if with_extra:
        extra = copies.start(extra_hbm.at[layer - 2], rest[14])
    wait_all(small)
    total = jnp.sum(st_ref[...], axis=0)
    inner = slice(ext + half_taps, ext + half_taps + frames)
    prev = slice(layer - 2, layer - 1)
    for c, (mean, rstd) in enumerate(moments(total, 0, blocks, samples)):
        prev_copies[c].wait()
        z = (prev_ref[:, cols(c)] - mean) * (rstd * gain_ref[prev, cols(c)])
        z = z + shift_ref[prev, cols(c)]
        low = (z * sigmoid(z)).astype(bf16)
        planes[c] = low.astype(f32)
        low_ref[:, cols(c)] = low[inner]
    h_copy = copies.start(low_ref, h_ref)
    seg_copy.wait()
    convolve(acc_ref.shape[0], base, planes, seg_ref, w_vmem, w_copies, False, row_dot, acc_ref)
    out = copies.start(acc_ref, a_ref)
    pieces = conv_sums(acc_ref, slice(ext, ext + frames))
    if with_extra:
        extra.wait()
        pieces.append(rest[14][...])
    sent = send_sums(copies, pieces, wide_ref, snd_ref)
    wait_all([h_copy, out, sent])


def branch_weights(rw_ref, sources):
    at, out = 0, []
    for p in sources:
        out.append(rw_ref[:, at : at + p.shape[1]])
        at += p.shape[1]
    return out


def branch_sums(p_ref, l_ref, x_ref, rw_ref, out_ref):
    blocks = rw_ref.shape[0] // lane
    sources = (p_ref, l_ref, x_ref)
    for branch, (p, w) in enumerate(zip(sources, branch_weights(rw_ref, sources), strict=True)):
        q = dot(p[...], w, row_dot)
        for c in range(blocks):
            out_ref[branch, c : c + 1] = sum_rows(q[:, cols(c)])
            out_ref[branch, blocks + c : blocks + c + 1] = sum_rows(q[:, cols(c)] * q[:, cols(c)])


def join(
    frames, ext, samples, layer,
    a_hbm, st_hbm, p_hbm, l_hbm, x_hbm, rw_hbm, q0_hbm, q1_hbm, q2_hbm, cot_hbm, xl_hbm, xh_hbm, sl_hbm, sh_hbm,
    gain_ref, shift_ref, rg_ref, rb_ref,
    out_ref, du_ref, snd_ref, snd_res_ref, q_tot_ref,
    a_ref, st_ref, p_ref, l_ref, x_ref, rw_ref, qst_refs, cot_ref, x_low, x_high, s_low, s_high,
    q_ref, du_v, out_v, wide_ref, wide_res_ref, sems,
):
    copies = Copies(sems)
    blocks = a_ref.shape[1] // lane
    early = copies.load([
        (rw_hbm, rw_ref), (p_hbm, p_ref), (l_hbm, l_ref), (x_hbm, x_ref), (xl_hbm, x_low), (xh_hbm, x_high),
        (sl_hbm, s_low), (sh_hbm, s_high),
    ])
    first = copies.load(
        [(q, qst_refs.at[i]) for i, q in enumerate((q0_hbm, q1_hbm, q2_hbm))] + [(st_hbm, st_ref)]
    )
    columns = [
        copies.load([
            (a_hbm.at[:, cols(c)], a_ref.at[:, cols(c)]), (cot_hbm.at[:, cols(c)], cot_ref.at[:, cols(c)]),
        ])
        for c in range(blocks)
    ]
    wait_all(early)
    sources = (p_ref, l_ref, x_ref)
    edge, side = x_low.shape[0], s_low.shape[0]
    own = slice(ext, ext + frames)
    at = 0
    for branch, w in enumerate(branch_weights(rw_ref, sources)):
        width = sources[branch].shape[1]
        if branch < 2:
            low, high = s_low[:, at : at + width], s_high[:, at : at + width]
            at += width
        else:
            low, high = x_low[edge - side :], x_high[:side]
        q_ref[branch, :ext] = dot(low, w, row_dot)[side - ext :]
        q_ref[branch, own] = dot(sources[branch][...], w, row_dot)
        q_ref[branch, ext + frames :] = dot(high, w, row_dot)[:ext]
    wait_all(first)
    total = jnp.sum(st_ref[...], axis=0)
    main = moments(total, 0, blocks, samples)
    res = []
    for branch in range(3):
        q_tot_ref[branch] = jnp.sum(qst_refs[branch], axis=0)[2 * blocks :]
        res.append(moments(q_tot_ref[branch], 0, blocks, samples))
    shift_sums, gain_sums, res_sums, done = [], [], [[], [], []], []
    mine = slice(layer - 1, layer)
    for c in range(blocks):
        wait_all(columns[c])
        normed = (a_ref[:, cols(c)] - main[c][0]) * main[c][1]
        u = normed * gain_ref[mine, cols(c)] + shift_ref[mine, cols(c)]
        normed_q = []
        for branch in range(3):
            mean, rstd = res[branch][c]
            qn = (q_ref[branch, :, cols(c)] - mean) * rstd
            normed_q.append(qn[own])
            u = u + qn * rg_ref[branch : branch + 1, cols(c)] + rb_ref[branch : branch + 1, cols(c)]
        s = sigmoid(u)
        out_v[:, cols(c)] = (u * s)[own].astype(bf16)
        slope = s * (1.0 + u * (1.0 - s))
        cot = slice(at + c * lane, at + (c + 1) * lane)
        du_v[:ext, cols(c)] = s_low[:, cot].astype(f32)[side - ext :] * slope[:ext]
        du_v[ext + frames :, cols(c)] = s_high[:, cot].astype(f32)[:ext] * slope[ext + frames :]
        du = cot_ref[:, cols(c)].astype(f32) * slope[own]
        du_v[own, cols(c)] = du
        done.append(copies.start(du_v.at[:, cols(c)], du_ref.at[:, cols(c)]))
        shift_sums.append(sum_rows(du))
        gain_sums.append(sum_rows(du * normed[own]))
        for branch in range(3):
            res_sums[branch].append(sum_rows(du * normed_q[branch]))
    done.append(copies.start(out_v, out_ref))
    done.append(send_sums(copies, shift_sums + gain_sums, wide_ref, snd_ref))
    done.append(send_sums(copies, res_sums[0] + res_sums[1] + res_sums[2], wide_res_ref, snd_res_ref))
    wait_all(done)


def branch_grads(
    frames, ext, samples,
    du_ref, bst_ref, rst_ref, p_ref, l_ref, x_ref, rw_ref, qst_ref, rg_ref,
    g0_ref, g1_ref, g2_ref, gw_ref, tot_ref,
):
    blocks = rw_ref.shape[0] // lane
    total = jnp.sum(bst_ref[...], axis=0) * (1.0 / samples)
    gains = jnp.sum(rst_ref[...], axis=0)
    tot_ref[...] = gains
    gains = gains * (1.0 / samples)
    own = slice(ext, ext + frames)
    sources = (p_ref, l_ref, x_ref)
    at_col = 0
    for branch, (g_ref, w) in enumerate(
        zip((g0_ref, g1_ref, g2_ref), branch_weights(rw_ref, sources), strict=True)
    ):
        p = sources[branch][...]
        q = dot(p, w, row_dot)
        low = []
        for c, (mean, rstd) in enumerate(moments(qst_ref[branch], 0, blocks, samples)):
            at = branch * blocks + c
            qn = (q[:, cols(c)] - mean) * rstd
            v = du_ref[own, cols(c)] - total[c : c + 1] - qn * gains[at : at + 1]
            low.append((v * (rg_ref[branch : branch + 1, cols(c)] * rstd)).astype(bf16))
        low = jnp.concatenate(low, axis=1)
        g_ref[...] = dot(low, w, plain_dot).astype(g_ref.dtype)
        width = p.shape[1]
        gw_ref[:, at_col : at_col + width] = dot(low, p, column_dot).astype(bf16)
        at_col += width


def channel_order(channels, peers, unit):
    per = channels // peers
    n = lax.broadcasted_iota(jnp.int32, (1, channels), 1)
    source = (n % per // unit * peers + n // per) * unit + n % unit
    row = lax.broadcasted_iota(jnp.int32, (channels, channels), 0)
    return jnp.where(row == source, 1.0, 0.0).astype(bf16)


def lane_group(per):
    return lax.broadcasted_iota(jnp.int32, (1, lane), 1) // per


def turn(v, lanes):
    return pltpu.roll(v, lanes % lane, 1) if lanes % lane else v


def pick_lanes(which, parts):
    out = parts[0]
    for j in range(1, len(parts)):
        out = jnp.where(which == j, parts[j], out)
    return out


class InputGrad:
    def __init__(self, copies, bst_hbm, st_hbm, dz_hbm, a_hbm, bst_v, st_v, dz_v, a_v, off_a):
        rows, channels = dz_v.shape
        self.blocks = channels // lane
        self.bst_v, self.st_v, self.dz_v, self.a_v = bst_v, st_v, dz_v, a_v
        self.first = copies.load([(bst_hbm, bst_v), (st_hbm, st_v)])
        self.columns = [
            copies.load([
                (dz_hbm.at[:, cols(c)], dz_v.at[:, cols(c)]),
                (a_hbm.at[off_a : off_a + rows, cols(c)], a_v.at[:, cols(c)]),
            ])
            for c in range(self.blocks)
        ]

    def make(self, samples, gain_row, tot_ref, at, low_ref, put):
        blocks = self.blocks
        wait_all(self.first)
        sums = jnp.sum(self.bst_v[...], axis=0)
        tot_ref[...] = sums
        sums = sums * (1.0 / samples)
        total = jnp.sum(self.st_v[...], axis=0)
        near = low_ref.shape[0]
        for c, (mean, rstd) in enumerate(moments(total, 0, blocks, samples)):
            wait_all(self.columns[c])
            normed = (self.a_v[:, cols(c)] - mean) * rstd
            v = self.dz_v[:, cols(c)] - sums[c : c + 1] - normed * sums[blocks + c : blocks + c + 1]
            low = (v * (gain_row[:, cols(c)] * rstd)).astype(bf16)
            put(c, low)
            low_ref[:, cols(c)] = low.astype(f32)[at : at + near].astype(bf16)


def pack_peers(frames, unit, low_ref, xs_ref):
    channels = low_ref.shape[1]
    peers, held = xs_ref.shape[:2]
    per = channels // peers
    fold = lane // per
    step = frames // fold
    which = lane_group(per)
    ordered = dot(low_ref[...], channel_order(channels, peers, unit), plain_dot)
    for c in range(channels // lane):
        v = ordered[:, cols(c)]
        turned = [turn(v, i * per) for i in range(fold)]
        for i in range(fold):
            parts = [turned[(j - i) % fold][j * step : j * step + held] for j in range(fold)]
            xs_ref[fold * c + i] = pick_lanes(which, parts).astype(bf16)


def backward_step(
    frames, ext_da, off_a, off_prev, base, samples, layer, unit,
    dz_hbm, bst_hbm, a_hbm, st_hbm, gain_hbm, shift_hbm, seg_hbm, w_ref, prev_hbm, prev_st_hbm,
    out_ref, x_ref, tot_ref, snd_ref,
    gain_ref, shift_ref, dz_v, bst_v, a_v, st_v, seg_ref, prev_v, prev_st_v, planes, low_ref, xs_ref, w_vmem, acc_ref, out_v, wide_ref,
    sems,
):
    copies = Copies(sems)
    affine = copies.load([(gain_hbm, gain_ref), (shift_hbm, shift_ref)])
    grad = InputGrad(copies, bst_hbm, st_hbm, dz_hbm, a_hbm, bst_v, st_v, dz_v, a_v, off_a)
    rows, channels = dz_v.shape
    blocks = channels // lane
    seg_copy = copies.start(seg_hbm, seg_ref)
    w_copies = start_weights(copies, w_ref, w_vmem, layer - 2, range(w_vmem.shape[0] - 1, -1, -1))
    out_rows = rows - 2 * half_taps
    late = copies.load([
        (prev_hbm.at[off_prev : off_prev + out_rows], prev_v), (prev_st_hbm, prev_st_v),
    ])

    def put(c, low):
        planes[c] = low.astype(f32)

    at = ext_da - half_taps
    wait_all(affine)
    grad.make(samples, gain_ref[layer - 1 : layer], tot_ref, at, low_ref, put)
    pack_peers(frames, unit, low_ref, xs_ref)
    x_copy = copies.start(xs_ref, x_ref)
    seg_copy.wait()
    convolve(out_rows, base, planes, seg_ref, w_vmem, w_copies, True, plain_dot, acc_ref)
    wait_all(late)
    prev_total = jnp.sum(prev_st_v[...], axis=0)
    own = slice(at, at + frames)
    shift_sums, gain_sums, done = [], [], [x_copy]
    before = slice(layer - 2, layer - 1)
    for c, (mean, rstd) in enumerate(moments(prev_total, 0, blocks, samples)):
        normed = (prev_v[:, cols(c)] - mean) * rstd
        z = normed * gain_ref[before, cols(c)] + shift_ref[before, cols(c)]
        s = sigmoid(z)
        dz = acc_ref[:, cols(c)] * (s * (1.0 + z * (1.0 - s)))
        out_v[:, cols(c)] = dz
        done.append(copies.start(out_v.at[:, cols(c)], out_ref.at[:, cols(c)]))
        dz = dz[own]
        shift_sums.append(sum_rows(dz))
        gain_sums.append(sum_rows(dz * normed[own]))
    done.append(send_sums(copies, shift_sums + gain_sums, wide_ref, snd_ref))
    wait_all(done)


def backward_norm(
    frames, ext_da, off_a, samples, layer, unit,
    dz_hbm, bst_hbm, a_hbm, st_hbm, gain_hbm,
    da_ref, x_ref, tot_ref,
    gain_ref, dz_v, bst_v, a_v, st_v, da_v, low_ref, xs_ref, sems,
):
    copies = Copies(sems)
    affine = copies.start(gain_hbm, gain_ref)
    grad = InputGrad(copies, bst_hbm, st_hbm, dz_hbm, a_hbm, bst_v, st_v, dz_v, a_v, off_a)
    affine.wait()

    def put(c, low):
        da_v[:, cols(c)] = low

    grad.make(samples, gain_ref[layer - 1 : layer], tot_ref, ext_da - half_taps, low_ref, put)
    pack_peers(frames, unit, low_ref, xs_ref)
    wait_all(copies.load([(xs_ref, x_ref), (da_v, da_ref)]))


def backward_conv(
    base, da_hbm, seg_hbm, w_ref, add_hbm, out_ref,
    da_v, seg_ref, add_v, planes, w_vmem, acc_ref, out_v, sems,
):
    copies = Copies(sems)
    first = copies.load([(da_hbm, da_v), (seg_hbm, seg_ref)])
    w_copies = start_weights(copies, w_ref, w_vmem, None, range(w_vmem.shape[0] - 1, -1, -1))
    late = copies.start(add_hbm, add_v)
    wait_all(first)
    for c in range(planes.shape[0]):
        planes[c] = da_v[:, cols(c)].astype(f32)
    convolve(acc_ref.shape[0], base, planes, seg_ref, w_vmem, w_copies, True, plain_dot, acc_ref)
    late.wait()
    out_v[...] = (acc_ref[...] + add_v[...]).astype(out_v.dtype)
    copies.start(out_v, out_ref).wait()


def weight_grads(
    frames, taps, unit,
    x_ref, segs_ref, h_ref, out_ref,
    acc_ref, x_v, seg_v, h_v, folded, stacked, seg_f, seg_stacked, out_v, sems,
):
    copies = Copies(sems)
    peers, held = x_ref.shape[:2]
    slots = out_ref.shape[0]
    per = slots * unit
    fold = lane // per
    step = frames // fold
    near = frames + 2 * half_taps
    chunk = [
        copies.load([(x_ref.at[r], x_v.at[r]), (segs_ref.at[r], seg_v.at[r]), (h_ref.at[r], h_v.at[r])])
        for r in range(peers)
    ]
    which = lane_group(per)
    pieces, done = -(-taps // fold), []
    edges = [0] + [q * step + half_taps for q in range(1, fold)] + [near]
    for r in range(peers):
        b = r % 2
        wait_all(chunk[r][:2])
        v = x_v[r].astype(f32)
        for i in range(fold):
            folded[b, i, :held] = turn(v, i * per)
        for q in range(fold):
            lo, hi = edges[q], edges[q + 1]
            at = lo - q * step
            stacked[b, lo:hi] = pick_lanes(
                which,
                [folded[b, (j - q) % fold, at + j : at + j + hi - lo] for j in range(fold)],
            )
        seg_f[b, :near] = seg_v[r].astype(f32)
        seg_stacked[b] = pick_lanes(which, [seg_f[b, j : j + near] for j in range(fold)])
        chunk[r][2].wait()
        for p in range(0, pieces, 3):
            q = min(pieces, p + 3)
            parts = [
                jnp.where(
                    seg_stacked[b, fold * n : fold * n + frames] == seg_f[b, half_taps : half_taps + frames],
                    stacked[b, fold * n : fold * n + frames],
                    0.0,
                ).astype(bf16)
                for n in range(p, q)
            ]
            d = dot(jnp.concatenate(parts, axis=1), h_v[r], column_dot)
            if r == 0:
                acc_ref[p * lane : q * lane] = d
            elif r < peers - 1:
                acc_ref[p * lane : q * lane] += d
            else:
                d = acc_ref[p * lane : q * lane] + d
                low, high = max(0, taps - q * fold), taps - p * fold
                for k in range(low, high):
                    at = (taps - 1 - k - p * fold) * per
                    for n in range(slots):
                        out_v[n, k] = d[at + n * unit : at + (n + 1) * unit].astype(bf16)
                done.append(copies.start(out_v.at[:, low:high], out_ref.at[:, low:high]))
    wait_all(done)


def call(body, name, out_shape, in_specs, scratch, flops, byte_count, args, out_specs=None, budget=60):
    out_specs = out_specs or jax.tree.map(lambda _: in_vmem(), out_shape)
    return pl.pallas_call(
        body,
        out_shape=out_shape,
        in_specs=in_specs,
        out_specs=out_specs,
        scratch_shapes=scratch,
        compiler_params=pltpu.CompilerParams(vmem_limit_bytes=budget << 20),
        cost_estimate=pl.CostEstimate(flops=flops, bytes_accessed=byte_count, transcendentals=0),
        name=name,
    )(*args)


def after(value, *others):
    return lax.optimization_barrier((value, *others))[0]


def per_device(
    block_entry_input,
    prelude_output,
    leading_block_output,
    lengths,
    leading_conv_weight,
    remaining_conv_weight,
    gain,
    shift,
    residual_pointwise_weight,
    residual_norm_scale,
    residual_norm_bias,
    cotangent,
):
    tm, rows_axis = lax.axis_size("tm"), lax.axis_size("batch")
    everyone = ("tm", "batch")
    devices = tm * rows_axis
    place = lax.axis_index("tm")
    frames, entry_width = block_entry_input.shape[1:]
    channels, taps = leading_conv_weight.shape[:2]
    blocks = channels // lane
    layers = remaining_conv_weight.shape[0] + 1
    samples = float(frames * tm * rows_axis)
    end = frames * tm
    reach = half_taps * 2 * layers
    ext = [reach - half_taps * i for i in range(layers + 1)]
    ext_u = ext[layers]
    side = -(-ext_u // 16) * 16
    unit = channels // tm
    group_count = devices // group
    groups = [[j * group + i for i in range(group)] for j in range(group_count)]
    across = [[j * group + i for j in range(group_count)] for i in range(group)]
    row_place = lax.axis_index("batch")
    me = place * rows_axis + row_place
    share_rows = channels // devices
    near = frames + 2 * half_taps

    def sds(shape, dtype):
        return jax.ShapeDtypeStruct(shape, dtype)

    def swap(v, axis, bit):
        n = lax.axis_size(axis)
        return lax.ppermute(v, axis, [(i, i ^ bit) for i in range(n)])

    def spread(v):
        return lax.all_to_all(v, everyone, 0, 0, tiled=True)

    x_own, p_own, l_own = block_entry_input[0], prelude_output[0], leading_block_output[0]
    cot_own = cotangent[0]
    side_width = p_own.shape[1] + l_own.shape[1] + channels
    place_1 = place.astype(jnp.int32).reshape(1)
    members = (me // group * group + jnp.arange(group)).astype(jnp.int32)
    group_places = jnp.stack([members // rows_axis, members % rows_axis])
    if rows_axis == 2:
        other_lengths = swap(lengths, "batch", 1)
        mine = jnp.where(row_place == 0, lengths, other_lengths)
        all_lengths = jnp.concatenate([mine, lengths + other_lengths - mine], axis=0)
    else:
        all_lengths = lax.all_gather(lengths[0], "batch")

    any_ = in_place
    vmem, smem = in_vmem, in_smem

    def sems(count):
        return pltpu.SemaphoreType.DMA((count,))

    seg, x_tail, x_head = call(
        functools.partial(prepare, frames, end, reach), "prepare",
        (
            sds((frames + 2 * reach, lane), f32),
            sds((reach, entry_width), bf16), sds((reach, entry_width), bf16),
        ),
        [smem()] * 2 + [any_()], [sems(2)], 1000, 1 << 20, (place_1, lengths, x_own),
    )
    upward = [(i, i + 1) for i in range(tm - 1)]
    downward = [(i + 1, i) for i in range(tm - 1)]
    x_low, x_high = lax.ppermute(x_tail, "tm", upward), lax.ppermute(x_head, "tm", downward)

    w_first = jnp.transpose(leading_conv_weight, (1, 0, 2))
    w_rest = jnp.transpose(remaining_conv_weight, (0, 2, 1, 3))

    def weights(layer):
        return (w_first, entry_width) if layer == 1 else (w_rest, channels)

    tile_sums = sds((devices, 2 * blocks, lane), f32)
    res_rows = -(-3 * blocks // 8) * 8
    sums_v = pltpu.VMEM(tile_sums.shape, f32)
    affine_v = [pltpu.VMEM(gain.shape, f32), pltpu.VMEM(shift.shape, f32)]
    seg_rows = pltpu.VMEM((frames + 2 * reach, lane), f32)

    def conv_cost(rows, width):
        return 2 * rows * width * channels * taps, 2 * taps * width * channels + 8 * rows * channels

    def planes(rows, width):
        return pltpu.VMEM((width // lane, rows, lane), f32)

    def wide_rows(rows, width, dtype=f32):
        return pltpu.VMEM((rows, width), dtype)

    def segments(chunk_places, counts):
        chunks = chunk_places.shape[1]
        return call(
            functools.partial(chunk_segments, frames, end, chunks), "chunk_segments",
            sds((chunks, near, lane), bf16), [smem()] * 2, [], 1000, 4 << 20, (chunk_places, counts),
        )

    segs = segments(group_places, after(all_lengths, x_tail))
    row_count = [frames + 2 * e for e in ext]
    a, snd = call(
        functools.partial(forward_first, frames, ext[1], reach - ext[0]), "forward_first",
        (sds((row_count[1], channels), f32), tile_sums),
        [any_()] * 5,
        [
            wide_rows(row_count[0], entry_width, bf16), planes(row_count[0], entry_width), seg_rows,
            pltpu.VMEM((taps, channels, entry_width), bf16), wide_rows(row_count[1], channels), sums_v,
            sems(taps + 6),
        ],
        *conv_cost(row_count[1], entry_width), (after(x_own, segs), x_low, x_high, seg, w_first),
        (any_(), any_()),
    )
    stats, acts = [None, spread(snd)], [None, a]
    gathered = []

    def gather(h):
        gathered.append(lax.all_gather(h, everyone, axis=0, axis_index_groups=groups))

    gather(x_own)
    q_sums = call(
        branch_sums, "branch_sums", sds((3, 2 * blocks, lane), f32),
        [vmem()] * 4, [], 2 * frames * residual_pointwise_weight.size, 4 << 20,
        (p_own, l_own, x_own, residual_pointwise_weight),
    )
    s_tail, s_head = call(
        functools.partial(pack_sides, frames), "pack_sides",
        (sds((side, side_width), bf16), sds((side, side_width), bf16)),
        [any_()] * 3, [sems(6)], 1000, 1 << 20, (p_own, l_own, cot_own),
    )
    s_low, s_high = lax.ppermute(s_tail, "tm", upward), lax.ppermute(s_head, "tm", downward)
    for layer in range(2, layers + 1):
        held = []
        if layer == 2:
            held = [s_tail, q_sums]
        if layer == 5:
            held = [s_low, s_high, gathered[0]]
        if held:
            stats[layer - 1] = after(stats[layer - 1], *held)
        rows, before = row_count[layer], row_count[layer - 1]
        st = stats[layer - 1]
        with_extra = layer <= 4
        tile = sds((devices, 4 * blocks, lane), f32) if with_extra else tile_sums
        a, h, snd = call(
            functools.partial(
                forward_next, frames, ext[layer], reach - ext[layer - 1], samples, layer, with_extra
            ),
            "forward_next",
            (sds((rows, channels), f32), sds((frames, channels), bf16), tile),
            [any_()] * (6 + with_extra),
            [
                *affine_v, wide_rows(before, channels), pltpu.VMEM(st.shape, f32), wide_rows(frames, channels, bf16),
                planes(before, channels), seg_rows, pltpu.VMEM((taps, channels, channels), bf16),
                wide_rows(rows, channels), pltpu.VMEM(tile.shape, f32), sems(taps + blocks + 8),
                *([pltpu.VMEM((2 * blocks, lane), f32)] if with_extra else []),
            ],
            *conv_cost(rows, channels),
            (acts[-1], st, gain, shift, seg, w_rest, *([q_sums] if with_extra else [])),
            (any_(), any_(), any_()),
        )
        stats.append(spread(snd))
        acts.append(a)
        gather(after(h, stats[layer]))

    rows = row_count[layers]
    rw = residual_pointwise_weight

    def like(v):
        return pltpu.VMEM(v.shape, v.dtype)

    block_output, du, snd, res_snd, q_tot = call(
        functools.partial(join, frames, ext_u, samples, layers), "join",
        (
            sds((frames, channels), bf16), sds((rows, channels), f32), tile_sums,
            sds((devices, res_rows, lane), f32), sds((3, 2 * blocks, lane), f32),
        ),
        [any_()] * 14 + [vmem()] * 4,
        [
            like(acts[layers]), like(stats[layers]), like(p_own), like(l_own), like(x_own), like(rw),
            pltpu.VMEM((3, *stats[2].shape), f32), like(cot_own), like(x_low), like(x_high), like(s_low),
            like(s_high),
            pltpu.VMEM((3, rows, channels), f32), wide_rows(rows, channels),
            wide_rows(frames, channels, bf16), sums_v, pltpu.VMEM((devices, res_rows, lane), f32),
            sems(3 * blocks + 15),
        ],
        2 * rows * rw.size, 8 << 20,
        (
            acts[layers], after(stats[layers], gathered[1]), p_own, l_own, x_own, rw, *stats[2:5],
            cot_own, x_low, x_high, s_low, s_high, gain, shift, residual_norm_scale, residual_norm_bias,
        ),
        (any_(), any_(), any_(), any_(), vmem()),
    )
    back = [None] * (layers + 1)
    back[layers] = spread(snd)
    res_back = spread(res_snd)

    prelude_gradient, grad_first, res_entry, res_weight, res_tot = call(
        functools.partial(branch_grads, frames, ext_u, samples), "branch_grads",
        (
            sds(p_own.shape, bf16), sds(l_own.shape, bf16), sds(x_own.shape, f32),
            sds(residual_pointwise_weight.shape, bf16), sds((res_rows, lane), f32),
        ),
        [vmem()] * 9, [], 6 * frames * residual_pointwise_weight.size, 8 << 20,
        (
            du, back[layers], res_back, p_own, l_own, x_own, residual_pointwise_weight, q_tot,
            residual_norm_scale,
        ),
    )
    grads, totals = [None] * (layers + 1), [None] * (layers + 1)
    xs, turned, made, sent, sums = {}, {}, {}, {}, {}

    def exchange(x):
        return lax.all_to_all(x, everyone, 0, 0, tiled=True, axis_index_groups=groups)

    x_sds = sds((group, frames * channels // group // lane + 2 * half_taps, lane), bf16)
    x_v = pltpu.VMEM(x_sds.shape, bf16)

    def make_grad(layer, x):
        width = gathered[layer - 1].shape[2]
        peers, held = x.shape[:2]
        per = channels // peers
        fold = lane // per
        rows = 16
        out = (per // rows, taps, rows, width)
        return call(
            functools.partial(weight_grads, frames, taps, rows), "weight_grads", sds(out, bf16),
            [any_()] * 3,
            [
                wide_rows(-(-taps // fold) * lane, width), pltpu.VMEM(x.shape, bf16),
                pltpu.VMEM((peers, near, lane), bf16), pltpu.VMEM((peers, frames, width), bf16),
                pltpu.VMEM((2, fold, held + 8, lane), f32), pltpu.VMEM((2, near, lane), f32),
                pltpu.VMEM((2, near + 8, lane), f32), pltpu.VMEM((2, near, lane), f32),
                pltpu.VMEM(out, bf16), sems(3 * peers + (taps + 2) // 3),
            ],
            2 * taps * per * frames * peers * width, 2 * peers * frames * width,
            (x, segs, gathered[layer - 1]), any_(),
        )

    def reduce_groups(part):
        parts, rows = part.shape[0], part.shape[2]
        split = rows // share_rows
        if split > 1:
            part = part.reshape(parts, taps, split, share_rows, -1).transpose(0, 2, 1, 3, 4)
            part = part.reshape(parts * split, taps, share_rows, -1)
        return lax.psum_scatter(part, everyone, scatter_dimension=0, axis_index_groups=across)

    def halve_groups(part, *late):
        if rows_axis != 2 or group_count != 4:
            return reduce_groups(part)
        number = me // group

        def pick(v, axis, i):
            return lax.dynamic_index_in_dim(v, i, axis, keepdims=False)

        pairs = part.reshape(2, 2, *part.shape[1:])
        away = after(swap(pick(pairs, 1, 1 - number % 2), "tm", tm // 4), *late)
        both = (pick(pairs, 1, number % 2).astype(f32) + away.astype(f32)).astype(bf16)
        away = swap(pick(both, 0, 1 - number // 2), "tm", tm // 2)
        return (pick(both, 0, number // 2).astype(f32) + away.astype(f32)).astype(bf16)

    def fetch(part):
        if rows_axis == 2:
            return swap(part, "batch", 1)
        return lax.all_gather(part, "batch", axis=0)

    def added(part, other):
        if rows_axis == 2:
            return part.astype(f32) + other.astype(f32)
        return jnp.sum(other.astype(f32), axis=0)

    def joined(part, other):
        if rows_axis == 2:
            first = jnp.where(row_place == 0, part, other)
            last = jnp.where(row_place == 0, other, part)
            return jnp.concatenate([first, last], axis=1).astype(f32)
        return jnp.concatenate([other[i] for i in range(rows_axis)], axis=1).astype(f32)

    class Halving:
        def __init__(self, part):
            bits = [1 << i for i in range((tm - 1).bit_length())]
            self.order = [1, *bits[2:], 2]
            self.left, self.part = bits, part
            self.send()

        def send(self):
            bit = self.order[0]
            below = 1 << self.left.index(bit)
            self.pairs = self.part.reshape(self.part.shape[0] // below // 2, 2, below, unit, -1)
            away = lax.dynamic_index_in_dim(self.pairs, 1 - place // bit % 2, 1, keepdims=False)
            self.there = swap(away, "tm", bit)

        def step(self, *late):
            bit = self.order.pop(0)
            self.left = [b for b in self.left if b != bit]
            mine = lax.dynamic_index_in_dim(self.pairs, place // bit % 2, 1, keepdims=False)
            there = after(self.there, *late)
            part = (mine.astype(f32) + there.astype(f32)).astype(bf16)
            self.part = part.reshape(-1, unit, part.shape[-1])
            if self.order:
                self.send()

    dz = du
    for layer in range(layers, 1, -1):
        ext_da = half_taps * layer
        rows = frames + 2 * ext_da
        out_rows = rows - 2 * half_taps
        held = []
        if layer + 2 <= layers:
            made[layer + 2] = make_grad(layer + 2, after(turned[layer + 2], sent[layer]))
            held.append(made[layer + 2])
            sums[layer + 2] = reduce_groups(after(made[layer + 2], back[layer]))
        if layer == layers:
            held += [gathered[2]]
        if layer == layers - 1:
            held += [prelude_gradient]
        if layer == layers - 2:
            held += [gathered[4]]
        bst = after(back[layer], *held) if held else back[layer]
        if layer == layers - 1:
            res_part = Halving(after(res_weight, bst).reshape(tm, unit, -1))
        if layer == 2:
            res_part.step(bst)
        if layer + 1 <= layers:
            turned[layer + 1] = exchange(after(xs[layer + 1], bst))
        dz, xs[layer], totals[layer], snd = call(
            functools.partial(
                backward_step, frames, ext_da, ext[layer] - ext_da,
                ext[layer - 1] - (ext_da - half_taps), reach - ext_da, samples, layer, share_rows,
            ),
            "backward_step",
            (sds((out_rows, channels), f32), x_sds, sds((2 * blocks, lane), f32), tile_sums),
            [any_()] * 10,
            [
                *affine_v, wide_rows(rows, channels), sums_v, wide_rows(rows, channels),
                pltpu.VMEM(stats[layer].shape, f32), seg_rows,
                wide_rows(out_rows, channels), pltpu.VMEM(stats[layer - 1].shape, f32), planes(rows, channels),
                wide_rows(near, channels, bf16), x_v,
                pltpu.VMEM((taps, channels, channels), bf16), wide_rows(out_rows, channels),
                wide_rows(out_rows, channels), sums_v,
                sems(taps + 3 * blocks + 9),
            ],
            *conv_cost(out_rows, channels),
            (
                dz, bst, acts[layer], stats[layer], gain, shift, seg, w_rest, acts[layer - 1],
                stats[layer - 1],
            ),
            (any_(), any_(), vmem(), any_()),
        )
        if layer + 1 <= layers:
            snd = after(snd, turned[layer + 1])
        if layer in (layers - 1, 2):
            snd = after(snd, res_part.there)
        back[layer - 1] = spread(snd)
        sent[layer - 1] = snd

    ext_da = half_taps
    rows = frames + 2 * ext_da
    made[3] = make_grad(3, after(turned[3], sent[1]))
    sums[3] = reduce_groups(after(made[3], back[1]))
    bst = after(back[1], made[3], sums[layers])
    res_part.step(bst)
    turned[2] = exchange(after(xs[2], bst))
    da, x, totals[1] = call(
        functools.partial(backward_norm, frames, ext_da, ext[1] - ext_da, samples, 1, share_rows),
        "backward_norm",
        (sds((rows, channels), bf16), x_sds, sds((2 * blocks, lane), f32)),
        [any_()] * 5,
        [
            affine_v[0], wide_rows(rows, channels), sums_v, wide_rows(rows, channels), sums_v,
            wide_rows(rows, channels, bf16), wide_rows(near, channels, bf16),
            x_v, sems(2 * blocks + 5),
        ],
        1000, 4 << 20, (dz, bst, acts[1], stats[1], gain), (any_(), any_(), vmem()),
    )
    turned[1] = exchange(after(x, turned[2]))
    made[2] = make_grad(2, after(turned[2], x))
    sums[2] = reduce_groups(after(made[2], turned[1]))
    made[1] = make_grad(1, after(turned[1], made[2]))
    dz = call(
        functools.partial(backward_conv, reach - ext_da), "backward_conv",
        sds((frames, entry_width), bf16),
        [any_()] * 4,
        [
            wide_rows(rows, channels, bf16), seg_rows, wide_rows(frames, entry_width), planes(rows, channels),
            pltpu.VMEM((taps, channels, entry_width), bf16), wide_rows(frames, entry_width),
            wide_rows(frames, entry_width, bf16), sems(taps + 4),
        ],
        *conv_cost(frames, entry_width), (after(da, made[1]), seg, w_first, res_entry), any_(),
    )
    while len(res_part.order) > 1:
        res_part.step(turned[1])
    others = {n: fetch(after(sums[n], x)) for n in range(layers, 3, -1)}
    sums[1] = halve_groups(made[1], dz)
    others[3] = fetch(after(sums[3], made[1]))
    res_part.step(dz)
    res_share = res_part.part[0]
    res_other = fetch(res_share)
    others[2] = fetch(sums[2])
    others[1] = fetch(sums[1])
    for layer in range(layers, 0, -1):
        grads[layer] = joined(sums[layer], others[layer])
    grad_res_weight = added(res_share, res_other)

    grad_block_input = dz[None]

    def share(v):
        return lax.dynamic_slice_in_dim(v, place * unit, unit, axis=v.ndim - 1)

    norm_sums = share(jnp.stack(totals[1:]).reshape(layers, 2, channels))
    grad_shift, grad_gain = norm_sums[: layers - 1, 0], norm_sums[:, 1]
    grad_last_shift = norm_sums[layers - 1, 0]
    grad_res_gain = share(res_tot[: 3 * blocks].reshape(3, channels))
    grad_res_shift = jnp.broadcast_to(grad_last_shift[None], (3, unit))
    grad_w_first = jnp.transpose(grads[1], (1, 0, 2))
    grad_w_rest = jnp.transpose(jnp.stack(grads[2:]), (0, 2, 1, 3))
    return (
        block_output[None],
        grad_block_input,
        prelude_gradient[None],
        grad_first[None],
        grad_w_first,
        grad_w_rest,
        grad_gain,
        grad_shift,
        grad_last_shift,
        grad_res_weight,
        grad_res_gain,
        grad_res_shift,
    )


def solution(mesh):
    split = P("batch", "tm", None)
    in_specs = (
        split, split, split, P("batch", None), P(), P(), P(), P(), P(), P(), P(), split,
    )
    out_specs = (
        split, split, split, split,
        P("tm", None, None), P(None, "tm", None, None), P(None, "tm"), P(None, "tm"), P("tm"),
        P("tm", None), P(None, "tm"), P(None, "tm"),
    )
    return jax.shard_map(
        per_device, mesh=mesh, in_specs=in_specs, out_specs=out_specs, check_vma=False
    )
```

```python
import functools

import jax
import jax.numpy as jnp
from jax import lax
from jax.experimental import pallas as pl
from jax.experimental.pallas import tpu as pltpu
from jax.sharding import PartitionSpec as P

norm_eps = 0.001
lane = 128
half_taps = 8
group = 8
bf16 = jnp.bfloat16
f32 = jnp.float32

row_dot = (((1,), (1,)), ((), ()))
plain_dot = (((1,), (0,)), ((), ()))
column_dot = (((0,), (0,)), ((), ()))


def in_vmem():
    return pl.BlockSpec(memory_space=pltpu.VMEM)


def in_place():
    return pl.BlockSpec(memory_space=pl.ANY)


def in_smem():
    return pl.BlockSpec(memory_space=pltpu.SMEM)


def dot(a, b, dims):
    return lax.dot_general(a, b, dims, preferred_element_type=f32)


def cols(c):
    return slice(c * lane, (c + 1) * lane)


def sigmoid(v):
    return 1.0 / (1.0 + jnp.exp(-v))


def sum_rows(v):
    return jnp.sum(v, axis=0, keepdims=True)


def moments(total, row, count, samples):
    out = []
    for c in range(count):
        mean = total[row + c : row + c + 1] * (1.0 / samples)
        spread = total[row + count + c : row + count + c + 1] * (1.0 / samples) - mean * mean
        out.append((mean, lax.rsqrt(spread + norm_eps)))
    return out


class Copies:
    def __init__(self, sems):
        self.sems, self.count = sems, 0

    def start(self, src, dst):
        copy = pltpu.make_async_copy(src, dst, self.sems.at[self.count])
        self.count += 1
        copy.start()
        return copy

    def load(self, pairs):
        return [self.start(src, dst) for src, dst in pairs]


def wait_all(copies):
    for copy in copies:
        copy.wait()


def start_weights(copies, w_ref, w_vmem, layer, order):
    made = {}
    for k in order:
        made[k] = copies.start(w_ref.at[k] if layer is None else w_ref.at[layer, k], w_vmem.at[k])
    return made


def convolve(rows, base, planes, seg_ref, w_vmem, w_copies, flip, dims, acc_ref, finish=None):
    taps = w_vmem.shape[0]
    blocks = planes.shape[0]

    def add(k, low, high):
        mask = (
            seg_ref[base + k + low : base + k + high]
            == seg_ref[base + half_taps + low : base + half_taps + high]
        )
        x = jnp.concatenate(
            [jnp.where(mask, planes[c, k + low : k + high], 0.0).astype(bf16) for c in range(blocks)],
            axis=1,
        )
        d = dot(x, w_vmem[taps - 1 - k if flip else k], dims)
        if k == 0:
            acc_ref[low:high] = d
        else:
            acc_ref[low:high] += d

    whole = taps - 4 if finish else taps
    for k in range(taps):
        w_copies[taps - 1 - k if flip else k].wait()
        if k < whole:
            add(k, 0, rows)
    if finish:
        middle = rows // 32 * 16
        for low, high in ((0, middle), (middle, rows)):
            for k in range(whole, taps):
                add(k, low, high)
            finish(low, high)


def send_sums(copies, pieces, wide_ref, snd_ref):
    tile = jnp.concatenate(pieces, axis=0)
    short = wide_ref.shape[1] - tile.shape[0]
    if short:
        tile = jnp.concatenate([tile, jnp.zeros((short, lane), f32)], axis=0)
    for d in range(wide_ref.shape[0]):
        wide_ref[d] = tile
    return copies.start(wide_ref, snd_ref)


def sums_within(values, low, high, own, totals):
    inside = slice(max(low, own.start) - low, min(high, own.stop) - low)
    for i, v in enumerate(values):
        part = sum_rows(v[inside])
        totals[i] = part if totals[i] is None else totals[i] + part


def conv_finish(copies, acc_ref, a_ref, own, totals, done):
    blocks = acc_ref.shape[1] // lane

    def finish(low, high):
        done.append(copies.start(acc_ref.at[low:high], a_ref.at[low:high]))
        values = [acc_ref[low:high, cols(c)] for c in range(blocks)]
        sums_within(values + [v * v for v in values], low, high, own, totals)

    return finish


def segment_of(position, counts_ref, end, row=0):
    number = counts_ref.shape[1]
    at = lax.broadcasted_iota(jnp.int32, (1, lane), 1)
    starts, start = jnp.full((1, lane), end + lane * lane, jnp.int32), jnp.int32(0)
    for j in range(number):
        starts = jnp.where(at == j, start, starts)
        start = start + counts_ref[row, j]
    begun = jnp.where(position >= starts, 1.0, 0.0).astype(bf16)
    inside = dot(begun, jnp.ones((lane, lane), bf16), plain_dot)
    return jnp.where(position < end, inside, -1.0)


def prepare(
    frames, end, reach,
    place_ref, counts_ref, x_ref,
    seg_ref, x_tail, x_head,
    sems,
):
    copies = Copies(sems)
    edge = x_tail.shape[0]
    first = copies.load([(x_ref.at[frames - edge :], x_tail), (x_ref.at[:edge], x_head)])
    rows = lax.broadcasted_iota(jnp.int32, seg_ref.shape, 0)
    seg_ref[...] = segment_of(place_ref[0] * frames - reach + rows, counts_ref, end)
    wait_all(first)


def pack_sides(frames, p_ref, l_ref, cot_ref, s_tail, s_head, sems):
    copies = Copies(sems)
    side = s_tail.shape[0]
    at, made = 0, []
    for ref in (p_ref, l_ref, cot_ref):
        width = ref.shape[1]
        made.append(copies.start(ref.at[frames - side :], s_tail.at[:, at : at + width]))
        made.append(copies.start(ref.at[:side], s_head.at[:, at : at + width]))
        at += width
    wait_all(made)


def chunk_segments(frames, end, chunks, place_ref, counts_ref, out_ref):
    ahead = lax.broadcasted_iota(jnp.int32, out_ref.shape[1:], 0) - half_taps
    for r in range(chunks):
        row = place_ref[1, r]
        out_ref[r] = segment_of(place_ref[0, r] * frames + ahead, counts_ref, end, row).astype(bf16)


def forward_first(
    frames, ext, base,
    x_ref, low_ref, high_ref, seg_hbm, w_ref,
    a_ref, snd_ref,
    x_v, planes, seg_ref, w_vmem, acc_ref, wide_ref, sems,
):
    copies = Copies(sems)
    taps = w_vmem.shape[0]
    edge = low_ref.shape[0]
    first = copies.load([
        (x_ref, x_v.at[edge : edge + frames]), (low_ref, x_v.at[:edge]), (high_ref, x_v.at[edge + frames :]),
        (seg_hbm, seg_ref),
    ])
    w_copies = start_weights(copies, w_ref, w_vmem, None, range(taps))
    wait_all(first)
    for c in range(planes.shape[0]):
        planes[c] = x_v[:, cols(c)].astype(f32)
    done, totals = [], [None] * (2 * acc_ref.shape[1] // lane)
    finish = conv_finish(copies, acc_ref, a_ref, slice(ext, ext + frames), totals, done)
    convolve(acc_ref.shape[0], base, planes, seg_ref, w_vmem, w_copies, False, row_dot, acc_ref, finish)
    wait_all(done + [send_sums(copies, totals, wide_ref, snd_ref)])


def forward_next(
    frames, ext, base, samples, layer, with_extra,
    prev_hbm, st_hbm, gain_hbm, shift_hbm, seg_hbm, w_ref, *rest,
):
    extra_hbm, rest = (rest[0], rest[1:]) if with_extra else (None, rest)
    a_ref, h_ref, snd_ref, gain_ref, shift_ref, prev_ref, st_ref, low_ref, planes = rest[:9]
    seg_ref, w_vmem, acc_ref, wide_ref, sems = rest[9:14]
    copies = Copies(sems)
    blocks = planes.shape[0]
    small = copies.load([(st_hbm, st_ref), (gain_hbm, gain_ref), (shift_hbm, shift_ref)])
    prev_copies = [copies.start(prev_hbm.at[:, cols(c)], prev_ref.at[:, cols(c)]) for c in range(blocks)]
    seg_copy = copies.start(seg_hbm, seg_ref)
    w_copies = start_weights(copies, w_ref, w_vmem, layer - 2, range(w_vmem.shape[0]))
    extra = None
    if with_extra:
        extra = copies.start(extra_hbm.at[layer - 2], rest[14])
    wait_all(small)
    total = jnp.sum(st_ref[...], axis=0)
    inner = slice(ext + half_taps, ext + half_taps + frames)
    prev = slice(layer - 2, layer - 1)
    for c, (mean, rstd) in enumerate(moments(total, 0, blocks, samples)):
        prev_copies[c].wait()
        z = (prev_ref[:, cols(c)] - mean) * (rstd * gain_ref[prev, cols(c)])
        z = z + shift_ref[prev, cols(c)]
        low = (z * sigmoid(z)).astype(bf16)
        planes[c] = low.astype(f32)
        low_ref[:, cols(c)] = low[inner]
    h_copy = copies.start(low_ref, h_ref)
    seg_copy.wait()
    done, totals = [h_copy], [None] * (2 * blocks)
    finish = conv_finish(copies, acc_ref, a_ref, slice(ext, ext + frames), totals, done)
    convolve(acc_ref.shape[0], base, planes, seg_ref, w_vmem, w_copies, False, row_dot, acc_ref, finish)
    if with_extra:
        extra.wait()
        totals.append(rest[14][...])
    wait_all(done + [send_sums(copies, totals, wide_ref, snd_ref)])


def branch_weights(rw_ref, sources):
    at, out = 0, []
    for p in sources:
        out.append(rw_ref[:, at : at + p.shape[1]])
        at += p.shape[1]
    return out


def branch_sums(p_ref, l_ref, x_ref, rw_ref, out_ref):
    blocks = rw_ref.shape[0] // lane
    sources = (p_ref, l_ref, x_ref)
    for branch, (p, w) in enumerate(zip(sources, branch_weights(rw_ref, sources), strict=True)):
        q = dot(p[...], w, row_dot)
        for c in range(blocks):
            out_ref[branch, c : c + 1] = sum_rows(q[:, cols(c)])
            out_ref[branch, blocks + c : blocks + c + 1] = sum_rows(q[:, cols(c)] * q[:, cols(c)])


def join(
    frames, ext, samples, layer,
    a_hbm, st_hbm, p_hbm, l_hbm, x_hbm, rw_hbm, q0_hbm, q1_hbm, q2_hbm, cot_hbm, xl_hbm, xh_hbm, sl_hbm, sh_hbm,
    gain_ref, shift_ref, rg_ref, rb_ref,
    out_ref, du_ref, snd_ref, snd_res_ref, q_tot_ref,
    a_ref, st_ref, p_ref, l_ref, x_ref, rw_ref, qst_refs, cot_ref, x_low, x_high, s_low, s_high,
    q_ref, du_v, out_v, wide_ref, wide_res_ref, sems,
):
    copies = Copies(sems)
    blocks = a_ref.shape[1] // lane
    early = copies.load([
        (rw_hbm, rw_ref), (p_hbm, p_ref), (l_hbm, l_ref), (x_hbm, x_ref), (xl_hbm, x_low), (xh_hbm, x_high),
        (sl_hbm, s_low), (sh_hbm, s_high),
    ])
    first = copies.load(
        [(q, qst_refs.at[i]) for i, q in enumerate((q0_hbm, q1_hbm, q2_hbm))] + [(st_hbm, st_ref)]
    )
    columns = [
        copies.load([
            (a_hbm.at[:, cols(c)], a_ref.at[:, cols(c)]), (cot_hbm.at[:, cols(c)], cot_ref.at[:, cols(c)]),
        ])
        for c in range(blocks)
    ]
    wait_all(early)
    sources = (p_ref, l_ref, x_ref)
    edge, side = x_low.shape[0], s_low.shape[0]
    own = slice(ext, ext + frames)
    at = 0
    for branch, w in enumerate(branch_weights(rw_ref, sources)):
        width = sources[branch].shape[1]
        if branch < 2:
            low, high = s_low[:, at : at + width], s_high[:, at : at + width]
            at += width
        else:
            low, high = x_low[edge - side :], x_high[:side]
        q_ref[branch, :ext] = dot(low, w, row_dot)[side - ext :]
        q_ref[branch, own] = dot(sources[branch][...], w, row_dot)
        q_ref[branch, ext + frames :] = dot(high, w, row_dot)[:ext]
    wait_all(first)
    total = jnp.sum(st_ref[...], axis=0)
    main = moments(total, 0, blocks, samples)
    res = []
    for branch in range(3):
        q_tot_ref[branch] = jnp.sum(qst_refs[branch], axis=0)[2 * blocks :]
        res.append(moments(q_tot_ref[branch], 0, blocks, samples))
    shift_sums, gain_sums, res_sums, done = [], [], [[], [], []], []
    mine = slice(layer - 1, layer)
    for c in range(blocks):
        wait_all(columns[c])
        normed = (a_ref[:, cols(c)] - main[c][0]) * main[c][1]
        u = normed * gain_ref[mine, cols(c)] + shift_ref[mine, cols(c)]
        normed_q = []
        for branch in range(3):
            mean, rstd = res[branch][c]
            qn = (q_ref[branch, :, cols(c)] - mean) * rstd
            normed_q.append(qn[own])
            u = u + qn * rg_ref[branch : branch + 1, cols(c)] + rb_ref[branch : branch + 1, cols(c)]
        s = sigmoid(u)
        out_v[:, cols(c)] = (u * s)[own].astype(bf16)
        slope = s * (1.0 + u * (1.0 - s))
        cot = slice(at + c * lane, at + (c + 1) * lane)
        du_v[:ext, cols(c)] = s_low[:, cot].astype(f32)[side - ext :] * slope[:ext]
        du_v[ext + frames :, cols(c)] = s_high[:, cot].astype(f32)[:ext] * slope[ext + frames :]
        du = cot_ref[:, cols(c)].astype(f32) * slope[own]
        du_v[own, cols(c)] = du
        done.append(copies.start(du_v.at[:, cols(c)], du_ref.at[:, cols(c)]))
        shift_sums.append(sum_rows(du))
        gain_sums.append(sum_rows(du * normed[own]))
        for branch in range(3):
            res_sums[branch].append(sum_rows(du * normed_q[branch]))
    done.append(copies.start(out_v, out_ref))
    done.append(send_sums(copies, shift_sums + gain_sums, wide_ref, snd_ref))
    done.append(send_sums(copies, res_sums[0] + res_sums[1] + res_sums[2], wide_res_ref, snd_res_ref))
    wait_all(done)


def branch_grads(
    frames, ext, samples,
    du_ref, bst_ref, rst_ref, p_ref, l_ref, x_ref, rw_ref, qst_ref, rg_ref,
    g0_ref, g1_ref, g2_ref, gw_ref, tot_ref,
):
    blocks = rw_ref.shape[0] // lane
    total = jnp.sum(bst_ref[...], axis=0) * (1.0 / samples)
    gains = jnp.sum(rst_ref[...], axis=0)
    tot_ref[...] = gains
    gains = gains * (1.0 / samples)
    own = slice(ext, ext + frames)
    sources = (p_ref, l_ref, x_ref)
    at_col = 0
    for branch, (g_ref, w) in enumerate(
        zip((g0_ref, g1_ref, g2_ref), branch_weights(rw_ref, sources), strict=True)
    ):
        p = sources[branch][...]
        q = dot(p, w, row_dot)
        low = []
        for c, (mean, rstd) in enumerate(moments(qst_ref[branch], 0, blocks, samples)):
            at = branch * blocks + c
            qn = (q[:, cols(c)] - mean) * rstd
            v = du_ref[own, cols(c)] - total[c : c + 1] - qn * gains[at : at + 1]
            low.append((v * (rg_ref[branch : branch + 1, cols(c)] * rstd)).astype(bf16))
        low = jnp.concatenate(low, axis=1)
        g_ref[...] = dot(low, w, plain_dot).astype(g_ref.dtype)
        width = p.shape[1]
        gw_ref[:, at_col : at_col + width] = dot(low, p, column_dot).astype(bf16)
        at_col += width


def channel_order(channels, peers, unit):
    per = channels // peers
    n = lax.broadcasted_iota(jnp.int32, (1, channels), 1)
    source = (n % per // unit * peers + n // per) * unit + n % unit
    row = lax.broadcasted_iota(jnp.int32, (channels, channels), 0)
    return jnp.where(row == source, 1.0, 0.0).astype(bf16)


def lane_group(per):
    return lax.broadcasted_iota(jnp.int32, (1, lane), 1) // per


def turn(v, lanes):
    return pltpu.roll(v, lanes % lane, 1) if lanes % lane else v


def pick_lanes(which, parts):
    out = parts[0]
    for j in range(1, len(parts)):
        out = jnp.where(which == j, parts[j], out)
    return out


class InputGrad:
    def __init__(self, copies, bst_hbm, st_hbm, dz_hbm, a_hbm, bst_v, st_v, dz_v, a_v, off_a):
        rows, channels = dz_v.shape
        self.blocks = channels // lane
        self.bst_v, self.st_v, self.dz_v, self.a_v = bst_v, st_v, dz_v, a_v
        self.first = copies.load([(bst_hbm, bst_v), (st_hbm, st_v)])
        self.columns = [
            copies.load([
                (dz_hbm.at[:, cols(c)], dz_v.at[:, cols(c)]),
                (a_hbm.at[off_a : off_a + rows, cols(c)], a_v.at[:, cols(c)]),
            ])
            for c in range(self.blocks)
        ]

    def make(self, samples, gain_row, tot_ref, at, low_ref, put):
        blocks = self.blocks
        wait_all(self.first)
        sums = jnp.sum(self.bst_v[...], axis=0)
        tot_ref[...] = sums
        sums = sums * (1.0 / samples)
        total = jnp.sum(self.st_v[...], axis=0)
        near = low_ref.shape[0]
        for c, (mean, rstd) in enumerate(moments(total, 0, blocks, samples)):
            wait_all(self.columns[c])
            normed = (self.a_v[:, cols(c)] - mean) * rstd
            v = self.dz_v[:, cols(c)] - sums[c : c + 1] - normed * sums[blocks + c : blocks + c + 1]
            low = (v * (gain_row[:, cols(c)] * rstd)).astype(bf16)
            put(c, low)
            low_ref[:, cols(c)] = low.astype(f32)[at : at + near].astype(bf16)


def pack_peers(frames, unit, low_ref, xs_ref):
    channels = low_ref.shape[1]
    peers, held = xs_ref.shape[:2]
    per = channels // peers
    fold = lane // per
    step = frames // fold
    which = lane_group(per)
    ordered = dot(low_ref[...], channel_order(channels, peers, unit), plain_dot)
    for c in range(channels // lane):
        v = ordered[:, cols(c)]
        turned = [turn(v, i * per) for i in range(fold)]
        for i in range(fold):
            parts = [turned[(j - i) % fold][j * step : j * step + held] for j in range(fold)]
            xs_ref[fold * c + i] = pick_lanes(which, parts).astype(bf16)


def backward_step(
    frames, ext_da, off_a, off_prev, base, samples, layer, unit,
    dz_hbm, bst_hbm, a_hbm, st_hbm, gain_hbm, shift_hbm, seg_hbm, w_ref, prev_hbm, prev_st_hbm,
    out_ref, x_ref, tot_ref, snd_ref,
    gain_ref, shift_ref, dz_v, bst_v, a_v, st_v, seg_ref, prev_v, prev_st_v, planes, low_ref, xs_ref, w_vmem, acc_ref, out_v, wide_ref,
    sems,
):
    copies = Copies(sems)
    affine = copies.load([(gain_hbm, gain_ref), (shift_hbm, shift_ref)])
    grad = InputGrad(copies, bst_hbm, st_hbm, dz_hbm, a_hbm, bst_v, st_v, dz_v, a_v, off_a)
    rows, channels = dz_v.shape
    blocks = channels // lane
    seg_copy = copies.start(seg_hbm, seg_ref)
    w_copies = start_weights(copies, w_ref, w_vmem, layer - 2, range(w_vmem.shape[0] - 1, -1, -1))
    out_rows = rows - 2 * half_taps
    late = copies.load([
        (prev_hbm.at[off_prev : off_prev + out_rows], prev_v), (prev_st_hbm, prev_st_v),
    ])

    def put(c, low):
        planes[c] = low.astype(f32)

    at = ext_da - half_taps
    wait_all(affine)
    grad.make(samples, gain_ref[layer - 1 : layer], tot_ref, at, low_ref, put)
    pack_peers(frames, unit, low_ref, xs_ref)
    x_copy = copies.start(xs_ref, x_ref)
    seg_copy.wait()
    own = slice(at, at + frames)
    done, totals = [x_copy], [None] * (2 * blocks)
    before = slice(layer - 2, layer - 1)

    def finish(low, high):
        if low == 0:
            wait_all(late)
        prev_moments = moments(jnp.sum(prev_st_v[...], axis=0), 0, blocks, samples)
        values, products = [], []
        for c, (mean, rstd) in enumerate(prev_moments):
            normed = (prev_v[low:high, cols(c)] - mean) * rstd
            z = normed * gain_ref[before, cols(c)] + shift_ref[before, cols(c)]
            s = sigmoid(z)
            dz = acc_ref[low:high, cols(c)] * (s * (1.0 + z * (1.0 - s)))
            out_v[low:high, cols(c)] = dz
            values.append(dz)
            products.append(dz * normed)
        done.append(copies.start(out_v.at[low:high], out_ref.at[low:high]))
        sums_within(values + products, low, high, own, totals)

    convolve(
        out_rows, base, planes, seg_ref, w_vmem, w_copies, True, plain_dot, acc_ref, finish
    )
    done.append(send_sums(copies, totals, wide_ref, snd_ref))
    wait_all(done)


def backward_norm(
    frames, ext_da, off_a, samples, layer, unit,
    dz_hbm, bst_hbm, a_hbm, st_hbm, gain_hbm,
    da_ref, x_ref, tot_ref,
    gain_ref, dz_v, bst_v, a_v, st_v, da_v, low_ref, xs_ref, sems,
):
    copies = Copies(sems)
    affine = copies.start(gain_hbm, gain_ref)
    grad = InputGrad(copies, bst_hbm, st_hbm, dz_hbm, a_hbm, bst_v, st_v, dz_v, a_v, off_a)
    affine.wait()

    def put(c, low):
        da_v[:, cols(c)] = low

    grad.make(samples, gain_ref[layer - 1 : layer], tot_ref, ext_da - half_taps, low_ref, put)
    pack_peers(frames, unit, low_ref, xs_ref)
    wait_all(copies.load([(xs_ref, x_ref), (da_v, da_ref)]))


def backward_conv(
    base, da_hbm, seg_hbm, w_ref, add_hbm, out_ref,
    da_v, seg_ref, add_v, planes, w_vmem, acc_ref, out_v, sems,
):
    copies = Copies(sems)
    first = copies.load([(da_hbm, da_v), (seg_hbm, seg_ref)])
    w_copies = start_weights(copies, w_ref, w_vmem, None, range(w_vmem.shape[0] - 1, -1, -1))
    late = copies.start(add_hbm, add_v)
    wait_all(first)
    for c in range(planes.shape[0]):
        planes[c] = da_v[:, cols(c)].astype(f32)
    convolve(acc_ref.shape[0], base, planes, seg_ref, w_vmem, w_copies, True, plain_dot, acc_ref)
    late.wait()
    out_v[...] = (acc_ref[...] + add_v[...]).astype(out_v.dtype)
    copies.start(out_v, out_ref).wait()


def weight_grads(
    frames, taps, unit,
    x_ref, segs_ref, h_ref, out_ref,
    acc_ref, x_v, seg_v, h_v, folded, stacked, seg_f, seg_stacked, out_v, sems,
):
    copies = Copies(sems)
    peers, held = x_ref.shape[:2]
    slots = out_ref.shape[0]
    per = slots * unit
    fold = lane // per
    step = frames // fold
    near = frames + 2 * half_taps
    chunk = [
        copies.load([(x_ref.at[r], x_v.at[r]), (segs_ref.at[r], seg_v.at[r]), (h_ref.at[r], h_v.at[r])])
        for r in range(peers)
    ]
    which = lane_group(per)
    pieces, done = -(-taps // fold), []
    edges = [0] + [q * step + half_taps for q in range(1, fold)] + [near]
    for r in range(peers):
        b = r % 2
        wait_all(chunk[r][:2])
        v = x_v[r].astype(f32)
        for i in range(fold):
            folded[b, i, :held] = turn(v, i * per)
        for q in range(fold):
            lo, hi = edges[q], edges[q + 1]
            at = lo - q * step
            stacked[b, lo:hi] = pick_lanes(
                which,
                [folded[b, (j - q) % fold, at + j : at + j + hi - lo] for j in range(fold)],
            )
        seg_f[b, :near] = seg_v[r].astype(f32)
        seg_stacked[b] = pick_lanes(which, [seg_f[b, j : j + near] for j in range(fold)])
        chunk[r][2].wait()
        for p in range(0, pieces, 3):
            q = min(pieces, p + 3)
            parts = [
                jnp.where(
                    seg_stacked[b, fold * n : fold * n + frames] == seg_f[b, half_taps : half_taps + frames],
                    stacked[b, fold * n : fold * n + frames],
                    0.0,
                ).astype(bf16)
                for n in range(p, q)
            ]
            d = dot(jnp.concatenate(parts, axis=1), h_v[r], column_dot)
            if r == 0:
                acc_ref[p * lane : q * lane] = d
            elif r < peers - 1:
                acc_ref[p * lane : q * lane] += d
            else:
                d = acc_ref[p * lane : q * lane] + d
                low, high = max(0, taps - q * fold), taps - p * fold
                for k in range(low, high):
                    at = (taps - 1 - k - p * fold) * per
                    for n in range(slots):
                        out_v[n, k] = d[at + n * unit : at + (n + 1) * unit].astype(bf16)
                done.append(copies.start(out_v.at[:, low:high], out_ref.at[:, low:high]))
    wait_all(done)


def call(body, name, out_shape, in_specs, scratch, flops, byte_count, args, out_specs=None, budget=60):
    out_specs = out_specs or jax.tree.map(lambda _: in_vmem(), out_shape)
    return pl.pallas_call(
        body,
        out_shape=out_shape,
        in_specs=in_specs,
        out_specs=out_specs,
        scratch_shapes=scratch,
        compiler_params=pltpu.CompilerParams(vmem_limit_bytes=budget << 20),
        cost_estimate=pl.CostEstimate(flops=flops, bytes_accessed=byte_count, transcendentals=0),
        name=name,
    )(*args)


def after(value, *others):
    return lax.optimization_barrier((value, *others))[0]


def per_device(
    block_entry_input,
    prelude_output,
    leading_block_output,
    lengths,
    leading_conv_weight,
    remaining_conv_weight,
    gain,
    shift,
    residual_pointwise_weight,
    residual_norm_scale,
    residual_norm_bias,
    cotangent,
):
    tm, rows_axis = lax.axis_size("tm"), lax.axis_size("batch")
    everyone = ("tm", "batch")
    devices = tm * rows_axis
    place = lax.axis_index("tm")
    frames, entry_width = block_entry_input.shape[1:]
    channels, taps = leading_conv_weight.shape[:2]
    blocks = channels // lane
    layers = remaining_conv_weight.shape[0] + 1
    samples = float(frames * tm * rows_axis)
    end = frames * tm
    reach = half_taps * 2 * layers
    ext = [reach - half_taps * i for i in range(layers + 1)]
    ext_u = ext[layers]
    side = -(-ext_u // 16) * 16
    unit = channels // tm
    group_count = devices // group
    groups = [[j * group + i for i in range(group)] for j in range(group_count)]
    across = [[j * group + i for j in range(group_count)] for i in range(group)]
    row_place = lax.axis_index("batch")
    me = place * rows_axis + row_place
    share_rows = channels // devices
    near = frames + 2 * half_taps

    def sds(shape, dtype):
        return jax.ShapeDtypeStruct(shape, dtype)

    def swap(v, axis, bit):
        n = lax.axis_size(axis)
        return lax.ppermute(v, axis, [(i, i ^ bit) for i in range(n)])

    def spread(v):
        return lax.all_to_all(v, everyone, 0, 0, tiled=True)

    x_own, p_own, l_own = block_entry_input[0], prelude_output[0], leading_block_output[0]
    cot_own = cotangent[0]
    side_width = p_own.shape[1] + l_own.shape[1] + channels
    place_1 = place.astype(jnp.int32).reshape(1)

    any_ = in_place
    vmem, smem = in_vmem, in_smem

    def sems(count):
        return pltpu.SemaphoreType.DMA((count,))

    seg, x_tail, x_head = call(
        functools.partial(prepare, frames, end, reach), "prepare",
        (
            sds((frames + 2 * reach, lane), f32),
            sds((reach, entry_width), bf16), sds((reach, entry_width), bf16),
        ),
        [smem()] * 2 + [any_()], [sems(2)], 1000, 1 << 20, (place_1, lengths, x_own),
    )
    upward = [(i, i + 1) for i in range(tm - 1)]
    downward = [(i + 1, i) for i in range(tm - 1)]
    x_low, x_high = lax.ppermute(x_tail, "tm", upward), lax.ppermute(x_head, "tm", downward)

    members = (me // group * group + jnp.arange(group)).astype(jnp.int32)
    group_places = jnp.stack([members // rows_axis, members % rows_axis])
    if rows_axis == 2:
        other_lengths = swap(after(lengths, x_low, x_high), "batch", 1)
        mine = jnp.where(row_place == 0, lengths, other_lengths)
        all_lengths = jnp.concatenate([mine, lengths + other_lengths - mine], axis=0)
    else:
        all_lengths = lax.all_gather(lengths[0], "batch")

    w_first = jnp.transpose(leading_conv_weight, (1, 0, 2))
    w_rest = jnp.transpose(remaining_conv_weight, (0, 2, 1, 3))

    def weights(layer):
        return (w_first, entry_width) if layer == 1 else (w_rest, channels)

    tile_sums = sds((devices, 2 * blocks, lane), f32)
    res_rows = -(-3 * blocks // 8) * 8
    sums_v = pltpu.VMEM(tile_sums.shape, f32)
    affine_v = [pltpu.VMEM(gain.shape, f32), pltpu.VMEM(shift.shape, f32)]
    seg_rows = pltpu.VMEM((frames + 2 * reach, lane), f32)

    def conv_cost(rows, width):
        return 2 * rows * width * channels * taps, 2 * taps * width * channels + 8 * rows * channels

    def planes(rows, width):
        return pltpu.VMEM((width // lane, rows, lane), f32)

    def wide_rows(rows, width, dtype=f32):
        return pltpu.VMEM((rows, width), dtype)

    def segments(chunk_places, counts):
        chunks = chunk_places.shape[1]
        return call(
            functools.partial(chunk_segments, frames, end, chunks), "chunk_segments",
            sds((chunks, near, lane), bf16), [smem()] * 2, [], 1000, 4 << 20, (chunk_places, counts),
        )

    segs = segments(group_places, all_lengths)
    row_count = [frames + 2 * e for e in ext]
    a, snd = call(
        functools.partial(forward_first, frames, ext[1], reach - ext[0]), "forward_first",
        (sds((row_count[1], channels), f32), tile_sums),
        [any_()] * 5,
        [
            wide_rows(row_count[0], entry_width, bf16), planes(row_count[0], entry_width), seg_rows,
            pltpu.VMEM((taps, channels, entry_width), bf16), wide_rows(row_count[1], channels), sums_v,
            sems(taps + 7),
        ],
        *conv_cost(row_count[1], entry_width), (x_own, x_low, x_high, seg, w_first),
        (any_(), any_()),
    )
    stats, acts = [None, spread(snd)], [None, a]
    gathered = []

    def gather(h):
        gathered.append(lax.all_gather(h, everyone, axis=0, axis_index_groups=groups))

    gather(x_own)
    q_sums = call(
        branch_sums, "branch_sums", sds((3, 2 * blocks, lane), f32),
        [vmem()] * 4, [], 2 * frames * residual_pointwise_weight.size, 4 << 20,
        (p_own, l_own, x_own, residual_pointwise_weight),
    )
    s_tail, s_head = call(
        functools.partial(pack_sides, frames), "pack_sides",
        (sds((side, side_width), bf16), sds((side, side_width), bf16)),
        [any_()] * 3, [sems(6)], 1000, 1 << 20, (p_own, l_own, cot_own),
    )
    s_low, s_high = lax.ppermute(s_tail, "tm", upward), lax.ppermute(s_head, "tm", downward)
    for layer in range(2, layers + 1):
        held = []
        if layer == 2:
            held = [s_tail, q_sums, segs]
        if layer == 5:
            held = [s_low, s_high, gathered[0]]
        if held:
            stats[layer - 1] = after(stats[layer - 1], *held)
        rows, before = row_count[layer], row_count[layer - 1]
        st = stats[layer - 1]
        with_extra = layer <= 4
        tile = sds((devices, 4 * blocks, lane), f32) if with_extra else tile_sums
        a, h, snd = call(
            functools.partial(
                forward_next, frames, ext[layer], reach - ext[layer - 1], samples, layer, with_extra
            ),
            "forward_next",
            (sds((rows, channels), f32), sds((frames, channels), bf16), tile),
            [any_()] * (6 + with_extra),
            [
                *affine_v, wide_rows(before, channels), pltpu.VMEM(st.shape, f32), wide_rows(frames, channels, bf16),
                planes(before, channels), seg_rows, pltpu.VMEM((taps, channels, channels), bf16),
                wide_rows(rows, channels), pltpu.VMEM(tile.shape, f32), sems(taps + blocks + 9),
                *([pltpu.VMEM((2 * blocks, lane), f32)] if with_extra else []),
            ],
            *conv_cost(rows, channels),
            (acts[-1], st, gain, shift, seg, w_rest, *([q_sums] if with_extra else [])),
            (any_(), any_(), any_()),
        )
        stats.append(spread(snd))
        acts.append(a)
        gather(after(h, stats[layer]))

    rows = row_count[layers]
    rw = residual_pointwise_weight

    def like(v):
        return pltpu.VMEM(v.shape, v.dtype)

    block_output, du, snd, res_snd, q_tot = call(
        functools.partial(join, frames, ext_u, samples, layers), "join",
        (
            sds((frames, channels), bf16), sds((rows, channels), f32), tile_sums,
            sds((devices, res_rows, lane), f32), sds((3, 2 * blocks, lane), f32),
        ),
        [any_()] * 14 + [vmem()] * 4,
        [
            like(acts[layers]), like(stats[layers]), like(p_own), like(l_own), like(x_own), like(rw),
            pltpu.VMEM((3, *stats[2].shape), f32), like(cot_own), like(x_low), like(x_high), like(s_low),
            like(s_high),
            pltpu.VMEM((3, rows, channels), f32), wide_rows(rows, channels),
            wide_rows(frames, channels, bf16), sums_v, pltpu.VMEM((devices, res_rows, lane), f32),
            sems(3 * blocks + 15),
        ],
        2 * rows * rw.size, 8 << 20,
        (
            acts[layers], after(stats[layers], gathered[1]), p_own, l_own, x_own, rw, *stats[2:5],
            cot_own, x_low, x_high, s_low, s_high, gain, shift, residual_norm_scale, residual_norm_bias,
        ),
        (any_(), any_(), any_(), any_(), vmem()),
    )
    back = [None] * (layers + 1)
    back[layers] = spread(snd)
    res_back = spread(res_snd)

    prelude_gradient, grad_first, res_entry, res_weight, res_tot = call(
        functools.partial(branch_grads, frames, ext_u, samples), "branch_grads",
        (
            sds(p_own.shape, bf16), sds(l_own.shape, bf16), sds(x_own.shape, f32),
            sds(residual_pointwise_weight.shape, bf16), sds((res_rows, lane), f32),
        ),
        [vmem()] * 9, [], 6 * frames * residual_pointwise_weight.size, 8 << 20,
        (
            du, back[layers], res_back, p_own, l_own, x_own, residual_pointwise_weight, q_tot,
            residual_norm_scale,
        ),
    )
    grads, totals = [None] * (layers + 1), [None] * (layers + 1)
    xs, turned, made, sent, sums = {}, {}, {}, {}, {}

    def exchange(x):
        return lax.all_to_all(x, everyone, 0, 0, tiled=True, axis_index_groups=groups)

    x_sds = sds((group, frames * channels // group // lane + 2 * half_taps, lane), bf16)
    x_v = pltpu.VMEM(x_sds.shape, bf16)

    def make_grad(layer, x):
        width = gathered[layer - 1].shape[2]
        peers, held = x.shape[:2]
        per = channels // peers
        fold = lane // per
        rows = 16
        out = (per // rows, taps, rows, width)
        return call(
            functools.partial(weight_grads, frames, taps, rows), "weight_grads", sds(out, bf16),
            [any_()] * 3,
            [
                wide_rows(-(-taps // fold) * lane, width), pltpu.VMEM(x.shape, bf16),
                pltpu.VMEM((peers, near, lane), bf16), pltpu.VMEM((peers, frames, width), bf16),
                pltpu.VMEM((2, fold, held + 8, lane), f32), pltpu.VMEM((2, near, lane), f32),
                pltpu.VMEM((2, near + 8, lane), f32), pltpu.VMEM((2, near, lane), f32),
                pltpu.VMEM(out, bf16), sems(3 * peers + (taps + 2) // 3),
            ],
            2 * taps * per * frames * peers * width, 2 * peers * frames * width,
            (x, segs, gathered[layer - 1]), any_(),
        )

    def reduce_groups(part):
        parts, rows = part.shape[0], part.shape[2]
        split = rows // share_rows
        if split > 1:
            part = part.reshape(parts, taps, split, share_rows, -1).transpose(0, 2, 1, 3, 4)
            part = part.reshape(parts * split, taps, share_rows, -1)
        return lax.psum_scatter(part, everyone, scatter_dimension=0, axis_index_groups=across)

    def halve_groups(part, late, later):
        if rows_axis != 2 or group_count != 4:
            return reduce_groups(part)
        number = me // group

        def pick(v, axis, i):
            return lax.dynamic_index_in_dim(v, i, axis, keepdims=False)

        pairs = part.reshape(2, 2, *part.shape[1:])
        away = after(swap(pick(pairs, 1, 1 - number % 2), "tm", tm // 4), late)
        both = (pick(pairs, 1, number % 2).astype(f32) + away.astype(f32)).astype(bf16)
        away = after(swap(pick(both, 0, 1 - number // 2), "tm", tm // 2), later)
        return (pick(both, 0, number // 2).astype(f32) + away.astype(f32)).astype(bf16)

    def fetch(part):
        if rows_axis == 2:
            return swap(part, "batch", 1)
        return lax.all_gather(part, "batch", axis=0)

    def added(part, other):
        if rows_axis == 2:
            return part.astype(f32) + other.astype(f32)
        return jnp.sum(other.astype(f32), axis=0)

    def joined(part, other):
        if rows_axis == 2:
            first = jnp.where(row_place == 0, part, other)
            last = jnp.where(row_place == 0, other, part)
            return jnp.concatenate([first, last], axis=1).astype(f32)
        return jnp.concatenate([other[i] for i in range(rows_axis)], axis=1).astype(f32)

    class Halving:
        def __init__(self, part):
            bits = [1 << i for i in range((tm - 1).bit_length())]
            self.order = [1, *bits[2:], 2]
            self.left, self.part = bits, part
            self.send()

        def send(self):
            bit = self.order[0]
            below = 1 << self.left.index(bit)
            self.pairs = self.part.reshape(self.part.shape[0] // below // 2, 2, below, unit, -1)
            away = lax.dynamic_index_in_dim(self.pairs, 1 - place // bit % 2, 1, keepdims=False)
            self.there = swap(away, "tm", bit)

        def step(self, *late):
            bit = self.order.pop(0)
            self.left = [b for b in self.left if b != bit]
            mine = lax.dynamic_index_in_dim(self.pairs, place // bit % 2, 1, keepdims=False)
            there = after(self.there, *late)
            part = (mine.astype(f32) + there.astype(f32)).astype(bf16)
            self.part = part.reshape(-1, unit, part.shape[-1])
            if self.order:
                self.send()

    dz = du
    for layer in range(layers, 1, -1):
        ext_da = half_taps * layer
        rows = frames + 2 * ext_da
        out_rows = rows - 2 * half_taps
        held = []
        if layer + 2 <= layers:
            made[layer + 2] = make_grad(layer + 2, after(turned[layer + 2], sent[layer]))
            held.append(made[layer + 2])
            sums[layer + 2] = reduce_groups(after(made[layer + 2], back[layer]))
        if layer == layers:
            held += [gathered[2]]
        if layer == layers - 1:
            held += [prelude_gradient]
        if layer == layers - 2:
            held += [gathered[4]]
        bst = after(back[layer], *held) if held else back[layer]
        if layer == layers - 1:
            res_part = Halving(after(res_weight, bst).reshape(tm, unit, -1))
        if layer == 2:
            res_part.step(bst)
        if layer + 1 <= layers:
            turned[layer + 1] = exchange(after(xs[layer + 1], bst))
        dz, xs[layer], totals[layer], snd = call(
            functools.partial(
                backward_step, frames, ext_da, ext[layer] - ext_da,
                ext[layer - 1] - (ext_da - half_taps), reach - ext_da, samples, layer, share_rows,
            ),
            "backward_step",
            (sds((out_rows, channels), f32), x_sds, sds((2 * blocks, lane), f32), tile_sums),
            [any_()] * 10,
            [
                *affine_v, wide_rows(rows, channels), sums_v, wide_rows(rows, channels),
                pltpu.VMEM(stats[layer].shape, f32), seg_rows,
                wide_rows(out_rows, channels), pltpu.VMEM(stats[layer - 1].shape, f32), planes(rows, channels),
                wide_rows(near, channels, bf16), x_v,
                pltpu.VMEM((taps, channels, channels), bf16), wide_rows(out_rows, channels),
                wide_rows(out_rows, channels), sums_v,
                sems(taps + 3 * blocks + 9),
            ],
            *conv_cost(out_rows, channels),
            (
                dz, bst, acts[layer], stats[layer], gain, shift, seg, w_rest, acts[layer - 1],
                stats[layer - 1],
            ),
            (any_(), any_(), vmem(), any_()),
        )
        if layer + 1 <= layers:
            snd = after(snd, turned[layer + 1])
        if layer in (layers - 1, 2):
            snd = after(snd, res_part.there)
        back[layer - 1] = spread(snd)
        sent[layer - 1] = snd

    ext_da = half_taps
    rows = frames + 2 * ext_da
    made[3] = make_grad(3, after(turned[3], sent[1]))
    sums[3] = reduce_groups(after(made[3], back[1]))
    bst = after(back[1], made[3], sums[layers])
    res_part.step(bst)
    turned[2] = exchange(after(xs[2], bst))
    da, x, totals[1] = call(
        functools.partial(backward_norm, frames, ext_da, ext[1] - ext_da, samples, 1, share_rows),
        "backward_norm",
        (sds((rows, channels), bf16), x_sds, sds((2 * blocks, lane), f32)),
        [any_()] * 5,
        [
            affine_v[0], wide_rows(rows, channels), sums_v, wide_rows(rows, channels), sums_v,
            wide_rows(rows, channels, bf16), wide_rows(near, channels, bf16),
            x_v, sems(2 * blocks + 5),
        ],
        1000, 4 << 20, (dz, bst, acts[1], stats[1], gain), (any_(), any_(), vmem()),
    )
    turned[1] = exchange(after(x, turned[2]))
    made[2] = make_grad(2, after(turned[2], x))
    sums[2] = reduce_groups(after(made[2], turned[1]))
    made[1] = make_grad(1, after(turned[1], made[2]))
    dz = call(
        functools.partial(backward_conv, reach - ext_da), "backward_conv",
        sds((frames, entry_width), bf16),
        [any_()] * 4,
        [
            wide_rows(rows, channels, bf16), seg_rows, wide_rows(frames, entry_width), planes(rows, channels),
            pltpu.VMEM((taps, channels, entry_width), bf16), wide_rows(frames, entry_width),
            wide_rows(frames, entry_width, bf16), sems(taps + 4),
        ],
        *conv_cost(frames, entry_width), (after(da, made[1]), seg, w_first, res_entry), any_(),
    )
    while len(res_part.order) > 1:
        res_part.step(turned[1])
    others = {n: fetch(after(sums[n], x)) for n in range(layers, 3, -1)}
    others[2] = fetch(sums[2])
    sums[1] = halve_groups(made[1], dz, others[2])
    others[3] = fetch(after(sums[3], made[1]))
    res_part.step(dz)
    res_share = res_part.part[0]
    res_other = fetch(res_share)
    others[1] = fetch(sums[1])
    for layer in range(layers, 0, -1):
        grads[layer] = joined(sums[layer], others[layer])
    grad_res_weight = added(res_share, res_other)

    grad_block_input = dz[None]

    def share(v):
        return lax.dynamic_slice_in_dim(v, place * unit, unit, axis=v.ndim - 1)

    norm_sums = share(jnp.stack(totals[1:]).reshape(layers, 2, channels))
    grad_shift, grad_gain = norm_sums[: layers - 1, 0], norm_sums[:, 1]
    grad_last_shift = norm_sums[layers - 1, 0]
    grad_res_gain = share(res_tot[: 3 * blocks].reshape(3, channels))
    grad_res_shift = jnp.broadcast_to(grad_last_shift[None], (3, unit))
    grad_w_first = jnp.transpose(grads[1], (1, 0, 2))
    grad_w_rest = jnp.transpose(jnp.stack(grads[2:]), (0, 2, 1, 3))
    return (
        block_output[None],
        grad_block_input,
        prelude_gradient[None],
        grad_first[None],
        grad_w_first,
        grad_w_rest,
        grad_gain,
        grad_shift,
        grad_last_shift,
        grad_res_weight,
        grad_res_gain,
        grad_res_shift,
    )


def solution(mesh):
    split = P("batch", "tm", None)
    in_specs = (
        split, split, split, P("batch", None), P(), P(), P(), P(), P(), P(), P(), split,
    )
    out_specs = (
        split, split, split, split,
        P("tm", None, None), P(None, "tm", None, None), P(None, "tm"), P(None, "tm"), P("tm"),
        P("tm", None), P(None, "tm"), P(None, "tm"),
    )
    return jax.shard_map(
        per_device, mesh=mesh, in_specs=in_specs, out_specs=out_specs, check_vma=False
    )
```

```python
import functools

import jax
import jax.numpy as jnp
from jax import lax
from jax.experimental import pallas as pl
from jax.experimental.pallas import tpu as pltpu
from jax.sharding import PartitionSpec as P

norm_eps = 0.001
lane = 128
half_taps = 8
group = 8
bf16 = jnp.bfloat16
f32 = jnp.float32

row_dot = (((1,), (1,)), ((), ()))
plain_dot = (((1,), (0,)), ((), ()))
column_dot = (((0,), (0,)), ((), ()))


def in_vmem():
    return pl.BlockSpec(memory_space=pltpu.VMEM)


def in_place():
    return pl.BlockSpec(memory_space=pl.ANY)


def in_smem():
    return pl.BlockSpec(memory_space=pltpu.SMEM)


def dot(a, b, dims):
    return lax.dot_general(a, b, dims, preferred_element_type=f32)


def cols(c):
    return slice(c * lane, (c + 1) * lane)


def sigmoid(v):
    return 1.0 / (1.0 + jnp.exp(-v))


def sum_rows(v):
    return jnp.sum(v, axis=0, keepdims=True)


def moments(total, row, count, samples):
    out = []
    for c in range(count):
        mean = total[row + c : row + c + 1] * (1.0 / samples)
        spread = total[row + count + c : row + count + c + 1] * (1.0 / samples) - mean * mean
        out.append((mean, lax.rsqrt(spread + norm_eps)))
    return out


class Copies:
    def __init__(self, sems):
        self.sems, self.count = sems, 0

    def start(self, src, dst):
        copy = pltpu.make_async_copy(src, dst, self.sems.at[self.count])
        self.count += 1
        copy.start()
        return copy

    def load(self, pairs):
        return [self.start(src, dst) for src, dst in pairs]


def wait_all(copies):
    for copy in copies:
        copy.wait()


def start_weights(copies, w_ref, w_vmem, layer, order):
    made = {}
    for k in order:
        made[k] = copies.start(w_ref.at[k] if layer is None else w_ref.at[layer, k], w_vmem.at[k])
    return made


def convolve(rows, base, planes, seg_ref, w_vmem, w_copies, flip, dims, acc_ref, finish=None):
    taps = w_vmem.shape[0]
    blocks = planes.shape[0]

    def add(k, low, high):
        mask = (
            seg_ref[base + k + low : base + k + high]
            == seg_ref[base + half_taps + low : base + half_taps + high]
        )
        x = jnp.concatenate(
            [jnp.where(mask, planes[c, k + low : k + high], 0.0).astype(bf16) for c in range(blocks)],
            axis=1,
        )
        d = dot(x, w_vmem[taps - 1 - k if flip else k], dims)
        if k == 0:
            acc_ref[low:high] = d
        else:
            acc_ref[low:high] += d

    whole = taps - 4 if finish else taps
    for k in range(taps):
        w_copies[taps - 1 - k if flip else k].wait()
        if k < whole:
            add(k, 0, rows)
    if finish:
        middle = rows // 32 * 16
        for low, high in ((0, middle), (middle, rows)):
            for k in range(whole, taps):
                add(k, low, high)
            finish(low, high)


def send_sums(copies, pieces, wide_ref, snd_ref):
    tile = jnp.concatenate(pieces, axis=0)
    short = wide_ref.shape[1] - tile.shape[0]
    if short:
        tile = jnp.concatenate([tile, jnp.zeros((short, lane), f32)], axis=0)
    for d in range(wide_ref.shape[0]):
        wide_ref[d] = tile
    return copies.start(wide_ref, snd_ref)


def sums_within(values, low, high, own, totals):
    inside = slice(max(low, own.start) - low, min(high, own.stop) - low)
    for i, v in enumerate(values):
        part = sum_rows(v[inside])
        totals[i] = part if totals[i] is None else totals[i] + part


def conv_finish(copies, acc_ref, a_ref, own, totals, done):
    blocks = acc_ref.shape[1] // lane

    def finish(low, high):
        done.append(copies.start(acc_ref.at[low:high], a_ref.at[low:high]))
        values = [acc_ref[low:high, cols(c)] for c in range(blocks)]
        sums_within(values + [v * v for v in values], low, high, own, totals)

    return finish


def segment_of(position, counts_ref, end, row=0):
    number = counts_ref.shape[1]
    at = lax.broadcasted_iota(jnp.int32, (1, lane), 1)
    starts, start = jnp.full((1, lane), end + lane * lane, jnp.int32), jnp.int32(0)
    for j in range(number):
        starts = jnp.where(at == j, start, starts)
        start = start + counts_ref[row, j]
    begun = jnp.where(position >= starts, 1.0, 0.0).astype(bf16)
    inside = dot(begun, jnp.ones((lane, lane), bf16), plain_dot)
    return jnp.where(position < end, inside, -1.0)


def prepare(
    frames, end, reach,
    place_ref, counts_ref, x_ref,
    seg_ref, x_tail, x_head,
    sems,
):
    copies = Copies(sems)
    edge = x_tail.shape[0]
    first = copies.load([(x_ref.at[frames - edge :], x_tail), (x_ref.at[:edge], x_head)])
    rows = lax.broadcasted_iota(jnp.int32, seg_ref.shape, 0)
    seg_ref[...] = segment_of(place_ref[0] * frames - reach + rows, counts_ref, end)
    wait_all(first)


def pack_sides(frames, p_ref, l_ref, cot_ref, s_tail, s_head, sems):
    copies = Copies(sems)
    side = s_tail.shape[0]
    at, made = 0, []
    for ref in (p_ref, l_ref, cot_ref):
        width = ref.shape[1]
        made.append(copies.start(ref.at[frames - side :], s_tail.at[:, at : at + width]))
        made.append(copies.start(ref.at[:side], s_head.at[:, at : at + width]))
        at += width
    wait_all(made)


def chunk_segments(frames, end, chunks, place_ref, counts_ref, out_ref):
    ahead = lax.broadcasted_iota(jnp.int32, out_ref.shape[1:], 0) - half_taps
    for r in range(chunks):
        row = place_ref[1, r]
        out_ref[r] = segment_of(place_ref[0, r] * frames + ahead, counts_ref, end, row).astype(bf16)


def forward_first(
    frames, ext, base,
    x_ref, low_ref, high_ref, seg_hbm, w_ref,
    a_ref, snd_ref,
    x_v, planes, seg_ref, w_vmem, acc_ref, wide_ref, sems,
):
    copies = Copies(sems)
    taps = w_vmem.shape[0]
    edge = low_ref.shape[0]
    first = copies.load([
        (x_ref, x_v.at[edge : edge + frames]), (low_ref, x_v.at[:edge]), (high_ref, x_v.at[edge + frames :]),
        (seg_hbm, seg_ref),
    ])
    w_copies = start_weights(copies, w_ref, w_vmem, None, range(taps))
    wait_all(first)
    for c in range(planes.shape[0]):
        planes[c] = x_v[:, cols(c)].astype(f32)
    done, totals = [], [None] * (2 * acc_ref.shape[1] // lane)
    finish = conv_finish(copies, acc_ref, a_ref, slice(ext, ext + frames), totals, done)
    convolve(acc_ref.shape[0], base, planes, seg_ref, w_vmem, w_copies, False, row_dot, acc_ref, finish)
    wait_all(done + [send_sums(copies, totals, wide_ref, snd_ref)])


def forward_next(
    frames, ext, base, samples, layer, with_extra,
    prev_hbm, st_hbm, gain_hbm, shift_hbm, seg_hbm, w_ref, *rest,
):
    extra_hbm, rest = (rest[0], rest[1:]) if with_extra else (None, rest)
    a_ref, h_ref, snd_ref, gain_ref, shift_ref, prev_ref, st_ref, low_ref, planes = rest[:9]
    seg_ref, w_vmem, acc_ref, wide_ref, sems = rest[9:14]
    copies = Copies(sems)
    blocks = planes.shape[0]
    small = copies.load([(st_hbm, st_ref), (gain_hbm, gain_ref), (shift_hbm, shift_ref)])
    prev_copies = [copies.start(prev_hbm.at[:, cols(c)], prev_ref.at[:, cols(c)]) for c in range(blocks)]
    seg_copy = copies.start(seg_hbm, seg_ref)
    w_copies = start_weights(copies, w_ref, w_vmem, layer - 2, range(w_vmem.shape[0]))
    extra = None
    if with_extra:
        extra = copies.start(extra_hbm.at[layer - 2], rest[14])
    wait_all(small)
    total = jnp.sum(st_ref[...], axis=0)
    inner = slice(ext + half_taps, ext + half_taps + frames)
    prev = slice(layer - 2, layer - 1)
    for c, (mean, rstd) in enumerate(moments(total, 0, blocks, samples)):
        prev_copies[c].wait()
        z = (prev_ref[:, cols(c)] - mean) * (rstd * gain_ref[prev, cols(c)])
        z = z + shift_ref[prev, cols(c)]
        low = (z * sigmoid(z)).astype(bf16)
        planes[c] = low.astype(f32)
        low_ref[:, cols(c)] = low[inner]
    h_copy = copies.start(low_ref, h_ref)
    seg_copy.wait()
    done, totals = [h_copy], [None] * (2 * blocks)
    finish = conv_finish(copies, acc_ref, a_ref, slice(ext, ext + frames), totals, done)
    convolve(acc_ref.shape[0], base, planes, seg_ref, w_vmem, w_copies, False, row_dot, acc_ref, finish)
    if with_extra:
        extra.wait()
        totals.append(rest[14][...])
    wait_all(done + [send_sums(copies, totals, wide_ref, snd_ref)])


def branch_weights(rw_ref, sources):
    at, out = 0, []
    for p in sources:
        out.append(rw_ref[:, at : at + p.shape[1]])
        at += p.shape[1]
    return out


def branch_sums(p_ref, l_ref, x_ref, rw_ref, out_ref):
    blocks = rw_ref.shape[0] // lane
    sources = (p_ref, l_ref, x_ref)
    for branch, (p, w) in enumerate(zip(sources, branch_weights(rw_ref, sources), strict=True)):
        q = dot(p[...], w, row_dot)
        for c in range(blocks):
            out_ref[branch, c : c + 1] = sum_rows(q[:, cols(c)])
            out_ref[branch, blocks + c : blocks + c + 1] = sum_rows(q[:, cols(c)] * q[:, cols(c)])


def join(
    frames, ext, samples, layer,
    a_hbm, st_hbm, p_hbm, l_hbm, x_hbm, rw_hbm, q0_hbm, q1_hbm, q2_hbm, cot_hbm, xl_hbm, xh_hbm, sl_hbm, sh_hbm,
    gain_ref, shift_ref, rg_ref, rb_ref,
    out_ref, du_ref, snd_ref, snd_res_ref, q_tot_ref,
    a_ref, st_ref, p_ref, l_ref, x_ref, rw_ref, qst_refs, cot_ref, x_low, x_high, s_low, s_high,
    q_ref, du_v, out_v, wide_ref, wide_res_ref, sems,
):
    copies = Copies(sems)
    blocks = a_ref.shape[1] // lane
    early = copies.load([
        (rw_hbm, rw_ref), (p_hbm, p_ref), (l_hbm, l_ref), (x_hbm, x_ref), (xl_hbm, x_low), (xh_hbm, x_high),
        (sl_hbm, s_low), (sh_hbm, s_high),
    ])
    first = copies.load(
        [(q, qst_refs.at[i]) for i, q in enumerate((q0_hbm, q1_hbm, q2_hbm))] + [(st_hbm, st_ref)]
    )
    columns = [
        copies.load([
            (a_hbm.at[:, cols(c)], a_ref.at[:, cols(c)]), (cot_hbm.at[:, cols(c)], cot_ref.at[:, cols(c)]),
        ])
        for c in range(blocks)
    ]
    wait_all(early)
    sources = (p_ref, l_ref, x_ref)
    edge, side = x_low.shape[0], s_low.shape[0]
    own = slice(ext, ext + frames)
    at = 0
    for branch, w in enumerate(branch_weights(rw_ref, sources)):
        width = sources[branch].shape[1]
        if branch < 2:
            low, high = s_low[:, at : at + width], s_high[:, at : at + width]
            at += width
        else:
            low, high = x_low[edge - side :], x_high[:side]
        q_ref[branch, :ext] = dot(low, w, row_dot)[side - ext :]
        q_ref[branch, own] = dot(sources[branch][...], w, row_dot)
        q_ref[branch, ext + frames :] = dot(high, w, row_dot)[:ext]
    wait_all(first)
    total = jnp.sum(st_ref[...], axis=0)
    main = moments(total, 0, blocks, samples)
    res = []
    for branch in range(3):
        q_tot_ref[branch] = jnp.sum(qst_refs[branch], axis=0)[2 * blocks :]
        res.append(moments(q_tot_ref[branch], 0, blocks, samples))
    shift_sums, gain_sums, res_sums, done = [], [], [[], [], []], []
    mine = slice(layer - 1, layer)
    for c in range(blocks):
        wait_all(columns[c])
        normed = (a_ref[:, cols(c)] - main[c][0]) * main[c][1]
        u = normed * gain_ref[mine, cols(c)] + shift_ref[mine, cols(c)]
        normed_q = []
        for branch in range(3):
            mean, rstd = res[branch][c]
            qn = (q_ref[branch, :, cols(c)] - mean) * rstd
            normed_q.append(qn[own])
            u = u + qn * rg_ref[branch : branch + 1, cols(c)] + rb_ref[branch : branch + 1, cols(c)]
        s = sigmoid(u)
        out_v[:, cols(c)] = (u * s)[own].astype(bf16)
        slope = s * (1.0 + u * (1.0 - s))
        cot = slice(at + c * lane, at + (c + 1) * lane)
        du_v[:ext, cols(c)] = s_low[:, cot].astype(f32)[side - ext :] * slope[:ext]
        du_v[ext + frames :, cols(c)] = s_high[:, cot].astype(f32)[:ext] * slope[ext + frames :]
        du = cot_ref[:, cols(c)].astype(f32) * slope[own]
        du_v[own, cols(c)] = du
        done.append(copies.start(du_v.at[:, cols(c)], du_ref.at[:, cols(c)]))
        shift_sums.append(sum_rows(du))
        gain_sums.append(sum_rows(du * normed[own]))
        for branch in range(3):
            res_sums[branch].append(sum_rows(du * normed_q[branch]))
    done.append(copies.start(out_v, out_ref))
    done.append(send_sums(copies, shift_sums + gain_sums, wide_ref, snd_ref))
    done.append(send_sums(copies, res_sums[0] + res_sums[1] + res_sums[2], wide_res_ref, snd_res_ref))
    wait_all(done)


def branch_grads(
    frames, ext, samples,
    du_ref, bst_ref, rst_ref, p_ref, l_ref, x_ref, rw_ref, qst_ref, rg_ref,
    g0_ref, g1_ref, g2_ref, gw_ref, tot_ref,
):
    blocks = rw_ref.shape[0] // lane
    total = jnp.sum(bst_ref[...], axis=0) * (1.0 / samples)
    gains = jnp.sum(rst_ref[...], axis=0)
    tot_ref[...] = gains
    gains = gains * (1.0 / samples)
    own = slice(ext, ext + frames)
    sources = (p_ref, l_ref, x_ref)
    at_col = 0
    for branch, (g_ref, w) in enumerate(
        zip((g0_ref, g1_ref, g2_ref), branch_weights(rw_ref, sources), strict=True)
    ):
        p = sources[branch][...]
        q = dot(p, w, row_dot)
        low = []
        for c, (mean, rstd) in enumerate(moments(qst_ref[branch], 0, blocks, samples)):
            at = branch * blocks + c
            qn = (q[:, cols(c)] - mean) * rstd
            v = du_ref[own, cols(c)] - total[c : c + 1] - qn * gains[at : at + 1]
            low.append((v * (rg_ref[branch : branch + 1, cols(c)] * rstd)).astype(bf16))
        low = jnp.concatenate(low, axis=1)
        g_ref[...] = dot(low, w, plain_dot).astype(g_ref.dtype)
        width = p.shape[1]
        gw_ref[:, at_col : at_col + width] = dot(low, p, column_dot).astype(bf16)
        at_col += width


def channel_order(channels, peers, unit):
    per = channels // peers
    n = lax.broadcasted_iota(jnp.int32, (1, channels), 1)
    source = (n % per // unit * peers + n // per) * unit + n % unit
    row = lax.broadcasted_iota(jnp.int32, (channels, channels), 0)
    return jnp.where(row == source, 1.0, 0.0).astype(bf16)


def lane_group(per):
    return lax.broadcasted_iota(jnp.int32, (1, lane), 1) // per


def turn(v, lanes):
    return pltpu.roll(v, lanes % lane, 1) if lanes % lane else v


def pick_lanes(which, parts):
    out = parts[0]
    for j in range(1, len(parts)):
        out = jnp.where(which == j, parts[j], out)
    return out


class InputGrad:
    def __init__(self, copies, bst_hbm, st_hbm, dz_hbm, a_hbm, bst_v, st_v, dz_v, a_v, off_a):
        rows, channels = dz_v.shape
        self.blocks = channels // lane
        self.bst_v, self.st_v, self.dz_v, self.a_v = bst_v, st_v, dz_v, a_v
        self.first = copies.load([(bst_hbm, bst_v), (st_hbm, st_v)])
        self.columns = [
            copies.load([
                (dz_hbm.at[:, cols(c)], dz_v.at[:, cols(c)]),
                (a_hbm.at[off_a : off_a + rows, cols(c)], a_v.at[:, cols(c)]),
            ])
            for c in range(self.blocks)
        ]

    def make(self, samples, gain_row, tot_ref, at, low_ref, put):
        blocks = self.blocks
        wait_all(self.first)
        sums = jnp.sum(self.bst_v[...], axis=0)
        tot_ref[...] = sums
        sums = sums * (1.0 / samples)
        total = jnp.sum(self.st_v[...], axis=0)
        near = low_ref.shape[0]
        for c, (mean, rstd) in enumerate(moments(total, 0, blocks, samples)):
            wait_all(self.columns[c])
            normed = (self.a_v[:, cols(c)] - mean) * rstd
            v = self.dz_v[:, cols(c)] - sums[c : c + 1] - normed * sums[blocks + c : blocks + c + 1]
            low = (v * (gain_row[:, cols(c)] * rstd)).astype(bf16)
            put(c, low)
            low_ref[:, cols(c)] = low.astype(f32)[at : at + near].astype(bf16)


def pack_peers(frames, unit, low_ref, xs_ref):
    channels = low_ref.shape[1]
    peers, held = xs_ref.shape[:2]
    per = channels // peers
    fold = lane // per
    step = frames // fold
    which = lane_group(per)
    ordered = dot(low_ref[...], channel_order(channels, peers, unit), plain_dot)
    for c in range(channels // lane):
        v = ordered[:, cols(c)]
        turned = [turn(v, i * per) for i in range(fold)]
        for i in range(fold):
            parts = [turned[(j - i) % fold][j * step : j * step + held] for j in range(fold)]
            xs_ref[fold * c + i] = pick_lanes(which, parts).astype(bf16)


def backward_step(
    frames, ext_da, off_a, off_prev, base, samples, layer, unit,
    dz_hbm, bst_hbm, a_hbm, st_hbm, gain_hbm, shift_hbm, seg_hbm, w_ref, prev_hbm, prev_st_hbm,
    out_ref, x_ref, tot_ref, snd_ref,
    gain_ref, shift_ref, dz_v, bst_v, a_v, st_v, seg_ref, prev_v, prev_st_v, planes, low_ref, xs_ref, w_vmem, acc_ref, out_v, wide_ref,
    sems,
):
    copies = Copies(sems)
    affine = copies.load([(gain_hbm, gain_ref), (shift_hbm, shift_ref)])
    grad = InputGrad(copies, bst_hbm, st_hbm, dz_hbm, a_hbm, bst_v, st_v, dz_v, a_v, off_a)
    rows, channels = dz_v.shape
    blocks = channels // lane
    seg_copy = copies.start(seg_hbm, seg_ref)
    w_copies = start_weights(copies, w_ref, w_vmem, layer - 2, range(w_vmem.shape[0] - 1, -1, -1))
    out_rows = rows - 2 * half_taps
    late = copies.load([
        (prev_hbm.at[off_prev : off_prev + out_rows], prev_v), (prev_st_hbm, prev_st_v),
    ])

    def put(c, low):
        planes[c] = low.astype(f32)

    at = ext_da - half_taps
    wait_all(affine)
    grad.make(samples, gain_ref[layer - 1 : layer], tot_ref, at, low_ref, put)
    pack_peers(frames, unit, low_ref, xs_ref)
    x_copy = copies.start(xs_ref, x_ref)
    seg_copy.wait()
    own = slice(at, at + frames)
    done, totals = [x_copy], [None] * (2 * blocks)
    before = slice(layer - 2, layer - 1)

    def finish(low, high):
        if low == 0:
            wait_all(late)
        prev_moments = moments(jnp.sum(prev_st_v[...], axis=0), 0, blocks, samples)
        values, products = [], []
        for c, (mean, rstd) in enumerate(prev_moments):
            normed = (prev_v[low:high, cols(c)] - mean) * rstd
            z = normed * gain_ref[before, cols(c)] + shift_ref[before, cols(c)]
            s = sigmoid(z)
            dz = acc_ref[low:high, cols(c)] * (s * (1.0 + z * (1.0 - s)))
            out_v[low:high, cols(c)] = dz
            values.append(dz)
            products.append(dz * normed)
        done.append(copies.start(out_v.at[low:high], out_ref.at[low:high]))
        sums_within(values + products, low, high, own, totals)

    convolve(
        out_rows, base, planes, seg_ref, w_vmem, w_copies, True, plain_dot, acc_ref, finish
    )
    done.append(send_sums(copies, totals, wide_ref, snd_ref))
    wait_all(done)


def backward_norm(
    frames, ext_da, off_a, samples, layer, unit,
    dz_hbm, bst_hbm, a_hbm, st_hbm, gain_hbm,
    da_ref, x_ref, tot_ref,
    gain_ref, dz_v, bst_v, a_v, st_v, da_v, low_ref, xs_ref, sems,
):
    copies = Copies(sems)
    affine = copies.start(gain_hbm, gain_ref)
    grad = InputGrad(copies, bst_hbm, st_hbm, dz_hbm, a_hbm, bst_v, st_v, dz_v, a_v, off_a)
    affine.wait()

    def put(c, low):
        da_v[:, cols(c)] = low

    grad.make(samples, gain_ref[layer - 1 : layer], tot_ref, ext_da - half_taps, low_ref, put)
    pack_peers(frames, unit, low_ref, xs_ref)
    wait_all(copies.load([(xs_ref, x_ref), (da_v, da_ref)]))


def backward_conv(
    base, da_hbm, seg_hbm, w_ref, add_hbm, out_ref,
    da_v, seg_ref, add_v, planes, w_vmem, acc_ref, out_v, sems,
):
    copies = Copies(sems)
    first = copies.load([(da_hbm, da_v), (seg_hbm, seg_ref)])
    w_copies = start_weights(copies, w_ref, w_vmem, None, range(w_vmem.shape[0] - 1, -1, -1))
    late = copies.start(add_hbm, add_v)
    wait_all(first)
    for c in range(planes.shape[0]):
        planes[c] = da_v[:, cols(c)].astype(f32)
    convolve(acc_ref.shape[0], base, planes, seg_ref, w_vmem, w_copies, True, plain_dot, acc_ref)
    late.wait()
    out_v[...] = (acc_ref[...] + add_v[...]).astype(out_v.dtype)
    copies.start(out_v, out_ref).wait()


def weight_grads(
    frames, taps, unit,
    x_ref, segs_ref, h_ref, out_ref,
    acc_ref, x_v, seg_v, h_v, folded, stacked, seg_f, seg_stacked, out_v, sems,
):
    copies = Copies(sems)
    peers, held = x_ref.shape[:2]
    slots = out_ref.shape[0]
    per = slots * unit
    fold = lane // per
    step = frames // fold
    near = frames + 2 * half_taps
    chunk = [
        copies.load([(x_ref.at[r], x_v.at[r]), (segs_ref.at[r], seg_v.at[r]), (h_ref.at[r], h_v.at[r])])
        for r in range(peers)
    ]
    which = lane_group(per)
    pieces, done = -(-taps // fold), []
    edges = [0] + [q * step + half_taps for q in range(1, fold)] + [near]
    for r in range(peers):
        b = r % 2
        wait_all(chunk[r][:2])
        v = x_v[r].astype(f32)
        for i in range(fold):
            folded[b, i, :held] = turn(v, i * per)
        for q in range(fold):
            lo, hi = edges[q], edges[q + 1]
            at = lo - q * step
            stacked[b, lo:hi] = pick_lanes(
                which,
                [folded[b, (j - q) % fold, at + j : at + j + hi - lo] for j in range(fold)],
            )
        seg_f[b, :near] = seg_v[r].astype(f32)
        seg_stacked[b] = pick_lanes(which, [seg_f[b, j : j + near] for j in range(fold)])
        chunk[r][2].wait()
        for p in range(0, pieces, 3):
            q = min(pieces, p + 3)
            parts = [
                jnp.where(
                    seg_stacked[b, fold * n : fold * n + frames] == seg_f[b, half_taps : half_taps + frames],
                    stacked[b, fold * n : fold * n + frames],
                    0.0,
                ).astype(bf16)
                for n in range(p, q)
            ]
            d = dot(jnp.concatenate(parts, axis=1), h_v[r], column_dot)
            if r == 0:
                acc_ref[p * lane : q * lane] = d
            elif r < peers - 1:
                acc_ref[p * lane : q * lane] += d
            else:
                d = acc_ref[p * lane : q * lane] + d
                low, high = max(0, taps - q * fold), taps - p * fold
                for k in range(low, high):
                    at = (taps - 1 - k - p * fold) * per
                    for n in range(slots):
                        out_v[n, k] = d[at + n * unit : at + (n + 1) * unit].astype(bf16)
                done.append(copies.start(out_v.at[:, low:high], out_ref.at[:, low:high]))
    wait_all(done)


def call(body, name, out_shape, in_specs, scratch, flops, byte_count, args, out_specs=None, budget=60):
    out_specs = out_specs or jax.tree.map(lambda _: in_vmem(), out_shape)
    return pl.pallas_call(
        body,
        out_shape=out_shape,
        in_specs=in_specs,
        out_specs=out_specs,
        scratch_shapes=scratch,
        compiler_params=pltpu.CompilerParams(vmem_limit_bytes=budget << 20),
        cost_estimate=pl.CostEstimate(flops=flops, bytes_accessed=byte_count, transcendentals=0),
        name=name,
    )(*args)


def after(value, *others):
    return lax.optimization_barrier((value, *others))[0]


def per_device(
    block_entry_input,
    prelude_output,
    leading_block_output,
    lengths,
    leading_conv_weight,
    remaining_conv_weight,
    gain,
    shift,
    residual_pointwise_weight,
    residual_norm_scale,
    residual_norm_bias,
    cotangent,
):
    tm, rows_axis = lax.axis_size("tm"), lax.axis_size("batch")
    everyone = ("tm", "batch")
    devices = tm * rows_axis
    place = lax.axis_index("tm")
    frames, entry_width = block_entry_input.shape[1:]
    channels, taps = leading_conv_weight.shape[:2]
    blocks = channels // lane
    layers = remaining_conv_weight.shape[0] + 1
    samples = float(frames * tm * rows_axis)
    end = frames * tm
    reach = half_taps * 2 * layers
    ext = [reach - half_taps * i for i in range(layers + 1)]
    ext_u = ext[layers]
    side = -(-ext_u // 16) * 16
    unit = channels // tm
    group_count = devices // group
    groups = [[j * group + i for i in range(group)] for j in range(group_count)]
    across = [[j * group + i for j in range(group_count)] for i in range(group)]
    row_place = lax.axis_index("batch")
    me = place * rows_axis + row_place
    share_rows = channels // devices
    near = frames + 2 * half_taps

    def sds(shape, dtype):
        return jax.ShapeDtypeStruct(shape, dtype)

    def swap(v, axis, bit):
        n = lax.axis_size(axis)
        return lax.ppermute(v, axis, [(i, i ^ bit) for i in range(n)])

    def spread(v):
        return lax.all_to_all(v, everyone, 0, 0, tiled=True)

    x_own, p_own, l_own = block_entry_input[0], prelude_output[0], leading_block_output[0]
    cot_own = cotangent[0]
    side_width = p_own.shape[1] + l_own.shape[1] + channels
    place_1 = place.astype(jnp.int32).reshape(1)

    any_ = in_place
    vmem, smem = in_vmem, in_smem

    def sems(count):
        return pltpu.SemaphoreType.DMA((count,))

    seg, x_tail, x_head = call(
        functools.partial(prepare, frames, end, reach), "prepare",
        (
            sds((frames + 2 * reach, lane), f32),
            sds((reach, entry_width), bf16), sds((reach, entry_width), bf16),
        ),
        [smem()] * 2 + [any_()], [sems(2)], 1000, 1 << 20, (place_1, lengths, x_own),
    )
    upward = [(i, i + 1) for i in range(tm - 1)]
    downward = [(i + 1, i) for i in range(tm - 1)]
    x_low, x_high = lax.ppermute(x_tail, "tm", upward), lax.ppermute(x_head, "tm", downward)

    members = (me // group * group + jnp.arange(group)).astype(jnp.int32)
    group_places = jnp.stack([members // rows_axis, members % rows_axis])
    if rows_axis == 2:
        other_lengths = swap(after(lengths, x_low, x_high), "batch", 1)
        mine = jnp.where(row_place == 0, lengths, other_lengths)
        all_lengths = jnp.concatenate([mine, lengths + other_lengths - mine], axis=0)
    else:
        all_lengths = lax.all_gather(lengths[0], "batch")

    w_first = jnp.transpose(leading_conv_weight, (1, 0, 2))
    w_rest = jnp.transpose(remaining_conv_weight, (0, 2, 1, 3))

    def weights(layer):
        return (w_first, entry_width) if layer == 1 else (w_rest, channels)

    tile_sums = sds((devices, 2 * blocks, lane), f32)
    res_rows = -(-3 * blocks // 8) * 8
    sums_v = pltpu.VMEM(tile_sums.shape, f32)
    affine_v = [pltpu.VMEM(gain.shape, f32), pltpu.VMEM(shift.shape, f32)]
    seg_rows = pltpu.VMEM((frames + 2 * reach, lane), f32)

    def conv_cost(rows, width):
        return 2 * rows * width * channels * taps, 2 * taps * width * channels + 8 * rows * channels

    def planes(rows, width):
        return pltpu.VMEM((width // lane, rows, lane), f32)

    def wide_rows(rows, width, dtype=f32):
        return pltpu.VMEM((rows, width), dtype)

    def segments(chunk_places, counts):
        chunks = chunk_places.shape[1]
        return call(
            functools.partial(chunk_segments, frames, end, chunks), "chunk_segments",
            sds((chunks, near, lane), bf16), [smem()] * 2, [], 1000, 4 << 20, (chunk_places, counts),
        )

    segs = segments(group_places, all_lengths)
    row_count = [frames + 2 * e for e in ext]
    a, snd = call(
        functools.partial(forward_first, frames, ext[1], reach - ext[0]), "forward_first",
        (sds((row_count[1], channels), f32), tile_sums),
        [any_()] * 5,
        [
            wide_rows(row_count[0], entry_width, bf16), planes(row_count[0], entry_width), seg_rows,
            pltpu.VMEM((taps, channels, entry_width), bf16), wide_rows(row_count[1], channels), sums_v,
            sems(taps + 7),
        ],
        *conv_cost(row_count[1], entry_width), (x_own, x_low, x_high, seg, w_first),
        (any_(), any_()),
    )
    stats, acts = [None, spread(snd)], [None, a]
    gathered = []

    def gather(h):
        gathered.append(lax.all_gather(h, everyone, axis=0, axis_index_groups=groups))

    gather(x_own)
    q_sums = call(
        branch_sums, "branch_sums", sds((3, 2 * blocks, lane), f32),
        [vmem()] * 4, [], 2 * frames * residual_pointwise_weight.size, 4 << 20,
        (p_own, l_own, x_own, residual_pointwise_weight),
    )
    s_tail, s_head = call(
        functools.partial(pack_sides, frames), "pack_sides",
        (sds((side, side_width), bf16), sds((side, side_width), bf16)),
        [any_()] * 3, [sems(6)], 1000, 1 << 20, (p_own, l_own, cot_own),
    )
    s_low, s_high = lax.ppermute(s_tail, "tm", upward), lax.ppermute(s_head, "tm", downward)
    for layer in range(2, layers + 1):
        held = []
        if layer == 2:
            held = [s_tail, q_sums, segs]
        if layer == 5:
            held = [s_low, s_high, gathered[0]]
        if held:
            stats[layer - 1] = after(stats[layer - 1], *held)
        rows, before = row_count[layer], row_count[layer - 1]
        st = stats[layer - 1]
        with_extra = layer <= 4
        tile = sds((devices, 4 * blocks, lane), f32) if with_extra else tile_sums
        a, h, snd = call(
            functools.partial(
                forward_next, frames, ext[layer], reach - ext[layer - 1], samples, layer, with_extra
            ),
            "forward_next",
            (sds((rows, channels), f32), sds((frames, channels), bf16), tile),
            [any_()] * (6 + with_extra),
            [
                *affine_v, wide_rows(before, channels), pltpu.VMEM(st.shape, f32), wide_rows(frames, channels, bf16),
                planes(before, channels), seg_rows, pltpu.VMEM((taps, channels, channels), bf16),
                wide_rows(rows, channels), pltpu.VMEM(tile.shape, f32), sems(taps + blocks + 9),
                *([pltpu.VMEM((2 * blocks, lane), f32)] if with_extra else []),
            ],
            *conv_cost(rows, channels),
            (acts[-1], st, gain, shift, seg, w_rest, *([q_sums] if with_extra else [])),
            (any_(), any_(), any_()),
        )
        stats.append(spread(snd))
        acts.append(a)
        gather(after(h, stats[layer]))

    rows = row_count[layers]
    rw = residual_pointwise_weight

    def like(v):
        return pltpu.VMEM(v.shape, v.dtype)

    block_output, du, snd, res_snd, q_tot = call(
        functools.partial(join, frames, ext_u, samples, layers), "join",
        (
            sds((frames, channels), bf16), sds((rows, channels), f32), tile_sums,
            sds((devices, res_rows, lane), f32), sds((3, 2 * blocks, lane), f32),
        ),
        [any_()] * 14 + [vmem()] * 4,
        [
            like(acts[layers]), like(stats[layers]), like(p_own), like(l_own), like(x_own), like(rw),
            pltpu.VMEM((3, *stats[2].shape), f32), like(cot_own), like(x_low), like(x_high), like(s_low),
            like(s_high),
            pltpu.VMEM((3, rows, channels), f32), wide_rows(rows, channels),
            wide_rows(frames, channels, bf16), sums_v, pltpu.VMEM((devices, res_rows, lane), f32),
            sems(3 * blocks + 15),
        ],
        2 * rows * rw.size, 8 << 20,
        (
            acts[layers], after(stats[layers], gathered[1]), p_own, l_own, x_own, rw, *stats[2:5],
            cot_own, x_low, x_high, s_low, s_high, gain, shift, residual_norm_scale, residual_norm_bias,
        ),
        (any_(), any_(), any_(), any_(), vmem()),
    )
    back = [None] * (layers + 1)
    back[layers] = spread(snd)
    res_back = spread(res_snd)

    prelude_gradient, grad_first, res_entry, res_weight, res_tot = call(
        functools.partial(branch_grads, frames, ext_u, samples), "branch_grads",
        (
            sds(p_own.shape, bf16), sds(l_own.shape, bf16), sds(x_own.shape, f32),
            sds(residual_pointwise_weight.shape, bf16), sds((res_rows, lane), f32),
        ),
        [vmem()] * 9, [], 6 * frames * residual_pointwise_weight.size, 8 << 20,
        (
            du, back[layers], res_back, p_own, l_own, x_own, residual_pointwise_weight, q_tot,
            residual_norm_scale,
        ),
    )
    grads, totals = [None] * (layers + 1), [None] * (layers + 1)
    xs, turned, made, sent, sums = {}, {}, {}, {}, {}

    def exchange(x):
        return lax.all_to_all(x, everyone, 0, 0, tiled=True, axis_index_groups=groups)

    x_sds = sds((group, frames * channels // group // lane + 2 * half_taps, lane), bf16)
    x_v = pltpu.VMEM(x_sds.shape, bf16)

    def make_grad(layer, x):
        width = gathered[layer - 1].shape[2]
        peers, held = x.shape[:2]
        per = channels // peers
        fold = lane // per
        rows = 16
        out = (per // rows, taps, rows, width)
        return call(
            functools.partial(weight_grads, frames, taps, rows), "weight_grads", sds(out, bf16),
            [any_()] * 3,
            [
                wide_rows(-(-taps // fold) * lane, width), pltpu.VMEM(x.shape, bf16),
                pltpu.VMEM((peers, near, lane), bf16), pltpu.VMEM((peers, frames, width), bf16),
                pltpu.VMEM((2, fold, held + 8, lane), f32), pltpu.VMEM((2, near, lane), f32),
                pltpu.VMEM((2, near + 8, lane), f32), pltpu.VMEM((2, near, lane), f32),
                pltpu.VMEM(out, bf16), sems(3 * peers + (taps + 2) // 3),
            ],
            2 * taps * per * frames * peers * width, 2 * peers * frames * width,
            (x, segs, gathered[layer - 1]), any_(),
        )

    def reduce_groups(part):
        parts, rows = part.shape[0], part.shape[2]
        split = rows // share_rows
        if split > 1:
            part = part.reshape(parts, taps, split, share_rows, -1).transpose(0, 2, 1, 3, 4)
            part = part.reshape(parts * split, taps, share_rows, -1)
        return lax.psum_scatter(part, everyone, scatter_dimension=0, axis_index_groups=across)

    def halve_groups(part, late, later):
        if rows_axis != 2 or group_count != 4:
            return reduce_groups(part)
        number = me // group

        def pick(v, axis, i):
            return lax.dynamic_index_in_dim(v, i, axis, keepdims=False)

        pairs = part.reshape(2, 2, *part.shape[1:])
        away = after(swap(pick(pairs, 1, 1 - number % 2), "tm", tm // 4), late)
        both = (pick(pairs, 1, number % 2).astype(f32) + away.astype(f32)).astype(bf16)
        away = after(swap(pick(both, 0, 1 - number // 2), "tm", tm // 2), later)
        return (pick(both, 0, number // 2).astype(f32) + away.astype(f32)).astype(bf16)

    def fetch(part):
        if rows_axis == 2:
            return swap(part, "batch", 1)
        return lax.all_gather(part, "batch", axis=0)

    def added(part, other):
        if rows_axis == 2:
            return part.astype(f32) + other.astype(f32)
        return jnp.sum(other.astype(f32), axis=0)

    def joined(part, other):
        if rows_axis == 2:
            first = jnp.where(row_place == 0, part, other)
            last = jnp.where(row_place == 0, other, part)
            return jnp.concatenate([first, last], axis=1).astype(f32)
        return jnp.concatenate([other[i] for i in range(rows_axis)], axis=1).astype(f32)

    class Halving:
        def __init__(self, part):
            bits = [1 << i for i in range((tm - 1).bit_length())]
            self.order = [1, *bits[2:], 2]
            self.left, self.part = bits, part
            self.send()

        def send(self):
            bit = self.order[0]
            below = 1 << self.left.index(bit)
            self.pairs = self.part.reshape(self.part.shape[0] // below // 2, 2, below, unit, -1)
            away = lax.dynamic_index_in_dim(self.pairs, 1 - place // bit % 2, 1, keepdims=False)
            self.there = swap(away, "tm", bit)

        def step(self, *late):
            bit = self.order.pop(0)
            self.left = [b for b in self.left if b != bit]
            mine = lax.dynamic_index_in_dim(self.pairs, place // bit % 2, 1, keepdims=False)
            there = after(self.there, *late)
            part = (mine.astype(f32) + there.astype(f32)).astype(bf16)
            self.part = part.reshape(-1, unit, part.shape[-1])
            if self.order:
                self.send()

    dz = du
    for layer in range(layers, 1, -1):
        ext_da = half_taps * layer
        rows = frames + 2 * ext_da
        out_rows = rows - 2 * half_taps
        held = []
        if layer + 2 <= layers:
            made[layer + 2] = make_grad(layer + 2, after(turned[layer + 2], sent[layer]))
            held.append(made[layer + 2])
            sums[layer + 2] = reduce_groups(after(made[layer + 2], back[layer]))
        if layer == layers:
            held += [gathered[2]]
        if layer == layers - 1:
            held += [prelude_gradient]
        if layer == layers - 2:
            held += [gathered[4]]
        bst = after(back[layer], *held) if held else back[layer]
        if layer == layers - 1:
            res_part = Halving(after(res_weight, bst).reshape(tm, unit, -1))
        if layer == 2:
            res_part.step(bst)
        if layer + 1 <= layers:
            turned[layer + 1] = exchange(after(xs[layer + 1], bst))
        dz, xs[layer], totals[layer], snd = call(
            functools.partial(
                backward_step, frames, ext_da, ext[layer] - ext_da,
                ext[layer - 1] - (ext_da - half_taps), reach - ext_da, samples, layer, share_rows,
            ),
            "backward_step",
            (sds((out_rows, channels), f32), x_sds, sds((2 * blocks, lane), f32), tile_sums),
            [any_()] * 10,
            [
                *affine_v, wide_rows(rows, channels), sums_v, wide_rows(rows, channels),
                pltpu.VMEM(stats[layer].shape, f32), seg_rows,
                wide_rows(out_rows, channels), pltpu.VMEM(stats[layer - 1].shape, f32), planes(rows, channels),
                wide_rows(near, channels, bf16), x_v,
                pltpu.VMEM((taps, channels, channels), bf16), wide_rows(out_rows, channels),
                wide_rows(out_rows, channels), sums_v,
                sems(taps + 3 * blocks + 9),
            ],
            *conv_cost(out_rows, channels),
            (
                dz, bst, acts[layer], stats[layer], gain, shift, seg, w_rest, acts[layer - 1],
                stats[layer - 1],
            ),
            (any_(), any_(), vmem(), any_()),
        )
        if layer + 1 <= layers:
            snd = after(snd, turned[layer + 1])
        if layer in (layers - 1, 2):
            snd = after(snd, res_part.there)
        back[layer - 1] = spread(snd)
        sent[layer - 1] = snd

    ext_da = half_taps
    rows = frames + 2 * ext_da
    made[3] = make_grad(3, after(turned[3], sent[1]))
    sums[3] = reduce_groups(made[3])
    bst = after(back[1], made[3], sums[layers])
    res_part.step(bst)
    turned[2] = exchange(after(xs[2], bst))
    da, x, totals[1] = call(
        functools.partial(backward_norm, frames, ext_da, ext[1] - ext_da, samples, 1, share_rows),
        "backward_norm",
        (sds((rows, channels), bf16), x_sds, sds((2 * blocks, lane), f32)),
        [any_()] * 5,
        [
            affine_v[0], wide_rows(rows, channels), sums_v, wide_rows(rows, channels), sums_v,
            wide_rows(rows, channels, bf16), wide_rows(near, channels, bf16),
            x_v, sems(2 * blocks + 5),
        ],
        1000, 4 << 20, (dz, bst, acts[1], stats[1], gain), (any_(), any_(), vmem()),
    )
    turned[1] = exchange(after(x, turned[2]))
    made[2] = make_grad(2, after(turned[2], x))
    sums[2] = reduce_groups(after(made[2], turned[1]))
    made[1] = make_grad(1, after(turned[1], made[2]))
    dz = call(
        functools.partial(backward_conv, reach - ext_da), "backward_conv",
        sds((frames, entry_width), bf16),
        [any_()] * 4,
        [
            wide_rows(rows, channels, bf16), seg_rows, wide_rows(frames, entry_width), planes(rows, channels),
            pltpu.VMEM((taps, channels, entry_width), bf16), wide_rows(frames, entry_width),
            wide_rows(frames, entry_width, bf16), sems(taps + 4),
        ],
        *conv_cost(frames, entry_width), (after(da, made[1]), seg, w_first, res_entry), any_(),
    )
    while len(res_part.order) > 1:
        res_part.step(turned[1])
    others = {n: fetch(after(sums[n], x)) for n in range(layers, 3, -1)}
    others[2] = fetch(sums[2])
    sums[1] = halve_groups(made[1], dz, others[2])
    others[3] = fetch(after(sums[3], made[1]))
    res_part.step(dz)
    res_share = res_part.part[0]
    res_other = fetch(res_share)
    others[1] = fetch(sums[1])
    for layer in range(layers, 0, -1):
        grads[layer] = joined(sums[layer], others[layer])
    grad_res_weight = added(res_share, res_other)

    grad_block_input = dz[None]

    def share(v):
        return lax.dynamic_slice_in_dim(v, place * unit, unit, axis=v.ndim - 1)

    norm_sums = share(jnp.stack(totals[1:]).reshape(layers, 2, channels))
    grad_shift, grad_gain = norm_sums[: layers - 1, 0], norm_sums[:, 1]
    grad_last_shift = norm_sums[layers - 1, 0]
    grad_res_gain = share(res_tot[: 3 * blocks].reshape(3, channels))
    grad_res_shift = jnp.broadcast_to(grad_last_shift[None], (3, unit))
    grad_w_first = jnp.transpose(grads[1], (1, 0, 2))
    grad_w_rest = jnp.transpose(jnp.stack(grads[2:]), (0, 2, 1, 3))
    return (
        block_output[None],
        grad_block_input,
        prelude_gradient[None],
        grad_first[None],
        grad_w_first,
        grad_w_rest,
        grad_gain,
        grad_shift,
        grad_last_shift,
        grad_res_weight,
        grad_res_gain,
        grad_res_shift,
    )


def solution(mesh):
    split = P("batch", "tm", None)
    in_specs = (
        split, split, split, P("batch", None), P(), P(), P(), P(), P(), P(), P(), split,
    )
    out_specs = (
        split, split, split, split,
        P("tm", None, None), P(None, "tm", None, None), P(None, "tm"), P(None, "tm"), P("tm"),
        P("tm", None), P(None, "tm"), P(None, "tm"),
    )
    return jax.shard_map(
        per_device, mesh=mesh, in_specs=in_specs, out_specs=out_specs, check_vma=False
    )
```
